32 devices in a mesh: seq: 4 (over y, x), tp: 8 (over z, core).
Axes of the slice: x: 2, y: 2, z: 4, core: 2. Of those that a mesh axis runs over, the one named last changes fastest.
Arguments:
- hidden_in: bfloat16 [24, 4, 1024], P('tp'), may hold values from -6 to 6
- new_query: bfloat16 [24, 4, 1024], P('tp'), may hold values from -70 to 70
- new_key: bfloat16 [24, 4, 1024], P('tp'), may hold values from -15 to 15
- new_value: bfloat16 [24, 4, 1024], P('tp'), may hold values from -6 to 6
- key_cache: bfloat16 [24, 4096, 1024], P('tp', 'seq'), may hold values from -16 to 16
- value_cache: bfloat16 [24, 4096, 1024], P('tp', 'seq'), may hold values from -6 to 6
- lengths: int32 [24], P('tp'), may hold values from 64 to 4096, as said below
- out_weight: bfloat16 [1024, 1024], replicated, may hold values from -0.1875 to 0.1875
- norm_gain: float32 [1024], replicated, may hold values from 0.5 to 1.5
- router_weight: bfloat16 [1024, 16], replicated, may hold values from -0.1875 to 0.1875
- expert_ids: int32 [24, 4, 2], P('tp'), may hold values from 0 to 15, all different within a row
- gate_weight: bfloat16 [45056, 1024], P(('seq', 'tp')), may hold values from -0.1875 to 0.1875
- up_weight: bfloat16 [45056, 1024], P(('seq', 'tp')), may hold values from -0.1875 to 0.1875
- down_weight: bfloat16 [45056, 1024], P(('seq', 'tp')), may hold values from -0.109375 to 0.109375
Outputs:
- attn_out: bfloat16 [24, 4, 1024], P('tp', None, 'seq')
- layer_out: bfloat16 [24, 4, 1024], P('tp', None, 'seq')
The draws below stay inside these ranges and needn't reach their ends.
Inputs may be any that keep to these rules, and one draw needn't show every extreme that they name: `lengths`: each length is 4096 or between 64 and 128; some request has 4096.
All inputs are finite; a program needn't handle non-finite values.
Results may differ from the reference program's by a relative error of at most 0.014.
Values may be sent and summed in bfloat16 or wider, within the bound.
No kernel may reach another device: no remote copies, remote signals or barrier semaphores. Data moves between devices by JAX's collectives and lax.ppermute only.
A program may use at most 64 MiB of HBM per device.

```python
import jax
import jax.numpy as jnp
from jax import lax

D = 1024
HEADS = 16
FF = 2816
EXPERTS = 16
TOPK = 2
NEW = 4
CACHE = 4096
SHORT = 128
REQUESTS = 24
CAP = 4
N_SEQ = 4


def draw_key_cache(key, part):
    base = jnp.clip(2.5 * jax.random.normal(jax.random.fold_in(key, 3), (REQUESTS, CACHE, D), jnp.float32), -16.0, 16.0)
    return base.astype(jnp.bfloat16)


def draw_new_query(key, part):
    base = jnp.clip(jax.random.normal(jax.random.fold_in(key, 5), (REQUESTS, NEW, D), jnp.float32), -6.0, 6.0)
    return base.astype(jnp.bfloat16)


def draw_lengths(key, part):
    picked = jax.random.randint(jax.random.fold_in(key, 1), (REQUESTS,), 0, 4)
    shorter = jax.random.randint(jax.random.fold_in(key, 2), (REQUESTS,), SHORT // 2, SHORT + 1)
    result = jnp.where(picked == 0, CACHE, shorter)
    forced = jax.random.randint(jax.random.fold_in(key, 4), (), 0, REQUESTS)
    return result.at[forced].set(CACHE).astype(jnp.int32)


def level_of(rng, extent, split, least, largest):
    def one(dim, blocks):
        steps = jax.random.uniform(jax.random.fold_in(jax.random.fold_in(rng, 6), dim), (blocks,), jnp.float32, least / len(split), largest / len(split))
        return jnp.repeat(jnp.exp(steps), extent[dim] // blocks).reshape((-1,) + (1,) * (len(extent) - dim - 1))

    gain = one(*split[0])
    for cut in split[1:]:
        gain = gain * one(*cut)
    return gain


def different_ones(own_key, rows, amount, top, lift):
    order = jax.random.permutation(jax.random.fold_in(own_key, 1), amount)
    favour = order
    for power in range(3):
        favour = favour * favour // amount
    favour = favour * lift // amount
    chance = jax.random.randint(jax.random.fold_in(own_key, 2), (rows, amount), 0, 4096) + favour
    holders = jax.random.permutation(jax.random.fold_in(own_key, 3), rows)[jnp.arange(amount) % rows]
    chance = jnp.where(jnp.arange(rows)[:, None] == holders[None, :], 1 << 14, chance)
    priority = chance * amount + jnp.arange(amount)
    return lax.top_k(priority.astype(jnp.int32), top)[1].astype(jnp.int32)


def noise(rng, shape, spread, most, pieces=(), held_as=jnp.bfloat16):
    level = level_of(rng, shape, pieces, -0.22, 0.18) if pieces else 1.0
    entries = jax.random.normal(rng, shape, jnp.float32) * spread * level
    return jnp.minimum(jnp.maximum(entries, -most), most).astype(held_as)


def setup_inputs(seed: int = 0) -> dict:
    arg_keys = jax.random.split(jax.random.key(seed), 15)
    hidden_in = noise(arg_keys[0], (REQUESTS, NEW, D), 1.0, 6.0, ((0, 8),))
    new_query = draw_new_query(jax.random.fold_in(arg_keys[14], 71), 0)
    new_key = noise(arg_keys[2], (REQUESTS, NEW, D), 2.5, 15.0, ((0, 8),))
    new_value = noise(arg_keys[3], (REQUESTS, NEW, D), 1.0, 6.0, ((0, 8),))
    key_cache = draw_key_cache(jax.random.fold_in(arg_keys[14], 71), 0)
    value_cache = noise(arg_keys[5], (REQUESTS, CACHE, D), 1.0, 6.0, ((0, 8), (1, 4)))
    lengths = draw_lengths(jax.random.fold_in(arg_keys[14], 71), 0)
    out_weight = noise(arg_keys[7], (D, D), D ** -0.5, 0.1875)
    norm_gain = jnp.clip(1.0 + 0.1 * jax.random.normal(arg_keys[8], (D,), jnp.float32), 0.5, 1.5)
    router_weight = noise(arg_keys[9], (D, EXPERTS), D ** -0.5, 0.1875)
    expert_ids = different_ones(arg_keys[10], REQUESTS * NEW, EXPERTS, TOPK, 1024).reshape((REQUESTS, NEW, TOPK))
    gate_weight = noise(arg_keys[11], (EXPERTS * FF, D), D ** -0.5, 0.1875, ((0, 32),))
    up_weight = noise(arg_keys[12], (EXPERTS * FF, D), D ** -0.5, 0.1875, ((0, 32),))
    down_weight = noise(arg_keys[13], (EXPERTS * FF, D), FF ** -0.5, 0.109375, ((0, 32),))
    return {"hidden_in": hidden_in, "new_query": new_query, "new_key": new_key, "new_value": new_value, "key_cache": key_cache, "value_cache": value_cache, "lengths": lengths, "out_weight": out_weight, "norm_gain": norm_gain, "router_weight": router_weight, "expert_ids": expert_ids, "gate_weight": gate_weight, "up_weight": up_weight, "down_weight": down_weight}


masked_score = -1e+30
norm_epsilon = 1e-06

def attend_request(packed):
    query, fresh_key, fresh_value, keys, values, length = packed
    head_size = D // HEADS
    block = CACHE // N_SEQ
    scale = head_size ** (-0.5)
    query_heads = query.reshape(NEW, HEADS, head_size).astype(jnp.float32)
    cache_keys = keys.reshape(N_SEQ, block, HEADS, head_size).astype(jnp.float32)
    cache_values = values.reshape(N_SEQ, block, HEADS, head_size).astype(jnp.float32)
    fresh_keys = fresh_key.reshape(NEW, HEADS, head_size).astype(jnp.float32)
    fresh_values = fresh_value.reshape(NEW, HEADS, head_size).astype(jnp.float32)
    scores = jnp.einsum('the,bphe->bhtp', query_heads, cache_keys) * scale
    positions = jnp.arange(CACHE, dtype=jnp.int32).reshape(N_SEQ, block)
    usable = (positions < length)[:, None, None, :]
    scores = jnp.where(usable, scores, masked_score)
    fresh_scores = jnp.einsum('the,she->hts', query_heads, fresh_keys) * scale
    causal = (jnp.arange(NEW)[:, None] >= jnp.arange(NEW)[None, :])[None]
    fresh_scores = jnp.where(causal, fresh_scores, masked_score)
    block_max = lax.optimization_barrier(jnp.max(scores, axis=3))
    first_max = jnp.maximum(block_max[0], lax.optimization_barrier(jnp.max(fresh_scores, axis=2)))
    block_max = jnp.concatenate([first_max[None], block_max[1:]], axis=0)
    weights = jnp.where(usable, jnp.exp(scores - block_max[..., None]), 0.0)
    fresh_weights = jnp.where(causal, jnp.exp(fresh_scores - first_max[..., None]), 0.0)
    totals = lax.optimization_barrier(jnp.sum(weights, axis=3))
    first_total = totals[0] + lax.optimization_barrier(jnp.sum(fresh_weights, axis=2))
    totals = jnp.concatenate([first_total[None], totals[1:]], axis=0)
    rounded = lax.optimization_barrier(weights.astype(jnp.bfloat16)).astype(jnp.float32)
    fresh_rounded = lax.optimization_barrier(fresh_weights.astype(jnp.bfloat16)).astype(jnp.float32)
    partial_sums = jnp.einsum('bhtp,bphe->bhte', rounded, cache_values)
    first_sum = partial_sums[0] + jnp.einsum('hts,she->hte', fresh_rounded, fresh_values)
    partial_sums = jnp.concatenate([first_sum[None], partial_sums[1:]], axis=0)
    overall = lax.optimization_barrier(jnp.max(block_max, axis=0))
    factors = jnp.exp(block_max - overall)
    context = lax.optimization_barrier(jnp.sum(factors[..., None] * partial_sums, axis=0)) / lax.optimization_barrier(jnp.sum(factors * totals, axis=0))[..., None]
    return context.transpose(1, 0, 2).reshape(NEW, D)

def pick_slot(chosen_ids, earlier):
    onehot = chosen_ids[..., None] == jnp.arange(earlier.shape[2], dtype=jnp.int32)
    return lax.optimization_barrier(jnp.sum(jnp.where(onehot, earlier[:, :, None, :], 0), axis=3)).astype(jnp.int32)

def reference(hidden_in, new_query, new_key, new_value, key_cache, value_cache, lengths, out_weight, norm_gain, router_weight, expert_ids, gate_weight, up_weight, down_weight):
    contexts = lax.map(attend_request, (new_query, new_key, new_value, key_cache, value_cache, lengths))
    context = contexts.astype(jnp.bfloat16)
    attention = jnp.dot(context.reshape(REQUESTS * NEW, D), out_weight, preferred_element_type=jnp.float32).reshape(REQUESTS, NEW, D)
    residual = hidden_in.astype(jnp.float32) + attention
    normed = (residual * lax.rsqrt(lax.optimization_barrier(jnp.mean(residual * residual, axis=-1, keepdims=True)) + norm_epsilon) * norm_gain).astype(jnp.bfloat16)
    logits = jnp.dot(normed.reshape(REQUESTS * NEW, D), router_weight, preferred_element_type=jnp.float32).reshape(REQUESTS, NEW, EXPERTS)
    onehot = expert_ids[..., None] == jnp.arange(EXPERTS, dtype=jnp.int32)
    chosen = lax.optimization_barrier(jnp.sum(jnp.where(onehot, logits[:, :, None, :], 0.0), axis=3))
    share = 1.0 / (1.0 + jnp.exp(chosen[:, :, ::-1] - chosen))
    hits = lax.optimization_barrier(jnp.sum(onehot.astype(jnp.int32), axis=2)).astype(jnp.int32)
    earlier = (jnp.cumsum(hits, axis=0) - hits).astype(jnp.int32)
    slots = pick_slot(expert_ids, earlier)
    slot_range = jnp.arange(CAP, dtype=jnp.int32)
    normed_wide = normed.astype(jnp.float32)
    mixture = jnp.zeros((REQUESTS, NEW, D), jnp.float32)
    for expert in range(EXPERTS):
        match = expert_ids == expert
        slot_mine = lax.optimization_barrier(jnp.sum(jnp.where(match, slots, 0), axis=2)).astype(jnp.int32)
        share_mine = lax.optimization_barrier(jnp.sum(jnp.where(match, share, 0.0), axis=2))
        kept = jnp.any(match, axis=2) & (slot_mine < CAP)
        select = kept[None] & (slot_mine[None] == slot_range[:, None, None])
        buffer = jnp.einsum('crt,rtd->tcd', select.astype(jnp.float32), normed_wide, precision=lax.Precision.HIGHEST).astype(jnp.bfloat16).reshape(NEW * CAP, D)
        gate_rows = gate_weight[expert * FF:(expert + 1) * FF]
        up_rows = up_weight[expert * FF:(expert + 1) * FF]
        down_rows = down_weight[expert * FF:(expert + 1) * FF]
        gate = jnp.dot(buffer, gate_rows.T, preferred_element_type=jnp.float32)
        upward = jnp.dot(buffer, up_rows.T, preferred_element_type=jnp.float32)
        inner = (jax.nn.gelu(gate) * upward).astype(jnp.bfloat16)
        produced = jnp.dot(inner, down_rows, preferred_element_type=jnp.float32).reshape(NEW, CAP, D)
        placed = select.astype(jnp.float32) * share_mine[None]
        mixture = mixture + jnp.einsum('crt,tcd->rtd', placed, produced, precision=lax.Precision.HIGHEST)
    layer_out = (residual + mixture).astype(jnp.bfloat16)
    return (attention.astype(jnp.bfloat16), layer_out)
```

```python
import functools

import jax
import jax.numpy as jnp
from jax import lax
from jax.experimental import pallas as pl
from jax.experimental.pallas import tpu as pltpu
from jax.sharding import PartitionSpec as P

HEADS = 16
SHORT = 128
ROWS = 16
LANES = 128
masked_score = -1e30
norm_epsilon = 1e-06
NT = (((1,), (1,)), ((), ()))
TN = (((0,), (0,)), ((), ()))


def iota(shape, dim):
    return lax.broadcasted_iota(jnp.int32, shape, dim)


def three_parts(x):
    hi = x.astype(jnp.bfloat16).astype(jnp.float32)
    mid = (x - hi).astype(jnp.bfloat16).astype(jnp.float32)
    return hi, mid, x - hi - mid


def tiled(x, times):
    return jnp.concatenate([x] * times, axis=0)


def attend(lens, q_ref, nk_ref, nv_ref, k_hbm, v_hbm, out_ref, kbuf, vbuf, acc, meta, sems):
    requests, block, width = k_hbm.shape
    steps = q_ref.shape[1]
    head = width // HEADS
    scale = head ** (-0.5)
    group = 256 // head
    chunks = width // 256
    rows = group * steps
    seq = lax.axis_index("seq")

    def moves(r, count):
        pair = []
        for which, (src, dst) in enumerate(((k_hbm, kbuf), (v_hbm, vbuf))):
            pair.append(
                pltpu.make_async_copy(
                    src.at[r, pl.ds(0, count)], dst.at[r, pl.ds(0, count)], sems.at[which, r]
                )
            )
        return pair

    left = [lens[r] - seq * block for r in range(requests)]
    for r in range(requests):

        @pl.when(left[r] >= block)
        def _():
            for move in moves(r, block):
                move.start()

        @pl.when((left[r] > 0) & (left[r] < block))
        def _():
            for move in moves(r, SHORT):
                move.start()

    acc[...] = jnp.zeros_like(acc)
    meta[...] = jnp.where(iota(meta.shape, 1) // HEADS == 3, 1.0, 0.0)

    diag = iota((rows, 256), 0) // steps == iota((rows, 256), 1) // head
    diag_all = iota((rows, width), 0) // steps == (iota((rows, width), 1) % 256) // head
    all_rows = chunks * rows

    def one(r, count, whole):
        key_move, value_move = moves(r, count)
        tiled_q = tiled(q_ref[r].astype(jnp.float32), group)
        query = jnp.where(diag_all, tiled_q, 0.0).astype(jnp.bfloat16)
        fresh_k = tiled(nk_ref[r].astype(jnp.float32), group).astype(jnp.bfloat16)
        fresh_v = tiled(nv_ref[r].astype(jnp.float32), group).astype(jnp.bfloat16)
        fresh = jnp.concatenate(
            [
                lax.dot_general(
                    query[:, c * 256 : (c + 1) * 256],
                    fresh_k[:, c * 256 : (c + 1) * 256],
                    NT,
                    preferred_element_type=jnp.float32,
                )
                for c in range(chunks)
            ],
            axis=0,
        )
        row = iota(fresh.shape, 0)
        column = iota(fresh.shape, 1)
        allowed = (column < steps) & (column <= row % steps) & (seq == 0)
        fresh = jnp.where(allowed, fresh * scale, masked_score)
        key_move.wait()
        score = (
            jnp.concatenate(
                [
                    lax.dot_general(
                        query[:, c * 256 : (c + 1) * 256],
                        kbuf[r, pl.ds(0, count), c * 256 : (c + 1) * 256],
                        NT,
                        preferred_element_type=jnp.float32,
                    )
                    for c in range(chunks)
                ],
                axis=0,
            )
            * scale
        )
        usable = iota(score.shape, 1) < left[r]
        if not whole:
            score = jnp.where(usable, score, masked_score)
        top = jnp.maximum(
            jnp.max(score, axis=1, keepdims=True), jnp.max(fresh, axis=1, keepdims=True)
        )
        weight = jnp.exp(score - top)
        if not whole:
            weight = jnp.where(usable, weight, 0.0)
        fresh_weight = jnp.where(allowed, jnp.exp(fresh - top), 0.0)
        total = jnp.sum(weight, axis=1, keepdims=True) + jnp.sum(
            fresh_weight, axis=1, keepdims=True
        )
        weight = weight.astype(jnp.bfloat16)
        fresh_weight = fresh_weight.astype(jnp.bfloat16)
        shape = (all_rows, LANES)
        part = iota(shape, 1) // HEADS
        spread = jnp.zeros(shape, jnp.float32)
        for place, piece in enumerate(three_parts(top) + three_parts(total)):
            spread = jnp.where(part == place, piece, spread)
        spread = jnp.where(iota(shape, 1) % HEADS == iota(shape, 0) // steps, spread, 0.0)
        pick = iota((ROWS, all_rows), 1) % steps == iota((ROWS, all_rows), 0)
        gathered = jnp.dot(
            jnp.where(pick, 1.0, 0.0).astype(jnp.bfloat16),
            spread.astype(jnp.bfloat16),
            preferred_element_type=jnp.float32,
        )
        meta[r * steps : (r + 1) * steps, :] = gathered[:steps]
        value_move.wait()
        for c in range(chunks):
            part_rows = slice(c * rows, (c + 1) * rows)
            lanes = slice(c * 256, (c + 1) * 256)
            mixed = jnp.dot(
                weight[part_rows],
                vbuf[r, pl.ds(0, count), lanes],
                preferred_element_type=jnp.float32,
            ) + jnp.dot(
                fresh_weight[part_rows], fresh_v[:, lanes], preferred_element_type=jnp.float32
            )
            mixed = jnp.where(diag, mixed, 0.0)
            half = mixed[: 2 * steps]
            for g in range(1, group // 2):
                half = half + mixed[2 * steps * g : 2 * steps * (g + 1)]
            acc[r * steps : (r + 1) * steps, lanes] = half[:steps] + half[steps:]

    for r in range(requests):

        @pl.when(left[r] >= block)
        def _():
            one(r, block, True)

        @pl.when((left[r] > 0) & (left[r] < block))
        def _():
            one(r, SHORT, False)

        @pl.when(left[r] <= 0)
        def _():
            shape = (steps, LANES)
            hi, mid, low = three_parts(jnp.full(shape, masked_score, jnp.float32))
            part = iota(shape, 1) // HEADS
            meta[r * steps : (r + 1) * steps, :] = jnp.where(
                part == 0, hi, jnp.where(part == 1, mid, jnp.where(part == 2, low, 0.0))
            )

    out_ref[:, :width] = acc[...].astype(jnp.bfloat16)
    out_ref[:, width:] = meta[...].astype(jnp.bfloat16)


def project(
    count, ids_ref, hidden_ref, gain_ref, weight_ref, *refs
):
    parts = refs[:count]
    attn_ref, own_ref, send_ref, attn_buf, res_buf = refs[count:]
    requests, steps, width = hidden_ref.shape
    feature = attn_ref.shape[2]
    head = width // HEADS
    seq = lax.axis_index("seq")
    tp = lax.axis_index("tp")

    def moved(x, amount):
        return pltpu.roll(x, LANES - amount, 1)

    tops, totals = [], []
    for ref in parts:
        x = ref[:, width:].astype(jnp.float32)
        tops.append(x + moved(x, HEADS) + moved(x, 2 * HEADS))
        totals.append(moved(x, 3 * HEADS) + moved(x, 4 * HEADS) + moved(x, 5 * HEADS))
    overall = functools.reduce(jnp.maximum, tops)
    factors = [jnp.exp(top - overall) for top in tops]
    total = functools.reduce(jnp.add, [f * t for f, t in zip(factors, totals)])
    real = iota(total.shape, 1) < HEADS
    inverse = jnp.where(real, 1.0 / jnp.where(real, total, 1.0), 0.0)
    ratio = jnp.concatenate([jnp.where(real, f, 0.0) * inverse for f in factors], axis=0)
    expand = jnp.where(
        iota((LANES, width), 0) == iota((LANES, width), 1) // head, 1.0, 0.0
    ).astype(jnp.bfloat16)
    hi, mid, low = three_parts(ratio)
    wide = (
        jnp.dot(hi.astype(jnp.bfloat16), expand, preferred_element_type=jnp.float32)
        + jnp.dot(mid.astype(jnp.bfloat16), expand, preferred_element_type=jnp.float32)
        + jnp.dot(low.astype(jnp.bfloat16), expand, preferred_element_type=jnp.float32)
    )
    context = jnp.zeros((ROWS, width), jnp.float32)
    for b, ref in enumerate(parts):
        context = context + wide[b * ROWS : (b + 1) * ROWS] * ref[:, :width].astype(jnp.float32)
    attention = jnp.dot(
        context.astype(jnp.bfloat16), weight_ref[...], preferred_element_type=jnp.float32
    )
    hidden = [hidden_ref[r].astype(jnp.float32) for r in range(requests)]
    hidden.append(jnp.zeros((ROWS - requests * steps, width), jnp.float32))
    residual = jnp.concatenate(hidden, axis=0) + attention
    normed = (
        residual
        * lax.rsqrt(jnp.mean(residual * residual, axis=1, keepdims=True) + norm_epsilon)
        * gain_ref[...]
    )
    row = iota((ROWS, width), 0)
    lane = iota((ROWS, width), 1) - tp * ROWS
    extra = jnp.zeros((ROWS, width), jnp.float32)
    for i in range(ROWS):
        for k in range(2):
            number = jnp.float32(-1.0)
            if i < requests * steps:
                number = ids_ref[(i // steps) * 2 * steps + (i % steps) * 2 + k].astype(jnp.float32)
            if k == 0:
                first = number
        extra = jnp.where(
            lane == i,
            jnp.where(row == requests * steps, first, number),
            extra,
        )
    send_ref[...] = jnp.where(row >= requests * steps, extra, normed).astype(jnp.bfloat16)
    attn_buf[...] = attention
    res_buf[...] = residual
    lanes = pl.ds(pl.multiple_of(seq * feature, feature), feature)
    mine = attn_buf[:, lanes]
    for r in range(requests):
        attn_ref[r] = mine[r * steps : (r + 1) * steps].astype(jnp.bfloat16)
    own_ref[...] = res_buf[:, lanes]


def feed(count, capacity, steps, used, slices, router_ref, gate_ref, up_ref, down_ref, *refs):
    parts = refs[:count]
    out_ref, tokens = refs[count:]
    width = gate_ref.shape[1]
    experts = router_ref.shape[1]
    seq_size, _, _, feature = out_ref.shape
    seq = lax.axis_index("seq")
    tp = lax.axis_index("tp")
    columns = count * ROWS
    for d in range(count):
        tokens[pl.ds(pl.multiple_of((tp ^ d) * ROWS, ROWS), ROWS), :] = parts[d][...]
    ids = jnp.zeros((8, columns), jnp.float32)
    for p in range(count):
        ids = ids + tokens[p * ROWS : (p + 1) * ROWS, :columns].astype(jnp.float32)[8:]
    place = used - 8
    first = ids[place : place + 1]
    second = ids[place + 1 : place + 2]
    mine = (seq * count + tp) // slices
    mine_f = mine.astype(jnp.float32)
    hit = jnp.where((first == mine_f) | (second == mine_f), 1.0, 0.0)
    other = jnp.where(first == mine_f, second, first)
    earlier = (iota((columns, columns), 0) < iota((columns, columns), 1)) & (
        iota((columns, columns), 0) % steps == iota((columns, columns), 1) % steps
    )
    slot = jnp.dot(
        jnp.broadcast_to(hit, (ROWS, columns)).astype(jnp.bfloat16),
        jnp.where(earlier, 1.0, 0.0).astype(jnp.bfloat16),
        preferred_element_type=jnp.float32,
    )[:1]
    rows = -(-steps * capacity // ROWS) * ROWS
    row = iota((rows, columns), 0)
    choose = (
        (hit > 0.5)
        & (slot == (row % capacity).astype(jnp.float32))
        & (iota((rows, columns), 1) % steps == row // capacity)
    )
    select = jnp.where(choose, 1.0, 0.0)
    rival = jnp.sum(select * other, axis=1, keepdims=True)
    select = select.astype(jnp.bfloat16)
    buffer = jnp.dot(select, tokens[...], preferred_element_type=jnp.float32).astype(jnp.bfloat16)
    logits = jnp.dot(buffer, router_ref[...], preferred_element_type=jnp.float32)
    index = iota((rows, experts), 1)
    ahead = jnp.sum(jnp.where(index == mine, logits, 0.0), axis=1, keepdims=True)
    behind = jnp.sum(
        jnp.where(index.astype(jnp.float32) == rival, logits, 0.0), axis=1, keepdims=True
    )
    share = 1.0 / (1.0 + jnp.exp(behind - ahead))
    gate = lax.dot_general(buffer, gate_ref[...], NT, preferred_element_type=jnp.float32)
    upward = lax.dot_general(buffer, up_ref[...], NT, preferred_element_type=jnp.float32)
    inner = (jax.nn.gelu(gate) * upward).astype(jnp.bfloat16)
    produced = jnp.dot(inner, down_ref[...], preferred_element_type=jnp.float32)
    shared = (produced * share).astype(jnp.bfloat16)
    term = lax.dot_general(select, shared, TN, preferred_element_type=jnp.float32).astype(
        jnp.bfloat16
    )
    for s in range(seq_size):
        for p in range(count):
            out_ref[s, p] = term[p * ROWS : (p + 1) * ROWS, s * feature : (s + 1) * feature]


def finish(own_ref, terms_ref, out_ref):
    requests, steps, _ = out_ref.shape
    total = own_ref[...]
    mixture = terms_ref[0].astype(jnp.float32)
    for i in range(1, terms_ref.shape[0]):
        mixture = mixture + terms_ref[i].astype(jnp.float32)
    total = total + mixture
    for r in range(requests):
        out_ref[r] = total[r * steps : (r + 1) * steps].astype(jnp.bfloat16)


def body(
    hidden_in,
    new_query,
    new_key,
    new_value,
    key_cache,
    value_cache,
    lengths,
    out_weight,
    norm_gain,
    router_weight,
    expert_ids,
    gate_weight,
    up_weight,
    down_weight,
):
    requests, steps, width = hidden_in.shape
    block = key_cache.shape[1]
    seq_size = lax.axis_size("seq")
    tp_size = lax.axis_size("tp")
    feature = width // seq_size
    experts = router_weight.shape[1]
    topk = expert_ids.shape[2]
    capacity = (5 * requests * tp_size * topk + 4 * experts - 1) // (4 * experts)
    slices = seq_size * tp_size // experts
    vmem = pl.BlockSpec(memory_space=pltpu.VMEM)
    smem = pl.BlockSpec(memory_space=pltpu.SMEM)
    anywhere = pl.BlockSpec(memory_space=pl.ANY)
    limit = pltpu.CompilerParams(vmem_limit_bytes=40 * 1024 * 1024)
    message = jax.ShapeDtypeStruct((ROWS, width + LANES), jnp.bfloat16)

    part = pl.pallas_call(
        attend,
        out_shape=message,
        in_specs=[smem, vmem, vmem, vmem, anywhere, anywhere],
        out_specs=vmem,
        scratch_shapes=[
            pltpu.VMEM((requests, block, width), jnp.bfloat16),
            pltpu.VMEM((requests, block, width), jnp.bfloat16),
            pltpu.VMEM((ROWS, width), jnp.float32),
            pltpu.VMEM((ROWS, LANES), jnp.float32),
            pltpu.SemaphoreType.DMA((2, requests)),
        ],
        compiler_params=limit,
        name="attend",
    )(lengths, new_query, new_key, new_value, key_cache, value_cache)

    def swapped(x, axis, size, d):
        return lax.ppermute(x, axis, [(i, i ^ d) for i in range(size)])

    parts = [part] + [swapped(part, "seq", seq_size, d) for d in range(1, seq_size)]
    attn_out, own_residual, packed = pl.pallas_call(
        functools.partial(project, seq_size),
        out_shape=(
            jax.ShapeDtypeStruct((requests, steps, feature), jnp.bfloat16),
            jax.ShapeDtypeStruct((ROWS, feature), jnp.float32),
            jax.ShapeDtypeStruct((ROWS, width), jnp.bfloat16),
        ),
        in_specs=[smem, vmem, vmem, vmem] + [vmem] * seq_size,
        out_specs=(vmem, vmem, vmem),
        scratch_shapes=[
            pltpu.VMEM((ROWS, width), jnp.float32),
            pltpu.VMEM((ROWS, width), jnp.float32),
        ],
        compiler_params=limit,
        name="project",
    )(expert_ids.reshape(-1), hidden_in, norm_gain.reshape(1, width), out_weight, *parts)
    tokens = [packed] + [swapped(packed, "tp", tp_size, d) for d in range(1, tp_size)]
    terms = pl.pallas_call(
        functools.partial(feed, tp_size, capacity, steps, requests * steps, slices),
        out_shape=jax.ShapeDtypeStruct((seq_size, tp_size, ROWS, feature), jnp.bfloat16),
        in_specs=[vmem] * (4 + tp_size),
        out_specs=vmem,
        scratch_shapes=[pltpu.VMEM((tp_size * ROWS, width), jnp.bfloat16)],
        compiler_params=limit,
        name="feed",
    )(router_weight, gate_weight, up_weight, down_weight, *tokens)
    terms = terms.reshape(seq_size * tp_size, ROWS, feature)
    arrived = lax.all_to_all(terms, ("seq", "tp"), 0, 0, tiled=True)
    layer_out = pl.pallas_call(
        finish,
        out_shape=jax.ShapeDtypeStruct((requests, steps, feature), jnp.bfloat16),
        in_specs=[vmem, vmem],
        out_specs=vmem,
        name="finish",
    )(own_residual, arrived)
    return (attn_out, layer_out)


def solution(mesh):
    return jax.shard_map(
        body,
        mesh=mesh,
        in_specs=(
            P("tp", None, None),
            P("tp", None, None),
            P("tp", None, None),
            P("tp", None, None),
            P("tp", "seq", None),
            P("tp", "seq", None),
            P("tp"),
            P(),
            P(),
            P(),
            P("tp", None, None),
            P(("seq", "tp"), None),
            P(("seq", "tp"), None),
            P(("seq", "tp"), None),
        ),
        out_specs=(P("tp", None, "seq"), P("tp", None, "seq")),
        check_vma=False,
    )
```

```python
import functools

import jax
import jax.numpy as jnp
from jax import lax
from jax.experimental import pallas as pl
from jax.experimental.pallas import tpu as pltpu
from jax.sharding import PartitionSpec as P

HEADS = 16
SHORT = 128
ROWS = 16
LANES = 128
masked_score = -1e30
norm_epsilon = 1e-06
NT = (((1,), (1,)), ((), ()))
TN = (((0,), (0,)), ((), ()))


def iota(shape, dim):
    return lax.broadcasted_iota(jnp.int32, shape, dim)


def three_parts(x):
    hi = x.astype(jnp.bfloat16).astype(jnp.float32)
    mid = (x - hi).astype(jnp.bfloat16).astype(jnp.float32)
    return hi, mid, x - hi - mid


def tiled(x, times):
    return jnp.concatenate([x] * times, axis=0)


def attend(
    lens_hbm, q_hbm, nk_hbm, nv_hbm, k_hbm, v_hbm, out_ref,
    lens, q_ref, nk_ref, nv_ref, kbuf, vbuf, acc, meta, sems, small_sems,
):
    requests, block, width = k_hbm.shape
    steps = q_ref.shape[1]
    head = width // HEADS
    scale = head ** (-0.5)
    group = 256 // head
    chunks = width // 256
    rows = group * steps
    seq = lax.axis_index("seq")

    def moves(r, count):
        pair = []
        for which, (src, dst) in enumerate(((k_hbm, kbuf), (v_hbm, vbuf))):
            pair.append(
                pltpu.make_async_copy(
                    src.at[r, pl.ds(0, count)], dst.at[r, pl.ds(0, count)], sems.at[which, r]
                )
            )
        return pair

    small = [
        pltpu.make_async_copy(src, dst, small_sems.at[i])
        for i, (src, dst) in enumerate(
            ((lens_hbm, lens), (q_hbm, q_ref), (nk_hbm, nk_ref), (nv_hbm, nv_ref))
        )
    ]
    for move in small:
        move.start()
    small[0].wait()
    left = [lens[r] - seq * block for r in range(requests)]
    for r in range(requests):

        @pl.when(left[r] >= block)
        def _():
            for move in moves(r, block):
                move.start()

        @pl.when((left[r] > 0) & (left[r] < block))
        def _():
            for move in moves(r, SHORT):
                move.start()

    acc[...] = jnp.zeros_like(acc)
    meta[...] = jnp.where(iota(meta.shape, 1) // HEADS == 3, 1.0, 0.0)

    for move in small[1:]:
        move.wait()
    diag = iota((rows, 256), 0) // steps == iota((rows, 256), 1) // head
    diag_all = iota((rows, width), 0) // steps == (iota((rows, width), 1) % 256) // head
    all_rows = chunks * rows

    def one(r, count, whole):
        key_move, value_move = moves(r, count)
        tiled_q = tiled(q_ref[r].astype(jnp.float32), group)
        query = jnp.where(diag_all, tiled_q, 0.0).astype(jnp.bfloat16)
        fresh_k = tiled(nk_ref[r].astype(jnp.float32), group).astype(jnp.bfloat16)
        fresh_v = tiled(nv_ref[r].astype(jnp.float32), group).astype(jnp.bfloat16)
        fresh = jnp.concatenate(
            [
                lax.dot_general(
                    query[:, c * 256 : (c + 1) * 256],
                    fresh_k[:, c * 256 : (c + 1) * 256],
                    NT,
                    preferred_element_type=jnp.float32,
                )
                for c in range(chunks)
            ],
            axis=0,
        )
        row = iota(fresh.shape, 0)
        column = iota(fresh.shape, 1)
        allowed = (column < steps) & (column <= row % steps) & (seq == 0)
        fresh = jnp.where(allowed, fresh * scale, masked_score)
        key_move.wait()
        score = (
            jnp.concatenate(
                [
                    lax.dot_general(
                        query[:, c * 256 : (c + 1) * 256],
                        kbuf[r, pl.ds(0, count), c * 256 : (c + 1) * 256],
                        NT,
                        preferred_element_type=jnp.float32,
                    )
                    for c in range(chunks)
                ],
                axis=0,
            )
            * scale
        )
        usable = iota(score.shape, 1) < left[r]
        if not whole:
            score = jnp.where(usable, score, masked_score)
        top = jnp.maximum(
            jnp.max(score, axis=1, keepdims=True), jnp.max(fresh, axis=1, keepdims=True)
        )
        weight = jnp.exp(score - top)
        if not whole:
            weight = jnp.where(usable, weight, 0.0)
        fresh_weight = jnp.where(allowed, jnp.exp(fresh - top), 0.0)
        total = jnp.sum(weight, axis=1, keepdims=True) + jnp.sum(
            fresh_weight, axis=1, keepdims=True
        )
        weight = weight.astype(jnp.bfloat16)
        fresh_weight = fresh_weight.astype(jnp.bfloat16)
        shape = (all_rows, LANES)
        part = iota(shape, 1) // HEADS
        spread = jnp.zeros(shape, jnp.float32)
        for place, piece in enumerate(three_parts(top) + three_parts(total)):
            spread = jnp.where(part == place, piece, spread)
        spread = jnp.where(iota(shape, 1) % HEADS == iota(shape, 0) // steps, spread, 0.0)
        pick = iota((ROWS, all_rows), 1) % steps == iota((ROWS, all_rows), 0)
        gathered = jnp.dot(
            jnp.where(pick, 1.0, 0.0).astype(jnp.bfloat16),
            spread.astype(jnp.bfloat16),
            preferred_element_type=jnp.float32,
        )
        meta[r * steps : (r + 1) * steps, :] = gathered[:steps]
        value_move.wait()
        for c in range(chunks):
            part_rows = slice(c * rows, (c + 1) * rows)
            lanes = slice(c * 256, (c + 1) * 256)
            mixed = jnp.dot(
                weight[part_rows],
                vbuf[r, pl.ds(0, count), lanes],
                preferred_element_type=jnp.float32,
            ) + jnp.dot(
                fresh_weight[part_rows], fresh_v[:, lanes], preferred_element_type=jnp.float32
            )
            mixed = jnp.where(diag, mixed, 0.0)
            half = mixed[: 2 * steps]
            for g in range(1, group // 2):
                half = half + mixed[2 * steps * g : 2 * steps * (g + 1)]
            acc[r * steps : (r + 1) * steps, lanes] = half[:steps] + half[steps:]

    for r in range(requests):

        @pl.when(left[r] >= block)
        def _():
            one(r, block, True)

        @pl.when((left[r] > 0) & (left[r] < block))
        def _():
            one(r, SHORT, False)

        @pl.when(left[r] <= 0)
        def _():
            shape = (steps, LANES)
            hi, mid, low = three_parts(jnp.full(shape, masked_score, jnp.float32))
            part = iota(shape, 1) // HEADS
            meta[r * steps : (r + 1) * steps, :] = jnp.where(
                part == 0, hi, jnp.where(part == 1, mid, jnp.where(part == 2, low, 0.0))
            )

    for b in range(out_ref.shape[0]):
        out_ref[b, :, :width] = acc[...].astype(jnp.bfloat16)
        out_ref[b, :, width:] = meta[...].astype(jnp.bfloat16)


def project(
    ids_ref, hidden_ref, gain_ref, weight_ref, parts_ref,
    attn_ref, own_ref, send_ref, attn_buf, res_buf,
):
    parts = [parts_ref.at[b] for b in range(parts_ref.shape[0])]
    requests, steps, width = hidden_ref.shape
    feature = attn_ref.shape[2]
    head = width // HEADS
    seq = lax.axis_index("seq")
    tp = lax.axis_index("tp")

    def moved(x, amount):
        return pltpu.roll(x, LANES - amount, 1)

    tops, totals = [], []
    for ref in parts:
        x = ref[:, width:].astype(jnp.float32)
        tops.append(x + moved(x, HEADS) + moved(x, 2 * HEADS))
        totals.append(moved(x, 3 * HEADS) + moved(x, 4 * HEADS) + moved(x, 5 * HEADS))
    overall = functools.reduce(jnp.maximum, tops)
    factors = [jnp.exp(top - overall) for top in tops]
    total = functools.reduce(jnp.add, [f * t for f, t in zip(factors, totals)])
    real = iota(total.shape, 1) < HEADS
    inverse = jnp.where(real, 1.0 / jnp.where(real, total, 1.0), 0.0)
    ratio = jnp.concatenate([jnp.where(real, f, 0.0) * inverse for f in factors], axis=0)
    expand = jnp.where(
        iota((LANES, width), 0) == iota((LANES, width), 1) // head, 1.0, 0.0
    ).astype(jnp.bfloat16)
    hi, mid, low = three_parts(ratio)
    wide = (
        jnp.dot(hi.astype(jnp.bfloat16), expand, preferred_element_type=jnp.float32)
        + jnp.dot(mid.astype(jnp.bfloat16), expand, preferred_element_type=jnp.float32)
        + jnp.dot(low.astype(jnp.bfloat16), expand, preferred_element_type=jnp.float32)
    )
    context = jnp.zeros((ROWS, width), jnp.float32)
    for b, ref in enumerate(parts):
        context = context + wide[b * ROWS : (b + 1) * ROWS] * ref[:, :width].astype(jnp.float32)
    attention = jnp.dot(
        context.astype(jnp.bfloat16), weight_ref[...], preferred_element_type=jnp.float32
    )
    hidden = [hidden_ref[r].astype(jnp.float32) for r in range(requests)]
    hidden.append(jnp.zeros((ROWS - requests * steps, width), jnp.float32))
    residual = jnp.concatenate(hidden, axis=0) + attention
    normed = (
        residual
        * lax.rsqrt(jnp.mean(residual * residual, axis=1, keepdims=True) + norm_epsilon)
        * gain_ref[...]
    )
    columns = send_ref.shape[0] * ROWS
    row = iota((ROWS, columns), 0)
    lane = iota((ROWS, columns), 1) - tp * ROWS
    extra = jnp.where((lane >= 0) & (lane < ROWS), -1.0, 0.0)
    for i in range(requests * steps):
        first, second = [
            ids_ref[i // steps, k, i % steps].astype(jnp.float32) for k in range(2)
        ]
        extra = jnp.where(lane == i, jnp.where(row == requests * steps, first, second), extra)
    tail = row >= requests * steps
    message = jnp.concatenate(
        [jnp.where(tail, extra, normed[:, :columns]), normed[:, columns:]], axis=1
    ).astype(jnp.bfloat16)
    for p in range(send_ref.shape[0]):
        send_ref[p] = message
    attn_buf[...] = attention
    res_buf[...] = residual
    lanes = pl.ds(pl.multiple_of(seq * feature, feature), feature)
    mine = attn_buf[:, lanes]
    for r in range(requests):
        attn_ref[r] = mine[r * steps : (r + 1) * steps].astype(jnp.bfloat16)
    own_ref[...] = res_buf[:, lanes]


def feed(
    capacity, steps, used, slices, router_ref, gate_ref, up_ref, down_ref, tokens, out_ref
):
    count = tokens.shape[0] // ROWS
    width = gate_ref.shape[1]
    experts = router_ref.shape[0]
    seq_size, _, _, feature = out_ref.shape
    seq = lax.axis_index("seq")
    tp = lax.axis_index("tp")
    columns = count * ROWS
    ids = jnp.zeros((8, columns), jnp.float32)
    for p in range(count):
        ids = ids + tokens[p * ROWS : (p + 1) * ROWS, :columns].astype(jnp.float32)[8:]
    place = used - 8
    first = ids[place : place + 1]
    second = ids[place + 1 : place + 2]
    mine = (seq * count + tp) // slices
    mine_f = mine.astype(jnp.float32)
    hit = jnp.where((first == mine_f) | (second == mine_f), 1.0, 0.0)
    other = jnp.where(first == mine_f, second, first)
    earlier = (iota((columns, columns), 0) < iota((columns, columns), 1)) & (
        iota((columns, columns), 0) % steps == iota((columns, columns), 1) % steps
    )
    slot = jnp.dot(
        jnp.broadcast_to(hit, (ROWS, columns)).astype(jnp.bfloat16),
        jnp.where(earlier, 1.0, 0.0).astype(jnp.bfloat16),
        preferred_element_type=jnp.float32,
    )[:1]
    rows = -(-steps * capacity // ROWS) * ROWS
    row = iota((rows, columns), 0)
    choose = (
        (hit > 0.5)
        & (slot == (row % capacity).astype(jnp.float32))
        & (iota((rows, columns), 1) % steps == row // capacity)
    )
    select = jnp.where(choose, 1.0, 0.0)
    rival = jnp.sum(select * other, axis=1, keepdims=True)
    select = select.astype(jnp.bfloat16)
    buffer = jnp.dot(select, tokens[...], preferred_element_type=jnp.float32).astype(jnp.bfloat16)
    logits = lax.dot_general(buffer, router_ref[...], NT, preferred_element_type=jnp.float32)
    index = iota((rows, experts), 1)
    ahead = jnp.sum(jnp.where(index == mine, logits, 0.0), axis=1, keepdims=True)
    behind = jnp.sum(
        jnp.where(index.astype(jnp.float32) == rival, logits, 0.0), axis=1, keepdims=True
    )
    share = 1.0 / (1.0 + jnp.exp(behind - ahead))
    gate = lax.dot_general(buffer, gate_ref[...], NT, preferred_element_type=jnp.float32)
    upward = lax.dot_general(buffer, up_ref[...], NT, preferred_element_type=jnp.float32)
    inner = (jax.nn.gelu(gate) * upward).astype(jnp.bfloat16)
    produced = jnp.dot(inner, down_ref[...], preferred_element_type=jnp.float32)
    shared = (produced * share).astype(jnp.bfloat16)
    term = lax.dot_general(select, shared, TN, preferred_element_type=jnp.float32).astype(
        jnp.bfloat16
    )
    for s in range(seq_size):
        for p in range(count):
            out_ref[s, p] = term[p * ROWS : (p + 1) * ROWS, s * feature : (s + 1) * feature]


def finish(own_ref, terms_ref, out_ref):
    requests, steps, _ = out_ref.shape
    total = own_ref[...]
    mixture = terms_ref[0].astype(jnp.float32)
    for i in range(1, terms_ref.shape[0]):
        mixture = mixture + terms_ref[i].astype(jnp.float32)
    total = total + mixture
    for r in range(requests):
        out_ref[r] = total[r * steps : (r + 1) * steps].astype(jnp.bfloat16)


def body(
    hidden_in,
    new_query,
    new_key,
    new_value,
    key_cache,
    value_cache,
    lengths,
    out_weight,
    norm_gain,
    router_weight,
    expert_ids,
    gate_weight,
    up_weight,
    down_weight,
):
    requests, steps, width = hidden_in.shape
    block = key_cache.shape[1]
    seq_size = lax.axis_size("seq")
    tp_size = lax.axis_size("tp")
    feature = width // seq_size
    experts = router_weight.shape[1]
    topk = expert_ids.shape[2]
    capacity = (5 * requests * tp_size * topk + 4 * experts - 1) // (4 * experts)
    slices = seq_size * tp_size // experts
    vmem = pl.BlockSpec(memory_space=pltpu.VMEM)
    smem = pl.BlockSpec(memory_space=pltpu.SMEM)
    hbm = pl.BlockSpec(memory_space=pltpu.HBM)

    def limit(mebibytes):
        return pltpu.CompilerParams(vmem_limit_bytes=mebibytes * 1024 * 1024)

    small = pltpu.VMEM((requests, steps, width), jnp.bfloat16)
    part = pl.pallas_call(
        attend,
        out_shape=jax.ShapeDtypeStruct((seq_size, ROWS, width + LANES), jnp.bfloat16),
        in_specs=[hbm] * 6,
        out_specs=vmem,
        scratch_shapes=[
            pltpu.SMEM((requests,), jnp.int32),
            small,
            small,
            small,
            pltpu.VMEM((requests, block, width), jnp.bfloat16),
            pltpu.VMEM((requests, block, width), jnp.bfloat16),
            pltpu.VMEM((ROWS, width), jnp.float32),
            pltpu.VMEM((ROWS, LANES), jnp.float32),
            pltpu.SemaphoreType.DMA((2, requests)),
            pltpu.SemaphoreType.DMA((4,)),
        ],
        compiler_params=limit(20),
        name="attend",
    )(
        *[
            pltpu.with_memory_space_constraint(x, pltpu.HBM)
            for x in (lengths, new_query, new_key, new_value, key_cache, value_cache)
        ]
    )
    parts = lax.all_to_all(part, "seq", 0, 0, tiled=True)
    attn_out, own_residual, packed = pl.pallas_call(
        project,
        out_shape=(
            jax.ShapeDtypeStruct((requests, steps, feature), jnp.bfloat16),
            jax.ShapeDtypeStruct((ROWS, feature), jnp.float32),
            jax.ShapeDtypeStruct((tp_size, ROWS, width), jnp.bfloat16),
        ),
        in_specs=[smem, vmem, vmem, vmem, vmem],
        out_specs=(vmem, vmem, vmem),
        scratch_shapes=[
            pltpu.VMEM((ROWS, width), jnp.float32),
            pltpu.VMEM((ROWS, width), jnp.float32),
        ],
        compiler_params=limit(8),
        name="project",
    )(expert_ids.transpose(0, 2, 1), hidden_in, norm_gain.reshape(1, width), out_weight, parts)
    tokens = lax.all_to_all(packed, "tp", 0, 0, tiled=True).reshape(tp_size * ROWS, width)
    terms = pl.pallas_call(
        functools.partial(feed, capacity, steps, requests * steps, slices),
        out_shape=jax.ShapeDtypeStruct((seq_size, tp_size, ROWS, feature), jnp.bfloat16),
        in_specs=[vmem] * 5,
        out_specs=vmem,
        compiler_params=limit(16),
        name="feed",
    )(router_weight.T, gate_weight, up_weight, down_weight, tokens)
    terms = terms.reshape(seq_size * tp_size, ROWS, feature)
    arrived = lax.all_to_all(terms, ("seq", "tp"), 0, 0, tiled=True)
    layer_out = pl.pallas_call(
        finish,
        out_shape=jax.ShapeDtypeStruct((requests, steps, feature), jnp.bfloat16),
        in_specs=[vmem, vmem],
        out_specs=vmem,
        name="finish",
    )(own_residual, arrived)
    return (attn_out, layer_out)


def solution(mesh):
    return jax.shard_map(
        body,
        mesh=mesh,
        in_specs=(
            P("tp", None, None),
            P("tp", None, None),
            P("tp", None, None),
            P("tp", None, None),
            P("tp", "seq", None),
            P("tp", "seq", None),
            P("tp"),
            P(),
            P(),
            P(),
            P("tp", None, None),
            P(("seq", "tp"), None),
            P(("seq", "tp"), None),
            P(("seq", "tp"), None),
        ),
        out_specs=(P("tp", None, "seq"), P("tp", None, "seq")),
        check_vma=False,
    )
```

```python
import functools

import jax
import jax.numpy as jnp
from jax import lax
from jax.experimental import pallas as pl
from jax.experimental.pallas import tpu as pltpu
from jax.sharding import PartitionSpec as P

HEADS = 16
SHORT = 128
ROWS = 16
LANES = 128
masked_score = -1e30
norm_epsilon = 1e-06
NT = (((1,), (1,)), ((), ()))
TN = (((0,), (0,)), ((), ()))


def iota(shape, dim):
    return lax.broadcasted_iota(jnp.int32, shape, dim)


def three_parts(x):
    hi = x.astype(jnp.bfloat16).astype(jnp.float32)
    mid = (x - hi).astype(jnp.bfloat16).astype(jnp.float32)
    return hi, mid, x - hi - mid


def tiled(x, times):
    return jnp.concatenate([x] * times, axis=0)


def attend(
    lens_hbm, q_hbm, nk_hbm, nv_hbm, k_hbm, v_hbm, out_ref,
    lens, q_ref, nk_ref, nv_ref, kbuf, vbuf, acc, meta, sems, small_sems,
):
    requests, block, width = k_hbm.shape
    steps = q_ref.shape[1]
    head = width // HEADS
    scale = head ** (-0.5)
    group = 256 // head
    chunks = width // 256
    rows = group * steps
    seq = lax.axis_index("seq")

    def moves(r, count):
        pair = []
        for which, (src, dst) in enumerate(((k_hbm, kbuf), (v_hbm, vbuf))):
            pair.append(
                pltpu.make_async_copy(
                    src.at[r, pl.ds(0, count)], dst.at[r, pl.ds(0, count)], sems.at[which, r]
                )
            )
        return pair

    small = [
        pltpu.make_async_copy(src, dst, small_sems.at[i])
        for i, (src, dst) in enumerate(
            ((lens_hbm, lens), (q_hbm, q_ref), (nk_hbm, nk_ref), (nv_hbm, nv_ref))
        )
    ]
    for move in small:
        move.start()
    small[0].wait()
    left = [lens[r] - seq * block for r in range(requests)]
    for r in range(requests):

        @pl.when(left[r] >= block)
        def _():
            for move in moves(r, block):
                move.start()

        @pl.when((left[r] > 0) & (left[r] < block))
        def _():
            for move in moves(r, SHORT):
                move.start()

    acc[...] = jnp.zeros_like(acc)
    meta[...] = jnp.where(iota(meta.shape, 1) // HEADS == 3, 1.0, 0.0)

    for move in small[1:]:
        move.wait()
    diag = iota((rows, 256), 0) // steps == iota((rows, 256), 1) // head
    diag_all = iota((rows, width), 0) // steps == (iota((rows, width), 1) % 256) // head
    all_rows = chunks * rows

    def one(r, count, whole):
        key_move, value_move = moves(r, count)
        tiled_q = tiled(q_ref[r].astype(jnp.float32), group)
        query = jnp.where(diag_all, tiled_q, 0.0).astype(jnp.bfloat16)
        fresh_k = tiled(nk_ref[r].astype(jnp.float32), group).astype(jnp.bfloat16)
        fresh_v = tiled(nv_ref[r].astype(jnp.float32), group).astype(jnp.bfloat16)
        fresh = jnp.concatenate(
            [
                lax.dot_general(
                    query[:, c * 256 : (c + 1) * 256],
                    fresh_k[:, c * 256 : (c + 1) * 256],
                    NT,
                    preferred_element_type=jnp.float32,
                )
                for c in range(chunks)
            ],
            axis=0,
        )
        row = iota(fresh.shape, 0)
        column = iota(fresh.shape, 1)
        allowed = (column < steps) & (column <= row % steps) & (seq == 0)
        fresh = jnp.where(allowed, fresh * scale, masked_score)
        key_move.wait()
        score = (
            jnp.concatenate(
                [
                    lax.dot_general(
                        query[:, c * 256 : (c + 1) * 256],
                        kbuf[r, pl.ds(0, count), c * 256 : (c + 1) * 256],
                        NT,
                        preferred_element_type=jnp.float32,
                    )
                    for c in range(chunks)
                ],
                axis=0,
            )
            * scale
        )
        usable = iota(score.shape, 1) < left[r]
        if not whole:
            score = jnp.where(usable, score, masked_score)
        top = jnp.maximum(
            jnp.max(score, axis=1, keepdims=True), jnp.max(fresh, axis=1, keepdims=True)
        )
        weight = jnp.exp(score - top)
        if not whole:
            weight = jnp.where(usable, weight, 0.0)
        fresh_weight = jnp.where(allowed, jnp.exp(fresh - top), 0.0)
        total = jnp.sum(weight, axis=1, keepdims=True) + jnp.sum(
            fresh_weight, axis=1, keepdims=True
        )
        weight = weight.astype(jnp.bfloat16)
        fresh_weight = fresh_weight.astype(jnp.bfloat16)
        shape = (all_rows, LANES)
        part = iota(shape, 1) // HEADS
        spread = jnp.zeros(shape, jnp.float32)
        for place, piece in enumerate(three_parts(top) + three_parts(total)):
            spread = jnp.where(part == place, piece, spread)
        spread = jnp.where(iota(shape, 1) % HEADS == iota(shape, 0) // steps, spread, 0.0)
        pick = iota((ROWS, all_rows), 1) % steps == iota((ROWS, all_rows), 0)
        gathered = jnp.dot(
            jnp.where(pick, 1.0, 0.0).astype(jnp.bfloat16),
            spread.astype(jnp.bfloat16),
            preferred_element_type=jnp.float32,
        )
        meta[r * steps : (r + 1) * steps, :] = gathered[:steps]
        value_move.wait()
        for c in range(chunks):
            part_rows = slice(c * rows, (c + 1) * rows)
            lanes = slice(c * 256, (c + 1) * 256)
            mixed = jnp.dot(
                weight[part_rows],
                vbuf[r, pl.ds(0, count), lanes],
                preferred_element_type=jnp.float32,
            ) + jnp.dot(
                fresh_weight[part_rows], fresh_v[:, lanes], preferred_element_type=jnp.float32
            )
            mixed = jnp.where(diag, mixed, 0.0)
            half = mixed[: 2 * steps]
            for g in range(1, group // 2):
                half = half + mixed[2 * steps * g : 2 * steps * (g + 1)]
            acc[r * steps : (r + 1) * steps, lanes] = half[:steps] + half[steps:]

    for r in range(requests):

        @pl.when(left[r] >= block)
        def _():
            one(r, block, True)

        @pl.when((left[r] > 0) & (left[r] < block))
        def _():
            one(r, SHORT, False)

        @pl.when(left[r] <= 0)
        def _():
            shape = (steps, LANES)
            hi, mid, low = three_parts(jnp.full(shape, masked_score, jnp.float32))
            part = iota(shape, 1) // HEADS
            meta[r * steps : (r + 1) * steps, :] = jnp.where(
                part == 0, hi, jnp.where(part == 1, mid, jnp.where(part == 2, low, 0.0))
            )

    out_ref[:, :width] = acc[...].astype(jnp.bfloat16)
    out_ref[:, width:] = meta[...].astype(jnp.bfloat16)


def project(count, columns, ids_ref, hidden_ref, gain_ref, weight_ref, *refs):
    parts = refs[:count]
    attn_ref, own_ref, send_ref, attn_buf, res_buf = refs[count:]
    requests, steps, width = hidden_ref.shape
    feature = attn_ref.shape[2]
    head = width // HEADS
    seq = lax.axis_index("seq")
    tp = lax.axis_index("tp")

    def moved(x, amount):
        return pltpu.roll(x, LANES - amount, 1)

    tops, totals = [], []
    for ref in parts:
        x = ref[:, width:].astype(jnp.float32)
        tops.append(x + moved(x, HEADS) + moved(x, 2 * HEADS))
        totals.append(moved(x, 3 * HEADS) + moved(x, 4 * HEADS) + moved(x, 5 * HEADS))
    overall = functools.reduce(jnp.maximum, tops)
    factors = [jnp.exp(top - overall) for top in tops]
    total = functools.reduce(jnp.add, [f * t for f, t in zip(factors, totals)])
    real = iota(total.shape, 1) < HEADS
    inverse = jnp.where(real, 1.0 / jnp.where(real, total, 1.0), 0.0)
    ratio = jnp.concatenate([jnp.where(real, f, 0.0) * inverse for f in factors], axis=0)
    expand = jnp.where(
        (iota((LANES, width), 0) % HEADS == iota((LANES, width), 1) // head)
        & (iota((LANES, width), 0) < 3 * HEADS),
        1.0,
        0.0,
    ).astype(jnp.bfloat16)
    hi, mid, low = three_parts(ratio)
    packed = hi + pltpu.roll(mid, HEADS, 1) + pltpu.roll(low, 2 * HEADS, 1)
    wide = jnp.dot(packed.astype(jnp.bfloat16), expand, preferred_element_type=jnp.float32)
    context = jnp.zeros((ROWS, width), jnp.float32)
    for b, ref in enumerate(parts):
        context = context + wide[b * ROWS : (b + 1) * ROWS] * ref[:, :width].astype(jnp.float32)
    attention = jnp.dot(
        context.astype(jnp.bfloat16), weight_ref[...], preferred_element_type=jnp.float32
    )
    hidden = [hidden_ref[r].astype(jnp.float32) for r in range(requests)]
    hidden.append(jnp.zeros((ROWS - requests * steps, width), jnp.float32))
    residual = jnp.concatenate(hidden, axis=0) + attention
    normed = (
        residual
        * lax.rsqrt(jnp.mean(residual * residual, axis=1, keepdims=True) + norm_epsilon)
        * gain_ref[...]
    )
    row = iota((ROWS, columns), 0)
    lane = iota((ROWS, columns), 1) - tp * ROWS
    extra = jnp.where((lane >= 0) & (lane < ROWS), -1.0, 0.0)
    for i in range(requests * steps):
        first, second = [
            ids_ref[i // steps, k, i % steps].astype(jnp.float32) for k in range(2)
        ]
        extra = jnp.where(lane == i, jnp.where(row == requests * steps, first, second), extra)
    tail = row >= requests * steps
    message = jnp.concatenate(
        [jnp.where(tail, extra, normed[:, :columns]), normed[:, columns:]], axis=1
    ).astype(jnp.bfloat16)
    send_ref[...] = message
    attn_buf[...] = attention
    res_buf[...] = residual
    lanes = pl.ds(pl.multiple_of(seq * feature, feature), feature)
    mine = attn_buf[:, lanes]
    for r in range(requests):
        attn_ref[r] = mine[r * steps : (r + 1) * steps].astype(jnp.bfloat16)
    rest = res_buf[:, lanes]
    for r in range(requests):
        own_ref[r] = rest[r * steps : (r + 1) * steps]


def feed(
    capacity, steps, used, slices, router_ref, gate_ref, up_ref, down_ref, near_ref, far_ref,
    out_ref, tokens,
):
    half = near_ref.shape[0]
    count = 2 * half
    width = gate_ref.shape[1]
    experts = router_ref.shape[0]
    seq_size, _, requests, _, feature = out_ref.shape
    seq = lax.axis_index("seq")
    tp = lax.axis_index("tp")
    columns = count * ROWS
    core = tp % 2
    for d in range(half):
        chip = (tp // 2) ^ d
        for ref, which in ((near_ref, core), (far_ref, 1 - core)):
            start = pl.multiple_of((2 * chip + which) * ROWS, ROWS)
            tokens[pl.ds(start, ROWS), :] = ref[d]
    ids = jnp.zeros((8, columns), jnp.float32)
    for p in range(count):
        ids = ids + tokens[p * ROWS : (p + 1) * ROWS, :columns].astype(jnp.float32)[8:]
    place = used - 8
    first = ids[place : place + 1]
    second = ids[place + 1 : place + 2]
    mine = (seq * count + tp) // slices
    mine_f = mine.astype(jnp.float32)
    hit = jnp.where((first == mine_f) | (second == mine_f), 1.0, 0.0)
    other = jnp.where(first == mine_f, second, first)
    earlier = (iota((columns, columns), 0) < iota((columns, columns), 1)) & (
        iota((columns, columns), 0) % steps == iota((columns, columns), 1) % steps
    )
    slot = jnp.dot(
        jnp.broadcast_to(hit, (ROWS, columns)).astype(jnp.bfloat16),
        jnp.where(earlier, 1.0, 0.0).astype(jnp.bfloat16),
        preferred_element_type=jnp.float32,
    )[:1]
    rows = -(-steps * capacity // ROWS) * ROWS
    row = iota((rows, columns), 0)
    choose = (
        (hit > 0.5)
        & (slot == (row % capacity).astype(jnp.float32))
        & (iota((rows, columns), 1) % steps == row // capacity)
    )
    select = jnp.where(choose, 1.0, 0.0)
    rival = jnp.sum(select * other, axis=1, keepdims=True)
    select = select.astype(jnp.bfloat16)
    buffer = jnp.dot(select, tokens[...], preferred_element_type=jnp.float32).astype(jnp.bfloat16)
    logits = lax.dot_general(buffer, router_ref[...], NT, preferred_element_type=jnp.float32)
    index = iota((rows, experts), 1)
    ahead = jnp.sum(jnp.where(index == mine, logits, 0.0), axis=1, keepdims=True)
    behind = jnp.sum(
        jnp.where(index.astype(jnp.float32) == rival, logits, 0.0), axis=1, keepdims=True
    )
    share = 1.0 / (1.0 + jnp.exp(behind - ahead))
    gate = lax.dot_general(buffer, gate_ref[...], NT, preferred_element_type=jnp.float32)
    upward = lax.dot_general(buffer, up_ref[...], NT, preferred_element_type=jnp.float32)
    inner = (jax.nn.gelu(gate) * upward).astype(jnp.bfloat16)
    produced = jnp.dot(inner, down_ref[...], preferred_element_type=jnp.float32)
    shared = (produced * share).astype(jnp.bfloat16)
    term = lax.dot_general(select, shared, TN, preferred_element_type=jnp.float32)
    for s in range(seq_size):
        for p in range(count):
            for r in range(requests):
                start = p * ROWS + r * steps
                out_ref[s, p, r] = term[
                    start : start + steps, s * feature : (s + 1) * feature
                ].astype(jnp.bfloat16)


def limit(mebibytes):
    return pltpu.CompilerParams(vmem_limit_bytes=mebibytes * 1024 * 1024)


def stage(count, *refs):
    sources, copies, sems = refs[1 : 1 + count], refs[1 + count : 1 + 2 * count], refs[-1]
    moves = [
        pltpu.make_async_copy(source, copy, sems.at[i])
        for i, (source, copy) in enumerate(zip(sources, copies))
    ]
    for move in moves:
        move.start()
    for move in moves:
        move.wait()


def staged(after, *arrays):
    anywhere = pl.BlockSpec(memory_space=pl.ANY)
    count = len(arrays)
    size = sum(2 * x.size for x in arrays)
    return pl.pallas_call(
        functools.partial(stage, count),
        out_shape=tuple(pltpu.VMEM(x.shape, x.dtype) for x in arrays),
        in_specs=[anywhere] * (1 + count),
        out_specs=(anywhere,) * count,
        scratch_shapes=[pltpu.SemaphoreType.DMA((count,))],
        compiler_params=limit(4),
        cost_estimate=pl.CostEstimate(flops=0, bytes_accessed=2 * size, transcendentals=0),
        name="stage",
    )(after, *[pltpu.with_memory_space_constraint(x, pltpu.HBM) for x in arrays])


def body(
    hidden_in,
    new_query,
    new_key,
    new_value,
    key_cache,
    value_cache,
    lengths,
    out_weight,
    norm_gain,
    router_weight,
    expert_ids,
    gate_weight,
    up_weight,
    down_weight,
):
    requests, steps, width = hidden_in.shape
    block = key_cache.shape[1]
    seq_size = lax.axis_size("seq")
    tp_size = lax.axis_size("tp")
    feature = width // seq_size
    experts = router_weight.shape[1]
    topk = expert_ids.shape[2]
    capacity = (5 * requests * tp_size * topk + 4 * experts - 1) // (4 * experts)
    slices = seq_size * tp_size // experts
    vmem = pl.BlockSpec(memory_space=pltpu.VMEM)
    smem = pl.BlockSpec(memory_space=pltpu.SMEM)
    hbm = pl.BlockSpec(memory_space=pltpu.HBM)

    small = pltpu.VMEM((requests, steps, width), jnp.bfloat16)
    part = pl.pallas_call(
        attend,
        out_shape=pltpu.VMEM((ROWS, width + LANES), jnp.bfloat16),
        in_specs=[hbm] * 6,
        out_specs=vmem,
        scratch_shapes=[
            pltpu.SMEM((requests,), jnp.int32),
            small,
            small,
            small,
            pltpu.VMEM((requests, block, width), jnp.bfloat16),
            pltpu.VMEM((requests, block, width), jnp.bfloat16),
            pltpu.VMEM((ROWS, width), jnp.float32),
            pltpu.VMEM((ROWS, LANES), jnp.float32),
            pltpu.SemaphoreType.DMA((2, requests)),
            pltpu.SemaphoreType.DMA((4,)),
        ],
        compiler_params=limit(20),
        name="attend",
    )(
        *[
            pltpu.with_memory_space_constraint(x, pltpu.HBM)
            for x in (lengths, new_query, new_key, new_value, key_cache, value_cache)
        ]
    )

    def swapped(x, axis, size, d):
        return lax.ppermute(x, axis, [(i, i ^ d) for i in range(size)])

    out_weight, gate_weight = staged(part, out_weight, gate_weight)
    parts = [part] + [swapped(part, "seq", seq_size, d) for d in range(1, seq_size)]
    attn_out, own_residual, packed = pl.pallas_call(
        functools.partial(project, seq_size, tp_size * ROWS),
        out_shape=(
            jax.ShapeDtypeStruct((requests, steps, feature), jnp.bfloat16),
            jax.ShapeDtypeStruct((requests, steps, feature), jnp.float32),
            jax.ShapeDtypeStruct((ROWS, width), jnp.bfloat16),
        ),
        in_specs=[smem] + [vmem] * (3 + seq_size),
        out_specs=(vmem, vmem, vmem),
        scratch_shapes=[
            pltpu.VMEM((ROWS, width), jnp.float32),
            pltpu.VMEM((ROWS, width), jnp.float32),
        ],
        compiler_params=limit(8),
        name="project",
    )(expert_ids.transpose(0, 2, 1), hidden_in, norm_gain.reshape(1, width), out_weight, *parts)
    up_weight, down_weight = staged(packed, up_weight, down_weight)
    near = jnp.stack(
        [packed] + [swapped(packed, "tp", tp_size, 2 * d) for d in range(1, tp_size // 2)]
    )
    far = swapped(near, "tp", tp_size, 1)
    terms = pl.pallas_call(
        functools.partial(feed, capacity, steps, requests * steps, slices),
        out_shape=jax.ShapeDtypeStruct(
            (seq_size, tp_size, requests, steps, feature), jnp.bfloat16
        ),
        in_specs=[vmem] * 6,
        out_specs=vmem,
        scratch_shapes=[pltpu.VMEM((tp_size * ROWS, width), jnp.bfloat16)],
        compiler_params=limit(16),
        name="feed",
    )(router_weight.T, gate_weight, up_weight, down_weight, near, far)
    terms = terms.reshape(seq_size * tp_size, requests, steps, feature)
    arrived = lax.all_to_all(terms, ("seq", "tp"), 0, 0, tiled=True)
    mixture = jnp.sum(arrived.astype(jnp.float32), axis=0)
    return (attn_out, (own_residual + mixture).astype(jnp.bfloat16))


def solution(mesh):
    return jax.shard_map(
        body,
        mesh=mesh,
        in_specs=(
            P("tp", None, None),
            P("tp", None, None),
            P("tp", None, None),
            P("tp", None, None),
            P("tp", "seq", None),
            P("tp", "seq", None),
            P("tp"),
            P(),
            P(),
            P(),
            P("tp", None, None),
            P(("seq", "tp"), None),
            P(("seq", "tp"), None),
            P(("seq", "tp"), None),
        ),
        out_specs=(P("tp", None, "seq"), P("tp", None, "seq")),
        check_vma=False,
    )
```

```python
import functools

import jax
import jax.numpy as jnp
from jax import lax
from jax.experimental import pallas as pl
from jax.experimental.pallas import tpu as pltpu
from jax.sharding import PartitionSpec as P

HEADS = 16
SHORT = 128
ROWS = 16
LANES = 128
PIECES = 4
masked_score = -1e30
norm_epsilon = 1e-06
NT = (((1,), (1,)), ((), ()))
TN = (((0,), (0,)), ((), ()))


def iota(shape, dim):
    return lax.broadcasted_iota(jnp.int32, shape, dim)


def three_parts(x):
    hi = x.astype(jnp.bfloat16).astype(jnp.float32)
    mid = (x - hi).astype(jnp.bfloat16).astype(jnp.float32)
    return hi, mid, x - hi - mid


def tiled(x, times):
    return jnp.concatenate([x] * times, axis=0)


def attend(
    lens_hbm, q_hbm, nk_hbm, nv_hbm, k_hbm, v_hbm, out_ref,
    lens, q_ref, nk_ref, nv_ref, kbuf, vbuf, sems, small_sems,
):
    requests, block, width = k_hbm.shape
    steps = q_ref.shape[1]
    head = width // HEADS
    scale = head ** (-0.5)
    group = 256 // head
    chunks = width // 256
    rows = group * steps
    seq = lax.axis_index("seq")

    def moves(r, count):
        pair = []
        for which, (src, dst) in enumerate(((k_hbm, kbuf), (v_hbm, vbuf))):
            pair.append(
                pltpu.make_async_copy(
                    src.at[r, pl.ds(0, count)], dst.at[r, pl.ds(0, count)], sems.at[which, r]
                )
            )
        return pair

    small = [
        pltpu.make_async_copy(src, dst, small_sems.at[i])
        for i, (src, dst) in enumerate(
            ((lens_hbm, lens), (q_hbm, q_ref), (nk_hbm, nk_ref), (nv_hbm, nv_ref))
        )
    ]
    for move in small:
        move.start()
    small[0].wait()
    left = [lens[r] - seq * block for r in range(requests)]
    def begin(r, count, pieces):
        size = count // pieces
        for which, (src, dst) in enumerate(((k_hbm, kbuf), (v_hbm, vbuf))):
            for i in range(pieces):
                part = pl.ds(i * size, size)
                pltpu.make_async_copy(
                    src.at[r, part], dst.at[r, part], sems.at[which, r]
                ).start()

    full = [left[r] >= block for r in range(requests)]
    short = [(left[r] > 0) & (left[r] < block) for r in range(requests)]
    for r in range(requests):

        @pl.when(short[r])
        def _():
            begin(r, SHORT, 1)

    for r in range(requests):

        @pl.when(full[r])
        def _():
            begin(r, block, PIECES)

    for move in small[1:]:
        move.wait()
    diag = iota((rows, 256), 0) // steps == iota((rows, 256), 1) // head
    diag_all = iota((rows, width), 0) // steps == (iota((rows, width), 1) % 256) // head
    all_rows = chunks * rows

    def one(r, count, whole):
        key_move, value_move = moves(r, count)
        tiled_q = tiled(q_ref[r].astype(jnp.float32), group)
        query = jnp.where(diag_all, tiled_q, 0.0).astype(jnp.bfloat16)
        fresh_k = tiled(nk_ref[r].astype(jnp.float32), group).astype(jnp.bfloat16)
        fresh_v = tiled(nv_ref[r].astype(jnp.float32), group).astype(jnp.bfloat16)
        fresh = jnp.concatenate(
            [
                lax.dot_general(
                    query[:, c * 256 : (c + 1) * 256],
                    fresh_k[:, c * 256 : (c + 1) * 256],
                    NT,
                    preferred_element_type=jnp.float32,
                )
                for c in range(chunks)
            ],
            axis=0,
        )
        row = iota(fresh.shape, 0)
        column = iota(fresh.shape, 1)
        allowed = (column < steps) & (column <= row % steps) & (seq == 0)
        fresh = jnp.where(allowed, fresh * scale, masked_score)
        key_move.wait()
        score = (
            jnp.concatenate(
                [
                    lax.dot_general(
                        query[:, c * 256 : (c + 1) * 256],
                        kbuf[r, pl.ds(0, count), c * 256 : (c + 1) * 256],
                        NT,
                        preferred_element_type=jnp.float32,
                    )
                    for c in range(chunks)
                ],
                axis=0,
            )
            * scale
        )
        usable = iota(score.shape, 1) < left[r]
        if not whole:
            score = jnp.where(usable, score, masked_score)
        top = jnp.maximum(
            jnp.max(score, axis=1, keepdims=True), jnp.max(fresh, axis=1, keepdims=True)
        )
        weight = jnp.exp(score - top)
        if not whole:
            weight = jnp.where(usable, weight, 0.0)
        fresh_weight = jnp.where(allowed, jnp.exp(fresh - top), 0.0)
        total = jnp.sum(weight, axis=1, keepdims=True) + jnp.sum(
            fresh_weight, axis=1, keepdims=True
        )
        weight = weight.astype(jnp.bfloat16)
        fresh_weight = fresh_weight.astype(jnp.bfloat16)
        shape = (all_rows, LANES)
        part = iota(shape, 1) // HEADS
        spread = jnp.zeros(shape, jnp.float32)
        for place, piece in enumerate(three_parts(top) + three_parts(total)):
            spread = jnp.where(part == place, piece, spread)
        spread = jnp.where(iota(shape, 1) % HEADS == iota(shape, 0) // steps, spread, 0.0)
        pick = iota((ROWS, all_rows), 1) % steps == iota((ROWS, all_rows), 0)
        gathered = jnp.dot(
            jnp.where(pick, 1.0, 0.0).astype(jnp.bfloat16),
            spread.astype(jnp.bfloat16),
            preferred_element_type=jnp.float32,
        )
        out_ref[r, :, width:] = gathered[:steps].astype(jnp.bfloat16)
        value_move.wait()
        for c in range(chunks):
            part_rows = slice(c * rows, (c + 1) * rows)
            lanes = slice(c * 256, (c + 1) * 256)
            mixed = jnp.dot(
                weight[part_rows],
                vbuf[r, pl.ds(0, count), lanes],
                preferred_element_type=jnp.float32,
            ) + jnp.dot(
                fresh_weight[part_rows], fresh_v[:, lanes], preferred_element_type=jnp.float32
            )
            mixed = jnp.where(diag, mixed, 0.0)
            half = mixed[: 2 * steps]
            for g in range(1, group // 2):
                half = half + mixed[2 * steps * g : 2 * steps * (g + 1)]
            out_ref[r, :, lanes] = (half[:steps] + half[steps:]).astype(jnp.bfloat16)

    for r in range(requests):

        @pl.when(left[r] <= 0)
        def _():
            shape = (steps, LANES)
            hi, mid, low = three_parts(jnp.full(shape, masked_score, jnp.float32))
            part = iota(shape, 1) // HEADS
            empty = jnp.where(part == 0, hi, jnp.where(part == 1, mid, low))
            out_ref[r, :, width:] = jnp.where(part < 3, empty, 0.0).astype(jnp.bfloat16)
            out_ref[r, :, :width] = jnp.zeros((steps, width), jnp.bfloat16)

        @pl.when(short[r])
        def _():
            one(r, SHORT, False)

    for r in range(requests):

        @pl.when(full[r])
        def _():
            one(r, block, True)


def project(count, columns, ids_ref, hidden_ref, gain_ref, weight_ref, *refs):
    parts = refs[:count]
    attn_ref, own_ref, send_ref, attn_buf, res_buf = refs[count:]
    requests, steps, width = hidden_ref.shape
    feature = attn_ref.shape[2]
    head = width // HEADS
    seq = lax.axis_index("seq")
    tp = lax.axis_index("tp")

    def moved(x, amount):
        return pltpu.roll(x, LANES - amount, 1)

    def rows_of(ref, lanes):
        pieces = [ref[r, :, lanes].astype(jnp.float32) for r in range(requests)]
        blank = jnp.zeros((ROWS - requests * steps, pieces[0].shape[1]), jnp.float32)
        return jnp.concatenate(pieces + [blank], axis=0)

    tops, totals = [], []
    for ref in parts:
        x = rows_of(ref, slice(width, width + LANES))
        tops.append(x + moved(x, HEADS) + moved(x, 2 * HEADS))
        totals.append(moved(x, 3 * HEADS) + moved(x, 4 * HEADS) + moved(x, 5 * HEADS))
    overall = functools.reduce(jnp.maximum, tops)
    factors = [jnp.exp(top - overall) for top in tops]
    total = functools.reduce(jnp.add, [f * t for f, t in zip(factors, totals)])
    real = (iota(total.shape, 1) < HEADS) & (iota(total.shape, 0) < requests * steps)
    inverse = jnp.where(real, 1.0 / jnp.where(real, total, 1.0), 0.0)
    ratio = jnp.concatenate([jnp.where(real, f, 0.0) * inverse for f in factors], axis=0)
    expand = jnp.where(
        (iota((LANES, width), 0) % HEADS == iota((LANES, width), 1) // head)
        & (iota((LANES, width), 0) < 3 * HEADS),
        1.0,
        0.0,
    ).astype(jnp.bfloat16)
    hi, mid, low = three_parts(ratio)
    packed = hi + pltpu.roll(mid, HEADS, 1) + pltpu.roll(low, 2 * HEADS, 1)
    wide = jnp.dot(packed.astype(jnp.bfloat16), expand, preferred_element_type=jnp.float32)
    context = jnp.zeros((ROWS, width), jnp.float32)
    for b, ref in enumerate(parts):
        context = context + wide[b * ROWS : (b + 1) * ROWS] * rows_of(ref, slice(0, width))
    attention = jnp.dot(
        context.astype(jnp.bfloat16), weight_ref[...], preferred_element_type=jnp.float32
    )
    residual = rows_of(hidden_ref, slice(0, width)) + attention
    normed = (
        residual
        * lax.rsqrt(jnp.mean(residual * residual, axis=1, keepdims=True) + norm_epsilon)
        * gain_ref[...]
    )
    row = iota((ROWS, columns), 0)
    lane = iota((ROWS, columns), 1) - tp * ROWS
    extra = jnp.where((lane >= 0) & (lane < ROWS), -1.0, 0.0)
    for i in range(requests * steps):
        first, second = [
            ids_ref[i // steps, k, i % steps].astype(jnp.float32) for k in range(2)
        ]
        extra = jnp.where(lane == i, jnp.where(row == requests * steps, first, second), extra)
    tail = row >= requests * steps
    message = jnp.concatenate(
        [jnp.where(tail, extra, normed[:, :columns]), normed[:, columns:]], axis=1
    ).astype(jnp.bfloat16)
    send_ref[...] = message
    attn_buf[...] = attention
    res_buf[...] = residual
    lanes = pl.ds(pl.multiple_of(seq * feature, feature), feature)
    mine = attn_buf[:, lanes]
    for r in range(requests):
        attn_ref[r] = mine[r * steps : (r + 1) * steps].astype(jnp.bfloat16)
    rest = res_buf[:, lanes]
    for r in range(requests):
        own_ref[r] = rest[r * steps : (r + 1) * steps]


def feed(
    capacity, steps, used, slices, router_ref, gate_ref, up_ref, down_ref, near_ref, far_ref,
    out_ref, tokens,
):
    half = near_ref.shape[0]
    count = 2 * half
    width = gate_ref.shape[1]
    experts = router_ref.shape[0]
    seq_size, _, requests, _, feature = out_ref.shape
    seq = lax.axis_index("seq")
    tp = lax.axis_index("tp")
    columns = count * ROWS
    core = tp % 2
    for d in range(half):
        chip = (tp // 2) ^ d
        for ref, which in ((near_ref, core), (far_ref, 1 - core)):
            start = pl.multiple_of((2 * chip + which) * ROWS, ROWS)
            tokens[pl.ds(start, ROWS), :] = ref[d]
    ids = jnp.zeros((8, columns), jnp.float32)
    for p in range(count):
        ids = ids + tokens[p * ROWS : (p + 1) * ROWS, :columns].astype(jnp.float32)[8:]
    place = used - 8
    first = ids[place : place + 1]
    second = ids[place + 1 : place + 2]
    mine = (seq * count + tp) // slices
    mine_f = mine.astype(jnp.float32)
    hit = jnp.where((first == mine_f) | (second == mine_f), 1.0, 0.0)
    other = jnp.where(first == mine_f, second, first)
    earlier = (iota((columns, columns), 0) < iota((columns, columns), 1)) & (
        iota((columns, columns), 0) % steps == iota((columns, columns), 1) % steps
    )
    slot = jnp.dot(
        jnp.broadcast_to(hit, (ROWS, columns)).astype(jnp.bfloat16),
        jnp.where(earlier, 1.0, 0.0).astype(jnp.bfloat16),
        preferred_element_type=jnp.float32,
    )[:1]
    rows = -(-steps * capacity // ROWS) * ROWS
    row = iota((rows, columns), 0)
    choose = (
        (hit > 0.5)
        & (slot == (row % capacity).astype(jnp.float32))
        & (iota((rows, columns), 1) % steps == row // capacity)
    )
    select = jnp.where(choose, 1.0, 0.0)
    rival = jnp.sum(select * other, axis=1, keepdims=True)
    select = select.astype(jnp.bfloat16)
    buffer = jnp.dot(select, tokens[...], preferred_element_type=jnp.float32).astype(jnp.bfloat16)
    logits = lax.dot_general(buffer, router_ref[...], NT, preferred_element_type=jnp.float32)
    index = iota((rows, experts), 1)
    ahead = jnp.sum(jnp.where(index == mine, logits, 0.0), axis=1, keepdims=True)
    behind = jnp.sum(
        jnp.where(index.astype(jnp.float32) == rival, logits, 0.0), axis=1, keepdims=True
    )
    share = 1.0 / (1.0 + jnp.exp(behind - ahead))
    gate = lax.dot_general(buffer, gate_ref[...], NT, preferred_element_type=jnp.float32)
    upward = lax.dot_general(buffer, up_ref[...], NT, preferred_element_type=jnp.float32)
    inner = (jax.nn.gelu(gate) * upward).astype(jnp.bfloat16)
    produced = jnp.dot(inner, down_ref[...], preferred_element_type=jnp.float32)
    shared = (produced * share).astype(jnp.bfloat16)
    term = lax.dot_general(select, shared, TN, preferred_element_type=jnp.float32)
    for s in range(seq_size):
        for p in range(count):
            for r in range(requests):
                start = p * ROWS + r * steps
                out_ref[s, p, r] = term[
                    start : start + steps, s * feature : (s + 1) * feature
                ].astype(jnp.bfloat16)


def limit(mebibytes):
    return pltpu.CompilerParams(vmem_limit_bytes=mebibytes * 1024 * 1024)


def stage(count, *refs):
    sources, copies, sems = refs[1 : 1 + count], refs[1 + count : 1 + 2 * count], refs[-1]
    for i, (source, copy) in enumerate(zip(sources, copies)):
        pieces = PIECES if source.shape[0] % (16 * PIECES) == 0 else 1
        size = source.shape[0] // pieces
        for piece in range(pieces):
            part = pl.ds(piece * size, size)
            pltpu.make_async_copy(source.at[part], copy.at[part], sems.at[i]).start()
    for i, (source, copy) in enumerate(zip(sources, copies)):
        pltpu.make_async_copy(source, copy, sems.at[i]).wait()


def staged(after, *arrays):
    anywhere = pl.BlockSpec(memory_space=pl.ANY)
    count = len(arrays)
    size = sum(2 * x.size for x in arrays)
    return pl.pallas_call(
        functools.partial(stage, count),
        out_shape=tuple(pltpu.VMEM(x.shape, x.dtype) for x in arrays),
        in_specs=[anywhere] * (1 + count),
        out_specs=(anywhere,) * count,
        scratch_shapes=[pltpu.SemaphoreType.DMA((count,))],
        compiler_params=limit(4),
        cost_estimate=pl.CostEstimate(flops=0, bytes_accessed=2 * size, transcendentals=0),
        name="stage",
    )(after, *[pltpu.with_memory_space_constraint(x, pltpu.HBM) for x in arrays])


def body(
    hidden_in,
    new_query,
    new_key,
    new_value,
    key_cache,
    value_cache,
    lengths,
    out_weight,
    norm_gain,
    router_weight,
    expert_ids,
    gate_weight,
    up_weight,
    down_weight,
):
    requests, steps, width = hidden_in.shape
    block = key_cache.shape[1]
    seq_size = lax.axis_size("seq")
    tp_size = lax.axis_size("tp")
    feature = width // seq_size
    experts = router_weight.shape[1]
    topk = expert_ids.shape[2]
    capacity = (5 * requests * tp_size * topk + 4 * experts - 1) // (4 * experts)
    slices = seq_size * tp_size // experts
    vmem = pl.BlockSpec(memory_space=pltpu.VMEM)
    smem = pl.BlockSpec(memory_space=pltpu.SMEM)
    hbm = pl.BlockSpec(memory_space=pltpu.HBM)

    small = pltpu.VMEM((requests, steps, width), jnp.bfloat16)
    part = pl.pallas_call(
        attend,
        out_shape=pltpu.VMEM((requests, steps, width + LANES), jnp.bfloat16),
        in_specs=[hbm] * 6,
        out_specs=vmem,
        scratch_shapes=[
            pltpu.SMEM((requests,), jnp.int32),
            small,
            small,
            small,
            pltpu.VMEM((requests, block, width), jnp.bfloat16),
            pltpu.VMEM((requests, block, width), jnp.bfloat16),
            pltpu.SemaphoreType.DMA((2, requests)),
            pltpu.SemaphoreType.DMA((4,)),
        ],
        compiler_params=limit(20),
        name="attend",
    )(
        *[
            pltpu.with_memory_space_constraint(x, pltpu.HBM)
            for x in (lengths, new_query, new_key, new_value, key_cache, value_cache)
        ]
    )

    def swapped(x, axis, size, d):
        return lax.ppermute(x, axis, [(i, i ^ d) for i in range(size)])

    out_weight, gate_weight = staged(part, out_weight, gate_weight)
    parts = [part] + [swapped(part, "seq", seq_size, d) for d in range(1, seq_size)]
    attn_out, own_residual, packed = pl.pallas_call(
        functools.partial(project, seq_size, tp_size * ROWS),
        out_shape=(
            pltpu.VMEM((requests, steps, feature), jnp.bfloat16),
            jax.ShapeDtypeStruct((requests, steps, feature), jnp.float32),
            jax.ShapeDtypeStruct((ROWS, width), jnp.bfloat16),
        ),
        in_specs=[smem] + [vmem] * (3 + seq_size),
        out_specs=(vmem, vmem, vmem),
        scratch_shapes=[
            pltpu.VMEM((ROWS, width), jnp.float32),
            pltpu.VMEM((ROWS, width), jnp.float32),
        ],
        compiler_params=limit(8),
        name="project",
    )(expert_ids.transpose(0, 2, 1), hidden_in, norm_gain.reshape(1, width), out_weight, *parts)
    up_weight, down_weight = staged(packed, up_weight, down_weight)
    near = jnp.stack(
        [packed] + [swapped(packed, "tp", tp_size, 2 * d) for d in range(1, tp_size // 2)]
    )
    near, up_weight, down_weight = lax.optimization_barrier((near, up_weight, down_weight))
    far = swapped(near, "tp", tp_size, 1)
    terms = pl.pallas_call(
        functools.partial(feed, capacity, steps, requests * steps, slices),
        out_shape=jax.ShapeDtypeStruct(
            (seq_size, tp_size, requests, steps, feature), jnp.bfloat16
        ),
        in_specs=[vmem] * 6,
        out_specs=vmem,
        scratch_shapes=[pltpu.VMEM((tp_size * ROWS, width), jnp.bfloat16)],
        compiler_params=limit(16),
        name="feed",
    )(router_weight.T, gate_weight, up_weight, down_weight, near, far)
    terms = terms.reshape(seq_size * tp_size, requests, steps, feature)
    arrived = lax.all_to_all(terms, ("seq", "tp"), 0, 0, tiled=True)
    mixture = jnp.sum(arrived.astype(jnp.float32), axis=0)
    return (attn_out, (own_residual + mixture).astype(jnp.bfloat16))


def solution(mesh):
    return jax.shard_map(
        body,
        mesh=mesh,
        in_specs=(
            P("tp", None, None),
            P("tp", None, None),
            P("tp", None, None),
            P("tp", None, None),
            P("tp", "seq", None),
            P("tp", "seq", None),
            P("tp"),
            P(),
            P(),
            P(),
            P("tp", None, None),
            P(("seq", "tp"), None),
            P(("seq", "tp"), None),
            P(("seq", "tp"), None),
        ),
        out_specs=(P("tp", None, "seq"), P("tp", None, "seq")),
        check_vma=False,
    )
```

```python
import functools

import jax
import jax.numpy as jnp
from jax import lax
from jax.experimental import pallas as pl
from jax.experimental.pallas import tpu as pltpu
from jax.sharding import PartitionSpec as P

HEADS = 16
SHORT = 128
ROWS = 16
LANES = 128
PIECES = 4
masked_score = -1e30
norm_epsilon = 1e-06
NT = (((1,), (1,)), ((), ()))
TN = (((0,), (0,)), ((), ()))


def iota(shape, dim):
    return lax.broadcasted_iota(jnp.int32, shape, dim)


def three_parts(x):
    hi = x.astype(jnp.bfloat16).astype(jnp.float32)
    mid = (x - hi).astype(jnp.bfloat16).astype(jnp.float32)
    return hi, mid, x - hi - mid


def tiled(x, times):
    return jnp.concatenate([x] * times, axis=0)


def attend(
    lens_hbm, q_hbm, nk_hbm, nv_hbm, k_hbm, v_hbm, out_ref,
    lens, q_ref, nk_ref, nv_ref, kbuf, vbuf, kshort, vshort, sems, short_sems, small_sems,
):
    requests, block, width = k_hbm.shape
    steps = q_ref.shape[1]
    head = width // HEADS
    scale = head ** (-0.5)
    group = 256 // head
    chunks = width // 256
    rows = group * steps
    piece = block // PIECES
    seq = lax.axis_index("seq")
    small = [
        pltpu.make_async_copy(src, dst, small_sems.at[i])
        for i, (src, dst) in enumerate(
            ((lens_hbm, lens), (q_hbm, q_ref), (nk_hbm, nk_ref), (nv_hbm, nv_ref))
        )
    ]
    for move in small:
        move.start()
    small[0].wait()
    left = [lens[r] - seq * block for r in range(requests)]
    full = [left[r] >= block for r in range(requests)]
    short = [(left[r] > 0) & (left[r] < block) for r in range(requests)]
    some_short = functools.reduce(jnp.logical_or, short)

    def short_move(which, r):
        src, dst = ((k_hbm, kshort), (v_hbm, vshort))[which]
        return pltpu.make_async_copy(
            src.at[r, pl.ds(0, SHORT)], dst.at[r], short_sems.at[which, r]
        )

    def move(which, r, i):
        src, dst = ((k_hbm, kbuf), (v_hbm, vbuf))[which]
        part = pl.ds(i * piece, piece)
        return pltpu.make_async_copy(src.at[r, part], dst.at[r, part], sems.at[which, r, i])

    @pl.when(some_short)
    def _():
        for which in range(2):
            for r in range(requests):
                short_move(which, r).start()

    for r in range(requests):

        @pl.when(full[r])
        def _():
            for which in range(2):
                for i in range(PIECES):
                    move(which, r, i).start()

    for move_small in small[1:]:
        move_small.wait()
    diag = iota((rows, 256), 0) // steps == iota((rows, 256), 1) // head
    diag_all = iota((rows, width), 0) // steps == (iota((rows, width), 1) % 256) // head
    all_rows = chunks * rows

    def columns(c):
        return slice(c * 256, (c + 1) * 256)

    def against(query, keys):
        return jnp.concatenate(
            [
                lax.dot_general(
                    query[:, columns(c)], keys(c), NT, preferred_element_type=jnp.float32
                )
                for c in range(chunks)
            ],
            axis=0,
        )

    def prepare(r):
        tiled_q = tiled(q_ref[r].astype(jnp.float32), group)
        query = jnp.where(diag_all, tiled_q, 0.0).astype(jnp.bfloat16)
        fresh_k = tiled(nk_ref[r].astype(jnp.float32), group).astype(jnp.bfloat16)
        fresh_v = tiled(nv_ref[r].astype(jnp.float32), group).astype(jnp.bfloat16)
        fresh = against(query, lambda c: fresh_k[:, columns(c)])
        row = iota(fresh.shape, 0)
        column = iota(fresh.shape, 1)
        allowed = (column < steps) & (column <= row % steps) & (seq == 0)
        return query, jnp.where(allowed, fresh * scale, masked_score), allowed, fresh_v

    def summary(top, total):
        shape = (all_rows, LANES)
        part = iota(shape, 1) // HEADS
        spread = jnp.zeros(shape, jnp.float32)
        for place, value in enumerate(three_parts(top) + three_parts(total)):
            spread = jnp.where(part == place, value, spread)
        spread = jnp.where(iota(shape, 1) % HEADS == iota(shape, 0) // steps, spread, 0.0)
        pick = iota((ROWS, all_rows), 1) % steps == iota((ROWS, all_rows), 0)
        gathered = jnp.dot(
            jnp.where(pick, 1.0, 0.0).astype(jnp.bfloat16),
            spread.astype(jnp.bfloat16),
            preferred_element_type=jnp.float32,
        )
        return gathered[:steps].astype(jnp.bfloat16)

    def own_head(mixed):
        mixed = jnp.where(diag, mixed, 0.0)
        half = mixed[: 2 * steps]
        for g in range(1, group // 2):
            half = half + mixed[2 * steps * g : 2 * steps * (g + 1)]
        return (half[:steps] + half[steps:]).astype(jnp.bfloat16)

    def largest(x):
        return jnp.max(x, axis=1, keepdims=True)

    def summed(x):
        return jnp.sum(x, axis=1, keepdims=True)

    for r in range(requests):

        @pl.when(left[r] <= 0)
        def _():
            shape = (steps, LANES)
            hi, mid, low = three_parts(jnp.full(shape, masked_score, jnp.float32))
            part = iota(shape, 1) // HEADS
            empty = jnp.where(part == 0, hi, jnp.where(part == 1, mid, low))
            out_ref[r, :, width:] = jnp.where(part < 3, empty, 0.0).astype(jnp.bfloat16)
            out_ref[r, :, :width] = jnp.zeros((steps, width), jnp.bfloat16)

    @pl.when(some_short)
    def _():
        for which in range(2):
            for r in range(requests):
                short_move(which, r).wait()
        results = []
        for r in range(requests):
            query, fresh, allowed, fresh_v = prepare(r)
            score = against(query, lambda c: kshort[r, :, columns(c)]) * scale
            usable = iota(score.shape, 1) < left[r]
            score = jnp.where(usable, score, masked_score)
            top = jnp.maximum(largest(score), largest(fresh))
            weight = jnp.where(usable, jnp.exp(score - top), 0.0)
            fresh_weight = jnp.where(allowed, jnp.exp(fresh - top), 0.0)
            total = summed(weight) + summed(fresh_weight)
            weight = weight.astype(jnp.bfloat16)
            fresh_weight = fresh_weight.astype(jnp.bfloat16)
            mixed = []
            for c in range(chunks):
                part = slice(c * rows, (c + 1) * rows)
                value = jnp.dot(
                    weight[part], vshort[r, :, columns(c)], preferred_element_type=jnp.float32
                ) + jnp.dot(
                    fresh_weight[part], fresh_v[:, columns(c)], preferred_element_type=jnp.float32
                )
                mixed.append(own_head(value))
            results.append((summary(top, total), mixed))
        for r in range(requests):

            @pl.when(short[r])
            def _():
                out_ref[r, :, width:] = results[r][0]
                for c in range(chunks):
                    out_ref[r, :, columns(c)] = results[r][1][c]

    for r in range(requests):

        @pl.when(full[r])
        def _():
            query, fresh, allowed, fresh_v = prepare(r)
            scores = []
            top = largest(fresh)
            for i in range(PIECES):
                move(0, r, i).wait()
                scores.append(
                    against(query, lambda c: kbuf[r, pl.ds(i * piece, piece), columns(c)]) * scale
                )
            top = jnp.maximum(largest(functools.reduce(jnp.maximum, scores)), top)
            weights = [jnp.exp(score - top) for score in scores]
            fresh_weight = jnp.where(allowed, jnp.exp(fresh - top), 0.0)
            total = summed(functools.reduce(jnp.add, weights)) + summed(fresh_weight)
            weights = [weight.astype(jnp.bfloat16) for weight in weights]
            fresh_weight = fresh_weight.astype(jnp.bfloat16)
            out_ref[r, :, width:] = summary(top, total)
            mixed = [
                jnp.dot(
                    fresh_weight[c * rows : (c + 1) * rows],
                    fresh_v[:, columns(c)],
                    preferred_element_type=jnp.float32,
                )
                for c in range(chunks)
            ]
            for i in range(PIECES):
                move(1, r, i).wait()
                for c in range(chunks):
                    mixed[c] = mixed[c] + jnp.dot(
                        weights[i][c * rows : (c + 1) * rows],
                        vbuf[r, pl.ds(i * piece, piece), columns(c)],
                        preferred_element_type=jnp.float32,
                    )
            for c in range(chunks):
                out_ref[r, :, columns(c)] = own_head(mixed[c])


def project(count, columns, ids_ref, hidden_ref, gain_ref, weight_ref, *refs):
    parts = refs[:count]
    attn_ref, own_ref, send_ref, attn_buf, res_buf = refs[count:]
    requests, steps, width = hidden_ref.shape
    feature = attn_ref.shape[2]
    head = width // HEADS
    seq = lax.axis_index("seq")
    tp = lax.axis_index("tp")

    def moved(x, amount):
        return pltpu.roll(x, LANES - amount, 1)

    def rows_of(ref, lanes):
        pieces = [ref[r, :, lanes].astype(jnp.float32) for r in range(requests)]
        blank = jnp.zeros((ROWS - requests * steps, pieces[0].shape[1]), jnp.float32)
        return jnp.concatenate(pieces + [blank], axis=0)

    tops, totals = [], []
    for ref in parts:
        x = rows_of(ref, slice(width, width + LANES))
        tops.append(x + moved(x, HEADS) + moved(x, 2 * HEADS))
        totals.append(moved(x, 3 * HEADS) + moved(x, 4 * HEADS) + moved(x, 5 * HEADS))
    overall = functools.reduce(jnp.maximum, tops)
    factors = [jnp.exp(top - overall) for top in tops]
    total = functools.reduce(jnp.add, [f * t for f, t in zip(factors, totals)])
    real = (iota(total.shape, 1) < HEADS) & (iota(total.shape, 0) < requests * steps)
    inverse = jnp.where(real, 1.0 / jnp.where(real, total, 1.0), 0.0)
    ratio = jnp.concatenate([jnp.where(real, f, 0.0) * inverse for f in factors], axis=0)
    expand = jnp.where(
        (iota((LANES, width), 0) % HEADS == iota((LANES, width), 1) // head)
        & (iota((LANES, width), 0) < 3 * HEADS),
        1.0,
        0.0,
    ).astype(jnp.bfloat16)
    hi, mid, low = three_parts(ratio)
    packed = hi + pltpu.roll(mid, HEADS, 1) + pltpu.roll(low, 2 * HEADS, 1)
    wide = jnp.dot(packed.astype(jnp.bfloat16), expand, preferred_element_type=jnp.float32)
    context = jnp.zeros((ROWS, width), jnp.float32)
    for b, ref in enumerate(parts):
        context = context + wide[b * ROWS : (b + 1) * ROWS] * rows_of(ref, slice(0, width))
    attention = jnp.dot(
        context.astype(jnp.bfloat16), weight_ref[...], preferred_element_type=jnp.float32
    )
    residual = rows_of(hidden_ref, slice(0, width)) + attention
    normed = (
        residual
        * lax.rsqrt(jnp.mean(residual * residual, axis=1, keepdims=True) + norm_epsilon)
        * gain_ref[...]
    )
    row = iota((ROWS, columns), 0)
    lane = iota((ROWS, columns), 1) - tp * ROWS
    extra = jnp.where((lane >= 0) & (lane < ROWS), -1.0, 0.0)
    for i in range(requests * steps):
        first, second = [
            ids_ref[i // steps, k, i % steps].astype(jnp.float32) for k in range(2)
        ]
        extra = jnp.where(lane == i, jnp.where(row == requests * steps, first, second), extra)
    tail = row >= requests * steps
    message = jnp.concatenate(
        [jnp.where(tail, extra, normed[:, :columns]), normed[:, columns:]], axis=1
    ).astype(jnp.bfloat16)
    send_ref[...] = message
    attn_buf[...] = attention
    res_buf[...] = residual
    lanes = pl.ds(pl.multiple_of(seq * feature, feature), feature)
    mine = attn_buf[:, lanes]
    for r in range(requests):
        attn_ref[r] = mine[r * steps : (r + 1) * steps].astype(jnp.bfloat16)
    rest = res_buf[:, lanes]
    for r in range(requests):
        own_ref[r] = rest[r * steps : (r + 1) * steps]


def feed(count, capacity, steps, used, slices, router_ref, gate_ref, up_ref, down_ref, *refs):
    half = count // 2
    near, far = refs[:half], refs[half:count]
    out_ref, tokens = refs[count:]
    width = gate_ref.shape[1]
    experts = router_ref.shape[0]
    seq_size, _, requests, _, feature = out_ref.shape
    seq = lax.axis_index("seq")
    tp = lax.axis_index("tp")
    columns = count * ROWS
    core = tp % 2
    for d in range(half):
        chip = (tp // 2) ^ d
        for ref, which in ((near[d], core), (far[d], 1 - core)):
            start = pl.multiple_of((2 * chip + which) * ROWS, ROWS)
            tokens[pl.ds(start, ROWS), :] = ref[...]
    ids = jnp.zeros((8, columns), jnp.float32)
    for p in range(count):
        ids = ids + tokens[p * ROWS : (p + 1) * ROWS, :columns].astype(jnp.float32)[8:]
    place = used - 8
    first = ids[place : place + 1]
    second = ids[place + 1 : place + 2]
    mine = (seq * count + tp) // slices
    mine_f = mine.astype(jnp.float32)
    hit = jnp.where((first == mine_f) | (second == mine_f), 1.0, 0.0)
    other = jnp.where(first == mine_f, second, first)
    earlier = (iota((columns, columns), 0) < iota((columns, columns), 1)) & (
        iota((columns, columns), 0) % steps == iota((columns, columns), 1) % steps
    )
    slot = jnp.dot(
        jnp.broadcast_to(hit, (ROWS, columns)).astype(jnp.bfloat16),
        jnp.where(earlier, 1.0, 0.0).astype(jnp.bfloat16),
        preferred_element_type=jnp.float32,
    )[:1]
    rows = -(-steps * capacity // ROWS) * ROWS
    row = iota((rows, columns), 0)
    choose = (
        (hit > 0.5)
        & (slot == (row % capacity).astype(jnp.float32))
        & (iota((rows, columns), 1) % steps == row // capacity)
    )
    select = jnp.where(choose, 1.0, 0.0)
    rival = jnp.sum(select * other, axis=1, keepdims=True)
    select = select.astype(jnp.bfloat16)
    buffer = jnp.dot(select, tokens[...], preferred_element_type=jnp.float32).astype(jnp.bfloat16)
    logits = lax.dot_general(buffer, router_ref[...], NT, preferred_element_type=jnp.float32)
    index = iota((rows, experts), 1)
    ahead = jnp.sum(jnp.where(index == mine, logits, 0.0), axis=1, keepdims=True)
    behind = jnp.sum(
        jnp.where(index.astype(jnp.float32) == rival, logits, 0.0), axis=1, keepdims=True
    )
    share = 1.0 / (1.0 + jnp.exp(behind - ahead))
    gate = lax.dot_general(buffer, gate_ref[...], NT, preferred_element_type=jnp.float32)
    upward = lax.dot_general(buffer, up_ref[...], NT, preferred_element_type=jnp.float32)
    inner = (jax.nn.gelu(gate) * upward).astype(jnp.bfloat16)
    produced = jnp.dot(inner, down_ref[...], preferred_element_type=jnp.float32)
    shared = (produced * share).astype(jnp.bfloat16)
    term = lax.dot_general(select, shared, TN, preferred_element_type=jnp.float32)
    for s in range(seq_size):
        for p in range(count):
            for r in range(requests):
                start = p * ROWS + r * steps
                out_ref[s, p, r] = term[
                    start : start + steps, s * feature : (s + 1) * feature
                ].astype(jnp.bfloat16)


def limit(mebibytes):
    return pltpu.CompilerParams(vmem_limit_bytes=mebibytes * 1024 * 1024)


def stage(count, *refs):
    sources, copies, sems = refs[1 : 1 + count], refs[1 + count : 1 + 2 * count], refs[-1]
    for i, (source, copy) in enumerate(zip(sources, copies)):
        pieces = PIECES if source.shape[0] % (16 * PIECES) == 0 else 1
        size = source.shape[0] // pieces
        for piece in range(pieces):
            part = pl.ds(piece * size, size)
            pltpu.make_async_copy(source.at[part], copy.at[part], sems.at[i]).start()
    for i, (source, copy) in enumerate(zip(sources, copies)):
        pltpu.make_async_copy(source, copy, sems.at[i]).wait()


def staged(after, *arrays):
    anywhere = pl.BlockSpec(memory_space=pl.ANY)
    count = len(arrays)
    size = sum(2 * x.size for x in arrays)
    return pl.pallas_call(
        functools.partial(stage, count),
        out_shape=tuple(pltpu.VMEM(x.shape, x.dtype) for x in arrays),
        in_specs=[anywhere] * (1 + count),
        out_specs=(anywhere,) * count,
        scratch_shapes=[pltpu.SemaphoreType.DMA((count,))],
        compiler_params=limit(4),
        cost_estimate=pl.CostEstimate(flops=0, bytes_accessed=2 * size, transcendentals=0),
        name="stage",
    )(after, *[pltpu.with_memory_space_constraint(x, pltpu.HBM) for x in arrays])


def body(
    hidden_in,
    new_query,
    new_key,
    new_value,
    key_cache,
    value_cache,
    lengths,
    out_weight,
    norm_gain,
    router_weight,
    expert_ids,
    gate_weight,
    up_weight,
    down_weight,
):
    requests, steps, width = hidden_in.shape
    block = key_cache.shape[1]
    seq_size = lax.axis_size("seq")
    tp_size = lax.axis_size("tp")
    feature = width // seq_size
    experts = router_weight.shape[1]
    topk = expert_ids.shape[2]
    capacity = (5 * requests * tp_size * topk + 4 * experts - 1) // (4 * experts)
    slices = seq_size * tp_size // experts
    vmem = pl.BlockSpec(memory_space=pltpu.VMEM)
    smem = pl.BlockSpec(memory_space=pltpu.SMEM)
    hbm = pl.BlockSpec(memory_space=pltpu.HBM)

    small = pltpu.VMEM((requests, steps, width), jnp.bfloat16)
    part = pl.pallas_call(
        attend,
        out_shape=pltpu.VMEM((requests, steps, width + LANES), jnp.bfloat16),
        in_specs=[hbm] * 6,
        out_specs=vmem,
        scratch_shapes=[
            pltpu.SMEM((requests,), jnp.int32),
            small,
            small,
            small,
            pltpu.VMEM((requests, block, width), jnp.bfloat16),
            pltpu.VMEM((requests, block, width), jnp.bfloat16),
            pltpu.VMEM((requests, SHORT, width), jnp.bfloat16),
            pltpu.VMEM((requests, SHORT, width), jnp.bfloat16),
            pltpu.SemaphoreType.DMA((2, requests, PIECES)),
            pltpu.SemaphoreType.DMA((2, requests)),
            pltpu.SemaphoreType.DMA((4,)),
        ],
        compiler_params=limit(24),
        name="attend",
    )(
        *[
            pltpu.with_memory_space_constraint(x, pltpu.HBM)
            for x in (lengths, new_query, new_key, new_value, key_cache, value_cache)
        ]
    )

    def swapped(x, axis, size, d):
        return lax.ppermute(x, axis, [(i, i ^ d) for i in range(size)])

    out_weight, gate_weight = staged(part, out_weight, gate_weight)
    parts = [part] + [swapped(part, "seq", seq_size, d) for d in range(1, seq_size)]
    attn_out, own_residual, packed = pl.pallas_call(
        functools.partial(project, seq_size, tp_size * ROWS),
        out_shape=(
            pltpu.VMEM((requests, steps, feature), jnp.bfloat16),
            jax.ShapeDtypeStruct((requests, steps, feature), jnp.float32),
            jax.ShapeDtypeStruct((ROWS, width), jnp.bfloat16),
        ),
        in_specs=[smem] + [vmem] * (3 + seq_size),
        out_specs=(vmem, vmem, vmem),
        scratch_shapes=[
            pltpu.VMEM((ROWS, width), jnp.float32),
            pltpu.VMEM((ROWS, width), jnp.float32),
        ],
        compiler_params=limit(8),
        name="project",
    )(expert_ids.transpose(0, 2, 1), hidden_in, norm_gain.reshape(1, width), out_weight, *parts)
    up_weight, down_weight = staged(packed, up_weight, down_weight)
    near = [swapped(packed, "tp", tp_size, 2 * d) for d in range(1, tp_size // 2)]
    near[-1], up_weight, down_weight, first = lax.optimization_barrier(
        (near[-1], up_weight, down_weight, packed)
    )
    far = [swapped(x, "tp", tp_size, 1) for x in [first] + near]
    tokens = [packed] + near + far
    terms = pl.pallas_call(
        functools.partial(feed, tp_size, capacity, steps, requests * steps, slices),
        out_shape=pltpu.VMEM((seq_size, tp_size, requests, steps, feature), jnp.bfloat16),
        in_specs=[vmem] * (4 + tp_size),
        out_specs=vmem,
        scratch_shapes=[pltpu.VMEM((tp_size * ROWS, width), jnp.bfloat16)],
        compiler_params=limit(16),
        name="feed",
    )(router_weight.T, gate_weight, up_weight, down_weight, *tokens)
    terms = terms.reshape(seq_size * tp_size, requests, steps, feature)
    arrived = lax.all_to_all(terms, ("seq", "tp"), 0, 0, tiled=True)
    mixture = jnp.sum(arrived.astype(jnp.float32), axis=0)
    return (attn_out, (own_residual + mixture).astype(jnp.bfloat16))


def solution(mesh):
    return jax.shard_map(
        body,
        mesh=mesh,
        in_specs=(
            P("tp", None, None),
            P("tp", None, None),
            P("tp", None, None),
            P("tp", None, None),
            P("tp", "seq", None),
            P("tp", "seq", None),
            P("tp"),
            P(),
            P(),
            P(),
            P("tp", None, None),
            P(("seq", "tp"), None),
            P(("seq", "tp"), None),
            P(("seq", "tp"), None),
        ),
        out_specs=(P("tp", None, "seq"), P("tp", None, "seq")),
        check_vma=False,
    )
```

```python
import functools

import jax
import jax.numpy as jnp
from jax import lax
from jax.experimental import pallas as pl
from jax.experimental.pallas import tpu as pltpu
from jax.sharding import PartitionSpec as P

HEADS = 16
SHORT = 128
ROWS = 16
LANES = 128
masked_score = -1e30
norm_epsilon = 1e-06
NT = (((1,), (1,)), ((), ()))
TN = (((0,), (0,)), ((), ()))


def iota(shape, dim):
    return lax.broadcasted_iota(jnp.int32, shape, dim)


def over(x, n):
    if n & (n - 1) == 0:
        return lax.shift_right_logical(x, jnp.int32(n.bit_length() - 1))
    return x // n


def within(x, n):
    if n & (n - 1) == 0:
        return x & (n - 1)
    return x % n


def three_parts(x):
    hi = x.astype(jnp.bfloat16).astype(jnp.float32)
    mid = (x - hi).astype(jnp.bfloat16).astype(jnp.float32)
    return hi, mid, x - hi - mid


def tiled(x, times):
    return jnp.concatenate([x] * times, axis=0)


def attend(
    lens_hbm, q_hbm, nk_hbm, nv_hbm, k_hbm, v_hbm, out_ref,
    lens, q_ref, nk_ref, nv_ref, kbuf, vbuf, kshort, vshort, sems, short_sems, small_sems,
):
    requests, block, width = k_hbm.shape
    steps = q_ref.shape[1]
    head = width // HEADS
    scale = head ** (-0.5)
    group = 256 // head
    chunks = width // 256
    rows = group * steps
    seq = lax.axis_index("seq")
    small = [
        pltpu.make_async_copy(src, dst, small_sems.at[i])
        for i, (src, dst) in enumerate(
            ((lens_hbm, lens), (q_hbm, q_ref), (nk_hbm, nk_ref), (nv_hbm, nv_ref))
        )
    ]
    for move in small:
        move.start()
    small[0].wait()
    left = [lens[r] - seq * block for r in range(requests)]
    full = [left[r] >= block for r in range(requests)]
    short = [(left[r] > 0) & (left[r] < block) for r in range(requests)]
    some_short = functools.reduce(jnp.logical_or, short)

    def short_move(which, r):
        src, dst = ((k_hbm, kshort), (v_hbm, vshort))[which]
        return pltpu.make_async_copy(
            src.at[r, pl.ds(0, SHORT)], dst.at[r, pl.ds(0, SHORT)], short_sems.at[which, r]
        )

    def move(which, r):
        src, dst = ((k_hbm, kbuf), (v_hbm, vbuf))[which]
        return pltpu.make_async_copy(src.at[r], dst.at[r], sems.at[which, r])

    @pl.when(some_short)
    def _():
        for which in range(2):
            for r in range(requests):
                short_move(which, r).start()

    for r in range(requests):

        @pl.when(full[r])
        def _():
            for which in range(2):
                move(which, r).start()

    for move_small in small[1:]:
        move_small.wait()
    diag = over(iota((rows, 256), 0), steps) == over(iota((rows, 256), 1), head)
    diag_all = jnp.concatenate([diag] * chunks, axis=1)
    all_rows = chunks * rows

    def columns(c):
        return slice(c * 256, (c + 1) * 256)

    def against(query, keys):
        return jnp.concatenate(
            [
                lax.dot_general(
                    query[:, columns(c)], keys(c), NT, preferred_element_type=jnp.float32
                )
                for c in range(chunks)
            ],
            axis=0,
        )

    def prepare(r):
        tiled_q = tiled(q_ref[r].astype(jnp.float32), group)
        query = jnp.where(diag_all, tiled_q, 0.0).astype(jnp.bfloat16)
        fresh_k = tiled(nk_ref[r].astype(jnp.float32), group).astype(jnp.bfloat16)
        fresh_v = tiled(nv_ref[r].astype(jnp.float32), group).astype(jnp.bfloat16)
        return query, fresh_k, fresh_v

    def causal(shape, start):
        column = iota(shape, 1) - start
        return (column >= 0) & (column <= within(iota(shape, 0), steps)) & (seq == 0)

    def summary(top, total):
        shape = (all_rows, LANES)
        part = over(iota(shape, 1), HEADS)
        spread = jnp.zeros(shape, jnp.float32)
        for place, value in enumerate(three_parts(top) + three_parts(total)):
            spread = jnp.where(part == place, value, spread)
        spread = jnp.where(
            within(iota(shape, 1), HEADS) == over(iota(shape, 0), steps), spread, 0.0
        )
        pick = within(iota((ROWS, all_rows), 1), steps) == iota((ROWS, all_rows), 0)
        gathered = jnp.dot(
            jnp.where(pick, 1.0, 0.0).astype(jnp.bfloat16),
            spread.astype(jnp.bfloat16),
            preferred_element_type=jnp.float32,
        )
        return gathered[:steps].astype(jnp.bfloat16)

    def own_head(mixed):
        mixed = jnp.where(diag, mixed, 0.0)
        half = mixed[: 2 * steps]
        for g in range(1, group // 2):
            half = half + mixed[2 * steps * g : 2 * steps * (g + 1)]
        return (half[:steps] + half[steps:]).astype(jnp.bfloat16)

    def largest(x):
        return jnp.max(x, axis=1, keepdims=True)

    def summed(x):
        return jnp.sum(x, axis=1, keepdims=True)

    for r in range(requests):

        @pl.when(left[r] <= 0)
        def _():
            shape = (steps, LANES)
            hi, mid, low = three_parts(jnp.full(shape, masked_score, jnp.float32))
            part = over(iota(shape, 1), HEADS)
            empty = jnp.where(part == 0, hi, jnp.where(part == 1, mid, low))
            out_ref[r, :, width:] = jnp.where(part < 3, empty, 0.0).astype(jnp.bfloat16)
            out_ref[r, :, :width] = jnp.zeros((steps, width), jnp.bfloat16)

    @pl.when(some_short)
    def _():
        results = []
        prepared = [prepare(r) for r in range(requests)]
        for r in range(requests):
            kshort[r, SHORT:, :] = prepared[r][1]
            vshort[r, SHORT:, :] = prepared[r][2]
        for which in range(2):
            for r in range(requests):
                short_move(which, r).wait()
        for r in range(requests):
            score = against(prepared[r][0], lambda c: kshort[r, :, columns(c)]) * scale
            usable = (iota(score.shape, 1) < left[r]) | causal(score.shape, SHORT)
            score = jnp.where(usable, score, masked_score)
            top = largest(score)
            weight = jnp.where(usable, jnp.exp(score - top), 0.0)
            total = summed(weight)
            weight = weight.astype(jnp.bfloat16)
            mixed = [
                own_head(
                    jnp.dot(
                        weight[c * rows : (c + 1) * rows],
                        vshort[r, :, columns(c)],
                        preferred_element_type=jnp.float32,
                    )
                )
                for c in range(chunks)
            ]
            results.append((summary(top, total), mixed))
        for r in range(requests):

            @pl.when(short[r])
            def _():
                out_ref[r, :, width:] = results[r][0]
                for c in range(chunks):
                    out_ref[r, :, columns(c)] = results[r][1][c]

    for r in range(requests):

        @pl.when(full[r])
        def _():
            query, fresh_k, fresh_v = prepare(r)
            fresh = against(query, lambda c: fresh_k[:, columns(c)]) * scale
            allowed = causal(fresh.shape, 0)
            fresh = jnp.where(allowed, fresh, masked_score)
            fresh_top = largest(fresh)
            move(0, r).wait()
            score = against(query, lambda c: kbuf[r, :, columns(c)]) * scale
            top = jnp.maximum(largest(score), fresh_top)
            weight = jnp.exp(score - top)
            fresh_weight = jnp.where(allowed, jnp.exp(fresh - top), 0.0)
            total = summed(weight) + summed(fresh_weight)
            weight = weight.astype(jnp.bfloat16)
            fresh_weight = fresh_weight.astype(jnp.bfloat16)
            out_ref[r, :, width:] = summary(top, total)
            extra = jnp.dot(fresh_weight, fresh_v, preferred_element_type=jnp.float32)
            move(1, r).wait()
            for c in range(chunks):
                part = slice(c * rows, (c + 1) * rows)
                mixed = jnp.dot(
                    weight[part], vbuf[r, :, columns(c)], preferred_element_type=jnp.float32
                )
                out_ref[r, :, columns(c)] = own_head(mixed + extra[part, columns(c)])


def project(count, columns, ids_ref, hidden_ref, gain_ref, weight_ref, *refs):
    parts = refs[:count]
    attn_ref, own_ref, send_ref, attn_buf, res_buf = refs[count:]
    requests, steps, width = hidden_ref.shape
    feature = attn_ref.shape[2]
    head = width // HEADS
    seq = lax.axis_index("seq")
    tp = lax.axis_index("tp")

    def moved(x, amount):
        return pltpu.roll(x, LANES - amount, 1)

    def rows_of(ref, lanes):
        pieces = [ref[r, :, lanes].astype(jnp.float32) for r in range(requests)]
        blank = jnp.zeros((ROWS - requests * steps, pieces[0].shape[1]), jnp.float32)
        return jnp.concatenate(pieces + [blank], axis=0)

    tops, totals = [], []
    for ref in parts:
        x = rows_of(ref, slice(width, width + LANES))
        tops.append(x + moved(x, HEADS) + moved(x, 2 * HEADS))
        totals.append(moved(x, 3 * HEADS) + moved(x, 4 * HEADS) + moved(x, 5 * HEADS))
    overall = functools.reduce(jnp.maximum, tops)
    factors = [jnp.exp(top - overall) for top in tops]
    total = functools.reduce(jnp.add, [f * t for f, t in zip(factors, totals)])
    real = (iota(total.shape, 1) < HEADS) & (iota(total.shape, 0) < requests * steps)
    inverse = jnp.where(real, 1.0 / jnp.where(real, total, 1.0), 0.0)
    ratio = jnp.concatenate([jnp.where(real, f, 0.0) * inverse for f in factors], axis=0)
    expand = jnp.where(
        (within(iota((LANES, width), 0), HEADS) == over(iota((LANES, width), 1), head))
        & (iota((LANES, width), 0) < 3 * HEADS),
        1.0,
        0.0,
    ).astype(jnp.bfloat16)
    hi, mid, low = three_parts(ratio)
    packed = hi + pltpu.roll(mid, HEADS, 1) + pltpu.roll(low, 2 * HEADS, 1)
    wide = jnp.dot(packed.astype(jnp.bfloat16), expand, preferred_element_type=jnp.float32)
    context = jnp.zeros((ROWS, width), jnp.float32)
    for b, ref in enumerate(parts):
        context = context + wide[b * ROWS : (b + 1) * ROWS] * rows_of(ref, slice(0, width))
    attention = jnp.dot(
        context.astype(jnp.bfloat16), weight_ref[...], preferred_element_type=jnp.float32
    )
    residual = rows_of(hidden_ref, slice(0, width)) + attention
    normed = (
        residual
        * lax.rsqrt(jnp.mean(residual * residual, axis=1, keepdims=True) + norm_epsilon)
        * gain_ref[...]
    )
    row = iota((ROWS, columns), 0)
    lane = iota((ROWS, columns), 1) - tp * ROWS
    extra = jnp.where((lane >= 0) & (lane < ROWS), -1.0, 0.0)
    for i in range(requests * steps):
        first, second = [
            ids_ref[i // steps, k, i % steps].astype(jnp.float32) for k in range(2)
        ]
        extra = jnp.where(lane == i, jnp.where(row == requests * steps, first, second), extra)
    tail = row >= requests * steps
    message = jnp.concatenate(
        [jnp.where(tail, extra, normed[:, :columns]), normed[:, columns:]], axis=1
    ).astype(jnp.bfloat16)
    send_ref[...] = message
    attn_buf[...] = attention
    res_buf[...] = residual
    lanes = pl.ds(pl.multiple_of(seq * feature, feature), feature)
    mine = attn_buf[:, lanes]
    for r in range(requests):
        attn_ref[r] = mine[r * steps : (r + 1) * steps].astype(jnp.bfloat16)
    rest = res_buf[:, lanes]
    for r in range(requests):
        own_ref[r] = rest[r * steps : (r + 1) * steps]


def feed(
    capacity, steps, used, slices, router_ref, gate_ref, up_ref, down_ref, near_ref, far_ref,
    out_ref, tokens,
):
    half = near_ref.shape[0]
    count = 2 * half
    width = gate_ref.shape[1]
    experts = router_ref.shape[0]
    seq_size, _, requests, _, feature = out_ref.shape
    seq = lax.axis_index("seq")
    tp = lax.axis_index("tp")
    columns = count * ROWS
    core = within(tp, 2)
    for d in range(half):
        chip = over(tp, 2) ^ d
        for ref, which in ((near_ref, core), (far_ref, 1 - core)):
            start = pl.multiple_of((2 * chip + which) * ROWS, ROWS)
            tokens[pl.ds(start, ROWS), :] = ref[d]
    ids = jnp.zeros((8, columns), jnp.float32)
    for p in range(count):
        ids = ids + tokens[p * ROWS : (p + 1) * ROWS, :columns].astype(jnp.float32)[8:]
    place = used - 8
    first = ids[place : place + 1]
    second = ids[place + 1 : place + 2]
    mine = over(seq * count + tp, slices)
    mine_f = mine.astype(jnp.float32)
    hit = jnp.where((first == mine_f) | (second == mine_f), 1.0, 0.0)
    other = jnp.where(first == mine_f, second, first)
    earlier = (iota((columns, columns), 0) < iota((columns, columns), 1)) & (
        within(iota((columns, columns), 0), steps) == within(iota((columns, columns), 1), steps)
    )
    slot = jnp.dot(
        jnp.broadcast_to(hit, (ROWS, columns)).astype(jnp.bfloat16),
        jnp.where(earlier, 1.0, 0.0).astype(jnp.bfloat16),
        preferred_element_type=jnp.float32,
    )[:1]
    rows = -(-steps * capacity // ROWS) * ROWS
    row = iota((rows, columns), 0)
    choose = (
        (hit > 0.5)
        & (slot == within(row, capacity).astype(jnp.float32))
        & (within(iota((rows, columns), 1), steps) == over(row, capacity))
    )
    select = jnp.where(choose, 1.0, 0.0)
    rival = jnp.sum(select * other, axis=1, keepdims=True)
    select = select.astype(jnp.bfloat16)
    buffer = jnp.dot(select, tokens[...], preferred_element_type=jnp.float32).astype(jnp.bfloat16)
    logits = lax.dot_general(buffer, router_ref[...], NT, preferred_element_type=jnp.float32)
    index = iota((rows, experts), 1)
    ahead = jnp.sum(jnp.where(index == mine, logits, 0.0), axis=1, keepdims=True)
    behind = jnp.sum(
        jnp.where(index.astype(jnp.float32) == rival, logits, 0.0), axis=1, keepdims=True
    )
    share = 1.0 / (1.0 + jnp.exp(behind - ahead))
    gate = lax.dot_general(buffer, gate_ref[...], NT, preferred_element_type=jnp.float32)
    upward = lax.dot_general(buffer, up_ref[...], NT, preferred_element_type=jnp.float32)
    inner = (jax.nn.gelu(gate) * upward).astype(jnp.bfloat16)
    produced = jnp.dot(inner, down_ref[...], preferred_element_type=jnp.float32)
    shared = (produced * share).astype(jnp.bfloat16)
    term = lax.dot_general(select, shared, TN, preferred_element_type=jnp.float32)
    for s in range(seq_size):
        for p in range(count):
            for r in range(requests):
                start = p * ROWS + r * steps
                out_ref[s, p, r] = term[
                    start : start + steps, s * feature : (s + 1) * feature
                ].astype(jnp.bfloat16)


def limit(mebibytes):
    return pltpu.CompilerParams(vmem_limit_bytes=mebibytes * 1024 * 1024)


def stage(count, *refs):
    sources, copies, sems = refs[1 : 1 + count], refs[1 + count : 1 + 2 * count], refs[-1]
    moves = [
        pltpu.make_async_copy(source, copy, sems.at[i])
        for i, (source, copy) in enumerate(zip(sources, copies))
    ]
    for move in moves:
        move.start()
    for move in moves:
        move.wait()


def staged(after, *arrays, result=None):
    anywhere = pl.BlockSpec(memory_space=pl.ANY)
    inputs = [pltpu.with_memory_space_constraint(x, pltpu.HBM) for x in arrays]
    shapes = [pltpu.VMEM(x.shape, x.dtype) for x in arrays]
    if result is not None:
        inputs.append(result)
        shapes.append(pltpu.HBM(result.shape, result.dtype))
    count = len(inputs)
    size = sum(2 * x.size for x in arrays)
    return pl.pallas_call(
        functools.partial(stage, count),
        out_shape=tuple(shapes),
        in_specs=[anywhere] * (1 + count),
        out_specs=(anywhere,) * count,
        scratch_shapes=[pltpu.SemaphoreType.DMA((count,))],
        compiler_params=limit(4),
        cost_estimate=pl.CostEstimate(flops=0, bytes_accessed=2 * size, transcendentals=0),
        name="stage",
    )(after, *inputs)


def body(
    hidden_in,
    new_query,
    new_key,
    new_value,
    key_cache,
    value_cache,
    lengths,
    out_weight,
    norm_gain,
    router_weight,
    expert_ids,
    gate_weight,
    up_weight,
    down_weight,
):
    requests, steps, width = hidden_in.shape
    block = key_cache.shape[1]
    seq_size = lax.axis_size("seq")
    tp_size = lax.axis_size("tp")
    feature = width // seq_size
    experts = router_weight.shape[1]
    topk = expert_ids.shape[2]
    capacity = (5 * requests * tp_size * topk + 4 * experts - 1) // (4 * experts)
    slices = seq_size * tp_size // experts
    vmem = pl.BlockSpec(memory_space=pltpu.VMEM)
    smem = pl.BlockSpec(memory_space=pltpu.SMEM)
    hbm = pl.BlockSpec(memory_space=pltpu.HBM)

    small = pltpu.VMEM((requests, steps, width), jnp.bfloat16)
    part = pl.pallas_call(
        attend,
        out_shape=pltpu.VMEM((requests, steps, width + LANES), jnp.bfloat16),
        in_specs=[hbm] * 6,
        out_specs=vmem,
        scratch_shapes=[
            pltpu.SMEM((requests,), jnp.int32),
            small,
            small,
            small,
            pltpu.VMEM((requests, block, width), jnp.bfloat16),
            pltpu.VMEM((requests, block, width), jnp.bfloat16),
            pltpu.VMEM((requests, SHORT + ROWS, width), jnp.bfloat16),
            pltpu.VMEM((requests, SHORT + ROWS, width), jnp.bfloat16),
            pltpu.SemaphoreType.DMA((2, requests)),
            pltpu.SemaphoreType.DMA((2, requests)),
            pltpu.SemaphoreType.DMA((4,)),
        ],
        compiler_params=limit(24),
        name="attend",
    )(
        *[
            pltpu.with_memory_space_constraint(x, pltpu.HBM)
            for x in (lengths, new_query, new_key, new_value, key_cache, value_cache)
        ]
    )

    def swapped(x, axis, size, d):
        return lax.ppermute(x, axis, [(i, i ^ d) for i in range(size)])

    out_weight, gate_weight = staged(part, out_weight, gate_weight)
    parts = [part] + [swapped(part, "seq", seq_size, d) for d in range(1, seq_size)]
    attn_out, own_residual, packed = pl.pallas_call(
        functools.partial(project, seq_size, tp_size * ROWS),
        out_shape=(
            pltpu.VMEM((requests, steps, feature), jnp.bfloat16),
            jax.ShapeDtypeStruct((requests, steps, feature), jnp.float32),
            jax.ShapeDtypeStruct((ROWS, width), jnp.bfloat16),
        ),
        in_specs=[smem] + [vmem] * (3 + seq_size),
        out_specs=(vmem, vmem, vmem),
        scratch_shapes=[
            pltpu.VMEM((ROWS, width), jnp.float32),
            pltpu.VMEM((ROWS, width), jnp.float32),
        ],
        compiler_params=limit(8),
        name="project",
    )(expert_ids.transpose(0, 2, 1), hidden_in, norm_gain.reshape(1, width), out_weight, *parts)
    up_weight, down_weight, attn_out = staged(packed, up_weight, down_weight, result=attn_out)
    near = jnp.stack(
        [packed] + [swapped(packed, "tp", tp_size, 2 * d) for d in range(1, tp_size // 2)]
    )
    near, up_weight, down_weight = lax.optimization_barrier((near, up_weight, down_weight))
    far = swapped(near, "tp", tp_size, 1)
    terms = pl.pallas_call(
        functools.partial(feed, capacity, steps, requests * steps, slices),
        out_shape=pltpu.VMEM((seq_size, tp_size, requests, steps, feature), jnp.bfloat16),
        in_specs=[vmem] * 6,
        out_specs=vmem,
        scratch_shapes=[pltpu.VMEM((tp_size * ROWS, width), jnp.bfloat16)],
        compiler_params=limit(16),
        name="feed",
    )(router_weight.T, gate_weight, up_weight, down_weight, near, far)
    terms = terms.reshape(seq_size * tp_size, requests, steps, feature)
    arrived = lax.all_to_all(terms, ("seq", "tp"), 0, 0, tiled=True)
    mixture = jnp.sum(arrived.astype(jnp.float32), axis=0)
    return (attn_out, (own_residual + mixture).astype(jnp.bfloat16))


def solution(mesh):
    return jax.shard_map(
        body,
        mesh=mesh,
        in_specs=(
            P("tp", None, None),
            P("tp", None, None),
            P("tp", None, None),
            P("tp", None, None),
            P("tp", "seq", None),
            P("tp", "seq", None),
            P("tp"),
            P(),
            P(),
            P(),
            P("tp", None, None),
            P(("seq", "tp"), None),
            P(("seq", "tp"), None),
            P(("seq", "tp"), None),
        ),
        out_specs=(P("tp", None, "seq"), P("tp", None, "seq")),
        check_vma=False,
    )
```

```python
import functools

import jax
import jax.numpy as jnp
from jax import lax
from jax.experimental import pallas as pl
from jax.experimental.pallas import tpu as pltpu
from jax.sharding import PartitionSpec as P

HEADS = 16
SHORT = 128
ROWS = 16
LANES = 128
masked_score = -1e30
norm_epsilon = 1e-06
NT = (((1,), (1,)), ((), ()))
TN = (((0,), (0,)), ((), ()))


def iota(shape, dim):
    return lax.broadcasted_iota(jnp.int32, shape, dim)


def over(x, n):
    if n & (n - 1) == 0:
        return lax.shift_right_logical(x, jnp.int32(n.bit_length() - 1))
    return x // n


def within(x, n):
    if n & (n - 1) == 0:
        return x & (n - 1)
    return x % n


def three_parts(x):
    hi = x.astype(jnp.bfloat16).astype(jnp.float32)
    mid = (x - hi).astype(jnp.bfloat16).astype(jnp.float32)
    return hi, mid, x - hi - mid


def tiled(x, times):
    return jnp.concatenate([x] * times, axis=0)


def attend(
    lens_hbm, q_hbm, nk_hbm, nv_hbm, k_hbm, v_hbm, out_ref,
    lens, q_ref, nk_ref, nv_ref, kbuf, vbuf, kshort, vshort, sems, short_sems, small_sems,
):
    requests, block, width = k_hbm.shape
    steps = q_ref.shape[1]
    head = width // HEADS
    scale = head ** (-0.5)
    group = 256 // head
    chunks = width // 256
    rows = group * steps
    seq = lax.axis_index("seq")
    small = [
        pltpu.make_async_copy(src, dst, small_sems.at[i])
        for i, (src, dst) in enumerate(
            ((lens_hbm, lens), (q_hbm, q_ref), (nk_hbm, nk_ref), (nv_hbm, nv_ref))
        )
    ]
    for move in small:
        move.start()
    small[0].wait()

    def left(r):
        return lens[r] - seq * block

    def is_full(r):
        return left(r) >= block

    def is_short(r):
        return (left(r) > 0) & (left(r) < block)

    def short_move(which, r):
        src, dst = ((k_hbm, kshort), (v_hbm, vshort))[which]
        return pltpu.make_async_copy(
            src.at[r, pl.ds(0, SHORT)], dst.at[r, pl.ds(0, SHORT)], short_sems.at[which, r]
        )

    def move(which, r):
        src, dst = ((k_hbm, kbuf), (v_hbm, vbuf))[which]
        return pltpu.make_async_copy(src.at[r], dst.at[r], sems.at[which, r])

    for r in range(requests):

        @pl.when(is_short(r))
        def _():
            for which in range(2):
                short_move(which, r).start()

    for r in range(requests):

        @pl.when(is_full(r))
        def _():
            for which in range(2):
                move(which, r).start()

    for move_small in small[1:]:
        move_small.wait()
    diag = over(iota((rows, 256), 0), steps) == over(iota((rows, 256), 1), head)
    diag_all = jnp.concatenate([diag] * chunks, axis=1)
    all_rows = chunks * rows

    def columns(c):
        return slice(c * 256, (c + 1) * 256)

    def against(query, keys):
        return jnp.concatenate(
            [
                lax.dot_general(
                    query[:, columns(c)], keys(c), NT, preferred_element_type=jnp.float32
                )
                for c in range(chunks)
            ],
            axis=0,
        )

    def prepare(r):
        tiled_q = tiled(q_ref[r].astype(jnp.float32) * scale, group)
        query = jnp.where(diag_all, tiled_q, 0.0).astype(jnp.bfloat16)
        fresh_k = tiled(nk_ref[r].astype(jnp.float32), group).astype(jnp.bfloat16)
        fresh_v = tiled(nv_ref[r].astype(jnp.float32), group).astype(jnp.bfloat16)
        return query, fresh_k, fresh_v

    def causal(shape, start):
        column = iota(shape, 1) - start
        return (column >= 0) & (column <= within(iota(shape, 0), steps)) & (seq == 0)

    def summary(top, total):
        shape = (all_rows, LANES)
        part = over(iota(shape, 1), HEADS)
        spread = jnp.zeros(shape, jnp.float32)
        for place, value in enumerate(three_parts(top) + three_parts(total)):
            spread = jnp.where(part == place, value, spread)
        spread = jnp.where(
            within(iota(shape, 1), HEADS) == over(iota(shape, 0), steps), spread, 0.0
        )
        pick = within(iota((ROWS, all_rows), 1), steps) == iota((ROWS, all_rows), 0)
        gathered = jnp.dot(
            jnp.where(pick, 1.0, 0.0).astype(jnp.bfloat16),
            spread.astype(jnp.bfloat16),
            preferred_element_type=jnp.float32,
        )
        return gathered[:steps].astype(jnp.bfloat16)

    def own_head(mixed):
        mixed = jnp.where(diag, mixed, 0.0)
        half = mixed[: 2 * steps]
        for g in range(1, group // 2):
            half = half + mixed[2 * steps * g : 2 * steps * (g + 1)]
        return (half[:steps] + half[steps:]).astype(jnp.bfloat16)

    def largest(x):
        return jnp.max(x, axis=1, keepdims=True)

    def summed(x):
        return jnp.sum(x, axis=1, keepdims=True)

    @pl.loop(0, requests)
    def _(r):
        @pl.when(left(r) <= 0)
        def _():
            shape = (steps, LANES)
            hi, mid, low = three_parts(jnp.full(shape, masked_score, jnp.float32))
            part = over(iota(shape, 1), HEADS)
            empty = jnp.where(part == 0, hi, jnp.where(part == 1, mid, low))
            out_ref[r, :, width:] = jnp.where(part < 3, empty, 0.0).astype(jnp.bfloat16)
            out_ref[r, :, :width] = jnp.zeros((steps, width), jnp.bfloat16)

        @pl.when(is_short(r))
        def _():
            query, fresh_k, fresh_v = prepare(r)
            kshort[r, SHORT:, :] = fresh_k
            vshort[r, SHORT:, :] = fresh_v
            short_move(0, r).wait()
            score = against(query, lambda c: kshort[r, :, columns(c)])
            usable = (iota(score.shape, 1) < left(r)) | causal(score.shape, SHORT)
            score = jnp.where(usable, score, masked_score)
            top = largest(score)
            weight = jnp.where(usable, jnp.exp(score - top), 0.0)
            total = summed(weight)
            weight = weight.astype(jnp.bfloat16)
            out_ref[r, :, width:] = summary(top, total)
            short_move(1, r).wait()
            for c in range(chunks):
                mixed = jnp.dot(
                    weight[c * rows : (c + 1) * rows],
                    vshort[r, :, columns(c)],
                    preferred_element_type=jnp.float32,
                )
                out_ref[r, :, columns(c)] = own_head(mixed)

    @pl.loop(0, requests)
    def _(r):
        @pl.when(is_full(r))
        def _():
            query, fresh_k, fresh_v = prepare(r)
            fresh = against(query, lambda c: fresh_k[:, columns(c)])
            allowed = causal(fresh.shape, 0)
            fresh = jnp.where(allowed, fresh, masked_score)
            fresh_top = largest(fresh)
            move(0, r).wait()
            score = against(query, lambda c: kbuf[r, :, columns(c)])
            top = jnp.maximum(largest(score), fresh_top)
            weight = jnp.exp(score - top)
            fresh_weight = jnp.where(allowed, jnp.exp(fresh - top), 0.0)
            total = summed(weight) + summed(fresh_weight)
            weight = weight.astype(jnp.bfloat16)
            fresh_weight = fresh_weight.astype(jnp.bfloat16)
            out_ref[r, :, width:] = summary(top, total)
            move(1, r).wait()
            for c in range(chunks):
                part = slice(c * rows, (c + 1) * rows)
                mixed = jnp.dot(
                    weight[part], vbuf[r, :, columns(c)], preferred_element_type=jnp.float32
                ) + jnp.dot(
                    fresh_weight[part], fresh_v[:, columns(c)], preferred_element_type=jnp.float32
                )
                out_ref[r, :, columns(c)] = own_head(mixed)


def project(count, columns, ids_ref, hidden_ref, gain_ref, weight_ref, *refs):
    parts = refs[:count]
    attn_ref, own_ref, send_ref, attn_buf, res_buf = refs[count:]
    requests, steps, width = hidden_ref.shape
    feature = attn_ref.shape[2]
    head = width // HEADS
    seq = lax.axis_index("seq")
    tp = lax.axis_index("tp")

    def moved(x, amount):
        return pltpu.roll(x, LANES - amount, 1)

    def rows_of(ref, lanes):
        pieces = [ref[r, :, lanes].astype(jnp.float32) for r in range(requests)]
        blank = jnp.zeros((ROWS - requests * steps, pieces[0].shape[1]), jnp.float32)
        return jnp.concatenate(pieces + [blank], axis=0)

    tops, totals = [], []
    for ref in parts:
        x = rows_of(ref, slice(width, width + LANES))
        tops.append(x + moved(x, HEADS) + moved(x, 2 * HEADS))
        totals.append(moved(x, 3 * HEADS) + moved(x, 4 * HEADS) + moved(x, 5 * HEADS))
    overall = functools.reduce(jnp.maximum, tops)
    factors = [jnp.exp(top - overall) for top in tops]
    total = functools.reduce(jnp.add, [f * t for f, t in zip(factors, totals)])
    real = (iota(total.shape, 1) < HEADS) & (iota(total.shape, 0) < requests * steps)
    inverse = jnp.where(real, 1.0 / jnp.where(real, total, 1.0), 0.0)
    ratio = jnp.concatenate([jnp.where(real, f, 0.0) * inverse for f in factors], axis=0)
    expand = jnp.where(
        (within(iota((LANES, width), 0), HEADS) == over(iota((LANES, width), 1), head))
        & (iota((LANES, width), 0) < 3 * HEADS),
        1.0,
        0.0,
    ).astype(jnp.bfloat16)
    hi, mid, low = three_parts(ratio)
    packed = hi + pltpu.roll(mid, HEADS, 1) + pltpu.roll(low, 2 * HEADS, 1)
    wide = jnp.dot(packed.astype(jnp.bfloat16), expand, preferred_element_type=jnp.float32)
    context = jnp.zeros((ROWS, width), jnp.float32)
    for b, ref in enumerate(parts):
        context = context + wide[b * ROWS : (b + 1) * ROWS] * rows_of(ref, slice(0, width))
    attention = jnp.dot(
        context.astype(jnp.bfloat16), weight_ref[...], preferred_element_type=jnp.float32
    )
    residual = rows_of(hidden_ref, slice(0, width)) + attention
    normed = (
        residual
        * lax.rsqrt(jnp.mean(residual * residual, axis=1, keepdims=True) + norm_epsilon)
        * gain_ref[...]
    )
    row = iota((ROWS, columns), 0)
    lane = iota((ROWS, columns), 1) - tp * ROWS
    extra = jnp.where((lane >= 0) & (lane < ROWS), -1.0, 0.0)
    for i in range(requests * steps):
        first, second = [
            ids_ref[i // steps, k, i % steps].astype(jnp.float32) for k in range(2)
        ]
        extra = jnp.where(lane == i, jnp.where(row == requests * steps, first, second), extra)
    tail = row >= requests * steps
    message = jnp.concatenate(
        [jnp.where(tail, extra, normed[:, :columns]), normed[:, columns:]], axis=1
    ).astype(jnp.bfloat16)
    send_ref[...] = message
    attn_buf[...] = attention
    res_buf[...] = residual
    lanes = pl.ds(pl.multiple_of(seq * feature, feature), feature)
    mine = attn_buf[:, lanes]
    for r in range(requests):
        attn_ref[r] = mine[r * steps : (r + 1) * steps].astype(jnp.bfloat16)
    rest = res_buf[:, lanes]
    for r in range(requests):
        own_ref[r] = rest[r * steps : (r + 1) * steps]


def feed(
    capacity, steps, used, slices, router_ref, gate_ref, up_ref, down_ref, near_ref, far_ref,
    out_ref, tokens,
):
    half = near_ref.shape[0]
    count = 2 * half
    width = gate_ref.shape[1]
    experts = router_ref.shape[0]
    seq_size, _, requests, _, feature = out_ref.shape
    seq = lax.axis_index("seq")
    tp = lax.axis_index("tp")
    columns = count * ROWS
    core = within(tp, 2)
    for d in range(half):
        chip = over(tp, 2) ^ d
        for ref, which in ((near_ref, core), (far_ref, 1 - core)):
            start = pl.multiple_of((2 * chip + which) * ROWS, ROWS)
            tokens[pl.ds(start, ROWS), :] = ref[d]
    ids = jnp.zeros((8, columns), jnp.float32)
    for p in range(count):
        ids = ids + tokens[p * ROWS : (p + 1) * ROWS, :columns].astype(jnp.float32)[8:]
    place = used - 8
    first = ids[place : place + 1]
    second = ids[place + 1 : place + 2]
    mine = over(seq * count + tp, slices)
    mine_f = mine.astype(jnp.float32)
    hit = jnp.where((first == mine_f) | (second == mine_f), 1.0, 0.0)
    other = jnp.where(first == mine_f, second, first)
    earlier = (iota((columns, columns), 0) < iota((columns, columns), 1)) & (
        within(iota((columns, columns), 0), steps) == within(iota((columns, columns), 1), steps)
    )
    slot = jnp.dot(
        jnp.broadcast_to(hit, (ROWS, columns)).astype(jnp.bfloat16),
        jnp.where(earlier, 1.0, 0.0).astype(jnp.bfloat16),
        preferred_element_type=jnp.float32,
    )[:1]
    rows = -(-steps * capacity // ROWS) * ROWS
    row = iota((rows, columns), 0)
    choose = (
        (hit > 0.5)
        & (slot == within(row, capacity).astype(jnp.float32))
        & (within(iota((rows, columns), 1), steps) == over(row, capacity))
    )
    select = jnp.where(choose, 1.0, 0.0)
    rival = jnp.sum(select * other, axis=1, keepdims=True)
    select = select.astype(jnp.bfloat16)
    buffer = jnp.dot(select, tokens[...], preferred_element_type=jnp.float32).astype(jnp.bfloat16)
    logits = lax.dot_general(buffer, router_ref[...], NT, preferred_element_type=jnp.float32)
    index = iota((rows, experts), 1)
    ahead = jnp.sum(jnp.where(index == mine, logits, 0.0), axis=1, keepdims=True)
    behind = jnp.sum(
        jnp.where(index.astype(jnp.float32) == rival, logits, 0.0), axis=1, keepdims=True
    )
    share = 1.0 / (1.0 + jnp.exp(behind - ahead))
    gate = lax.dot_general(buffer, gate_ref[...], NT, preferred_element_type=jnp.float32)
    upward = lax.dot_general(buffer, up_ref[...], NT, preferred_element_type=jnp.float32)
    inner = (jax.nn.gelu(gate) * upward).astype(jnp.bfloat16)
    produced = jnp.dot(inner, down_ref[...], preferred_element_type=jnp.float32)
    shared = (produced * share).astype(jnp.bfloat16)
    term = lax.dot_general(select, shared, TN, preferred_element_type=jnp.float32)
    for s in range(seq_size):
        for p in range(count):
            for r in range(requests):
                start = p * ROWS + r * steps
                out_ref[s, p, r] = term[
                    start : start + steps, s * feature : (s + 1) * feature
                ].astype(jnp.bfloat16)


def limit(mebibytes):
    return pltpu.CompilerParams(vmem_limit_bytes=mebibytes * 1024 * 1024)


def stage(count, *refs):
    sources, copies, sems = refs[1 : 1 + count], refs[1 + count : 1 + 2 * count], refs[-1]
    moves = [
        pltpu.make_async_copy(source, copy, sems.at[i])
        for i, (source, copy) in enumerate(zip(sources, copies))
    ]
    for move in moves:
        move.start()
    for move in moves:
        move.wait()


def staged(after, *arrays, result=None):
    anywhere = pl.BlockSpec(memory_space=pl.ANY)
    inputs = [pltpu.with_memory_space_constraint(x, pltpu.HBM) for x in arrays]
    shapes = [pltpu.VMEM(x.shape, x.dtype) for x in arrays]
    if result is not None:
        inputs.append(result)
        shapes.append(pltpu.HBM(result.shape, result.dtype))
    count = len(inputs)
    size = sum(2 * x.size for x in arrays)
    return pl.pallas_call(
        functools.partial(stage, count),
        out_shape=tuple(shapes),
        in_specs=[anywhere] * (1 + count),
        out_specs=(anywhere,) * count,
        scratch_shapes=[pltpu.SemaphoreType.DMA((count,))],
        compiler_params=limit(4),
        cost_estimate=pl.CostEstimate(flops=0, bytes_accessed=2 * size, transcendentals=0),
        name="stage",
    )(after, *inputs)


def body(
    hidden_in,
    new_query,
    new_key,
    new_value,
    key_cache,
    value_cache,
    lengths,
    out_weight,
    norm_gain,
    router_weight,
    expert_ids,
    gate_weight,
    up_weight,
    down_weight,
):
    requests, steps, width = hidden_in.shape
    block = key_cache.shape[1]
    seq_size = lax.axis_size("seq")
    tp_size = lax.axis_size("tp")
    feature = width // seq_size
    experts = router_weight.shape[1]
    topk = expert_ids.shape[2]
    capacity = (5 * requests * tp_size * topk + 4 * experts - 1) // (4 * experts)
    slices = seq_size * tp_size // experts
    vmem = pl.BlockSpec(memory_space=pltpu.VMEM)
    smem = pl.BlockSpec(memory_space=pltpu.SMEM)
    hbm = pl.BlockSpec(memory_space=pltpu.HBM)

    small = pltpu.VMEM((requests, steps, width), jnp.bfloat16)
    part = pl.pallas_call(
        attend,
        out_shape=pltpu.VMEM((requests, steps, width + LANES), jnp.bfloat16),
        in_specs=[hbm] * 6,
        out_specs=vmem,
        scratch_shapes=[
            pltpu.SMEM((requests,), jnp.int32),
            small,
            small,
            small,
            pltpu.VMEM((requests, block, width), jnp.bfloat16),
            pltpu.VMEM((requests, block, width), jnp.bfloat16),
            pltpu.VMEM((requests, SHORT + ROWS, width), jnp.bfloat16),
            pltpu.VMEM((requests, SHORT + ROWS, width), jnp.bfloat16),
            pltpu.SemaphoreType.DMA((2, requests)),
            pltpu.SemaphoreType.DMA((2, requests)),
            pltpu.SemaphoreType.DMA((4,)),
        ],
        compiler_params=limit(24),
        name="attend",
    )(
        *[
            pltpu.with_memory_space_constraint(x, pltpu.HBM)
            for x in (lengths, new_query, new_key, new_value, key_cache, value_cache)
        ]
    )

    def swapped(x, axis, size, d):
        return lax.ppermute(x, axis, [(i, i ^ d) for i in range(size)])

    out_weight, gate_weight = staged(part, out_weight, gate_weight)
    parts = [part] + [swapped(part, "seq", seq_size, d) for d in range(1, seq_size)]
    attn_out, own_residual, packed = pl.pallas_call(
        functools.partial(project, seq_size, tp_size * ROWS),
        out_shape=(
            pltpu.VMEM((requests, steps, feature), jnp.bfloat16),
            jax.ShapeDtypeStruct((requests, steps, feature), jnp.float32),
            jax.ShapeDtypeStruct((ROWS, width), jnp.bfloat16),
        ),
        in_specs=[smem] + [vmem] * (3 + seq_size),
        out_specs=(vmem, vmem, vmem),
        scratch_shapes=[
            pltpu.VMEM((ROWS, width), jnp.float32),
            pltpu.VMEM((ROWS, width), jnp.float32),
        ],
        compiler_params=limit(8),
        name="project",
    )(expert_ids.transpose(0, 2, 1), hidden_in, norm_gain.reshape(1, width), out_weight, *parts)
    up_weight, down_weight, attn_out = staged(packed, up_weight, down_weight, result=attn_out)
    near = jnp.stack(
        [packed] + [swapped(packed, "tp", tp_size, 2 * d) for d in range(1, tp_size // 2)]
    )
    near, up_weight, down_weight = lax.optimization_barrier((near, up_weight, down_weight))
    far = swapped(near, "tp", tp_size, 1)
    terms = pl.pallas_call(
        functools.partial(feed, capacity, steps, requests * steps, slices),
        out_shape=pltpu.VMEM((seq_size, tp_size, requests, steps, feature), jnp.bfloat16),
        in_specs=[vmem] * 6,
        out_specs=vmem,
        scratch_shapes=[pltpu.VMEM((tp_size * ROWS, width), jnp.bfloat16)],
        compiler_params=limit(16),
        name="feed",
    )(router_weight.T, gate_weight, up_weight, down_weight, near, far)
    terms = terms.reshape(seq_size * tp_size, requests, steps, feature)
    arrived = lax.all_to_all(terms, ("seq", "tp"), 0, 0, tiled=True)
    mixture = jnp.sum(arrived.astype(jnp.float32), axis=0)
    return (attn_out, (own_residual + mixture).astype(jnp.bfloat16))


def solution(mesh):
    return jax.shard_map(
        body,
        mesh=mesh,
        in_specs=(
            P("tp", None, None),
            P("tp", None, None),
            P("tp", None, None),
            P("tp", None, None),
            P("tp", "seq", None),
            P("tp", "seq", None),
            P("tp"),
            P(),
            P(),
            P(),
            P("tp", None, None),
            P(("seq", "tp"), None),
            P(("seq", "tp"), None),
            P(("seq", "tp"), None),
        ),
        out_specs=(P("tp", None, "seq"), P("tp", None, "seq")),
        check_vma=False,
    )
```

```python
import functools

import jax
import jax.numpy as jnp
from jax import lax
from jax.experimental import pallas as pl
from jax.experimental.pallas import tpu as pltpu
from jax.sharding import PartitionSpec as P

HEADS = 16
SHORT = 128
ROWS = 16
LANES = 128
masked_score = -1e30
norm_epsilon = 1e-06
NT = (((1,), (1,)), ((), ()))
TN = (((0,), (0,)), ((), ()))


def iota(shape, dim):
    return lax.broadcasted_iota(jnp.int32, shape, dim)


def over(x, n):
    if n & (n - 1) == 0:
        return lax.shift_right_logical(x, jnp.int32(n.bit_length() - 1))
    return x // n


def within(x, n):
    if n & (n - 1) == 0:
        return x & (n - 1)
    return x % n


def three_parts(x):
    hi = x.astype(jnp.bfloat16).astype(jnp.float32)
    mid = (x - hi).astype(jnp.bfloat16).astype(jnp.float32)
    return hi, mid, x - hi - mid


def tiled(x, times):
    return jnp.concatenate([x] * times, axis=0)


def attend(
    lens_hbm, q_hbm, nk_hbm, nv_hbm, k_hbm, v_hbm, out_ref, fresh_ref,
    lens, q_ref, nk_ref, nv_ref, query_ref, kbuf, vbuf, sems, small_sems,
):
    requests, block, width = k_hbm.shape
    steps = q_ref.shape[1]
    head = width // HEADS
    scale = head ** (-0.5)
    group = 256 // head
    chunks = width // 256
    rows = group * steps
    seq = lax.axis_index("seq")
    small = [
        pltpu.make_async_copy(src, dst, small_sems.at[i])
        for i, (src, dst) in enumerate(
            ((lens_hbm, lens), (q_hbm, q_ref), (nk_hbm, nk_ref), (nv_hbm, nv_ref))
        )
    ]
    for move in small:
        move.start()
    small[0].wait()

    def left(r):
        return lens[r] - seq * block

    def is_full(r):
        return left(r) >= block

    def is_short(r):
        return (left(r) > 0) & (left(r) < block)

    def move(which, r, count):
        src, dst = ((k_hbm, kbuf), (v_hbm, vbuf))[which]
        part = pl.ds(0, count)
        return pltpu.make_async_copy(src.at[r, part], dst.at[r, part], sems.at[which, r])

    for kind, count in ((is_short, SHORT), (is_full, block)):
        for r in range(requests):

            @pl.when(kind(r))
            def _():
                for which in range(2):
                    move(which, r, count).start()

    for move_small in small[1:]:
        move_small.wait()
    diag = over(iota((rows, 256), 0), steps) == over(iota((rows, 256), 1), head)
    diag_all = jnp.concatenate([diag] * chunks, axis=1)
    all_rows = chunks * rows

    def columns(c):
        return slice(c * 256, (c + 1) * 256)

    def against(query, keys):
        return jnp.concatenate(
            [
                lax.dot_general(
                    query[:, columns(c)], keys(c), NT, preferred_element_type=jnp.float32
                )
                for c in range(chunks)
            ],
            axis=0,
        )

    def summary(top, total):
        shape = (all_rows, LANES)
        part = over(iota(shape, 1), HEADS)
        spread = jnp.zeros(shape, jnp.float32)
        for place, value in enumerate(three_parts(top) + three_parts(total)):
            spread = jnp.where(part == place, value, spread)
        spread = jnp.where(
            within(iota(shape, 1), HEADS) == over(iota(shape, 0), steps), spread, 0.0
        )
        pick = within(iota((ROWS, all_rows), 1), steps) == iota((ROWS, all_rows), 0)
        gathered = jnp.dot(
            jnp.where(pick, 1.0, 0.0).astype(jnp.bfloat16),
            spread.astype(jnp.bfloat16),
            preferred_element_type=jnp.float32,
        )
        return gathered[:steps].astype(jnp.bfloat16)

    def own_head(mixed):
        mixed = jnp.where(diag, mixed, 0.0)
        half = mixed[: 2 * steps]
        for g in range(1, group // 2):
            half = half + mixed[2 * steps * g : 2 * steps * (g + 1)]
        return (half[:steps] + half[steps:]).astype(jnp.bfloat16)

    def largest(x):
        return jnp.max(x, axis=1, keepdims=True)

    def summed(x):
        return jnp.sum(x, axis=1, keepdims=True)

    def weighted(weight, values):
        return [
            own_head(
                jnp.dot(
                    weight[c * rows : (c + 1) * rows],
                    values(c),
                    preferred_element_type=jnp.float32,
                )
            )
            for c in range(chunks)
        ]

    for r in range(requests):
        query = jnp.where(diag_all, tiled(q_ref[r].astype(jnp.float32) * scale, group), 0.0)
        query = query.astype(jnp.bfloat16)
        query_ref[r] = query
        keys = tiled(nk_ref[r].astype(jnp.float32), group).astype(jnp.bfloat16)
        values = tiled(nv_ref[r].astype(jnp.float32), group).astype(jnp.bfloat16)
        score = against(query, lambda c: keys[:, columns(c)])
        usable = iota(score.shape, 1) <= within(iota(score.shape, 0), steps)
        score = jnp.where(usable, score, masked_score)
        top = largest(score)
        weight = jnp.where(usable, jnp.exp(score - top), 0.0)
        fresh_ref[r, :, width:] = summary(top, summed(weight))
        mixed = weighted(weight.astype(jnp.bfloat16), lambda c: values[:, columns(c)])
        for c in range(chunks):
            fresh_ref[r, :, columns(c)] = mixed[c]

    @pl.loop(0, requests)
    def _(r):
        @pl.when(left(r) <= 0)
        def _():
            shape = (steps, LANES)
            hi, mid, low = three_parts(jnp.full(shape, masked_score, jnp.float32))
            part = over(iota(shape, 1), HEADS)
            empty = jnp.where(part == 0, hi, jnp.where(part == 1, mid, low))
            out_ref[r, :, width:] = jnp.where(part < 3, empty, 0.0).astype(jnp.bfloat16)
            out_ref[r, :, :width] = jnp.zeros((steps, width), jnp.bfloat16)

    def one(r, count):
        part = pl.ds(0, count)
        move(0, r, count).wait()
        query = query_ref[r]
        score = against(query, lambda c: kbuf[r, part, columns(c)])
        if count < block:
            usable = iota(score.shape, 1) < left(r)
            score = jnp.where(usable, score, masked_score)
        top = largest(score)
        weight = jnp.exp(score - top)
        if count < block:
            weight = jnp.where(usable, weight, 0.0)
        total = summed(weight)
        weight = weight.astype(jnp.bfloat16)
        move(1, r, count).wait()
        mixed = weighted(weight, lambda c: vbuf[r, part, columns(c)])
        out_ref[r, :, width:] = summary(top, total)
        for c in range(chunks):
            out_ref[r, :, columns(c)] = mixed[c]

    for kind, count in ((is_short, SHORT), (is_full, block)):

        @pl.loop(0, requests)
        def _(r):
            @pl.when(kind(r))
            def _():
                one(r, count)


def project(count, columns, ids_ref, hidden_ref, gain_ref, weight_ref, *refs):
    parts = refs[:count]
    attn_ref, own_ref, send_ref, attn_buf, res_buf = refs[count:]
    requests, steps, width = hidden_ref.shape
    feature = attn_ref.shape[2]
    head = width // HEADS
    seq = lax.axis_index("seq")
    tp = lax.axis_index("tp")

    def moved(x, amount):
        return pltpu.roll(x, LANES - amount, 1)

    def rows_of(ref, lanes):
        pieces = [ref[r, :, lanes].astype(jnp.float32) for r in range(requests)]
        blank = jnp.zeros((ROWS - requests * steps, pieces[0].shape[1]), jnp.float32)
        return jnp.concatenate(pieces + [blank], axis=0)

    tops, totals = [], []
    for ref in parts:
        x = rows_of(ref, slice(width, width + LANES))
        tops.append(x + moved(x, HEADS) + moved(x, 2 * HEADS))
        totals.append(moved(x, 3 * HEADS) + moved(x, 4 * HEADS) + moved(x, 5 * HEADS))
    overall = functools.reduce(jnp.maximum, tops)
    factors = [jnp.exp(top - overall) for top in tops]
    total = functools.reduce(jnp.add, [f * t for f, t in zip(factors, totals)])
    real = (iota(total.shape, 1) < HEADS) & (iota(total.shape, 0) < requests * steps)
    inverse = jnp.where(real, 1.0 / jnp.where(real, total, 1.0), 0.0)
    ratio = jnp.concatenate([jnp.where(real, f, 0.0) * inverse for f in factors], axis=0)
    expand = jnp.where(
        (within(iota((LANES, width), 0), HEADS) == over(iota((LANES, width), 1), head))
        & (iota((LANES, width), 0) < 3 * HEADS),
        1.0,
        0.0,
    ).astype(jnp.bfloat16)
    hi, mid, low = three_parts(ratio)
    packed = hi + pltpu.roll(mid, HEADS, 1) + pltpu.roll(low, 2 * HEADS, 1)
    wide = jnp.dot(packed.astype(jnp.bfloat16), expand, preferred_element_type=jnp.float32)
    context = jnp.zeros((ROWS, width), jnp.float32)
    for b, ref in enumerate(parts):
        context = context + wide[b * ROWS : (b + 1) * ROWS] * rows_of(ref, slice(0, width))
    attention = jnp.dot(
        context.astype(jnp.bfloat16), weight_ref[...], preferred_element_type=jnp.float32
    )
    residual = rows_of(hidden_ref, slice(0, width)) + attention
    normed = (
        residual
        * lax.rsqrt(jnp.mean(residual * residual, axis=1, keepdims=True) + norm_epsilon)
        * gain_ref[...]
    )
    row = iota((ROWS, columns), 0)
    lane = iota((ROWS, columns), 1) - tp * ROWS
    extra = jnp.where((lane >= 0) & (lane < ROWS), -1.0, 0.0)
    for i in range(requests * steps):
        first, second = [
            ids_ref[i // steps, k, i % steps].astype(jnp.float32) for k in range(2)
        ]
        extra = jnp.where(lane == i, jnp.where(row == requests * steps, first, second), extra)
    tail = row >= requests * steps
    message = jnp.concatenate(
        [jnp.where(tail, extra, normed[:, :columns]), normed[:, columns:]], axis=1
    ).astype(jnp.bfloat16)
    send_ref[...] = message
    attn_buf[...] = attention
    res_buf[...] = residual
    lanes = pl.ds(pl.multiple_of(seq * feature, feature), feature)
    mine = attn_buf[:, lanes]
    for r in range(requests):
        attn_ref[r] = mine[r * steps : (r + 1) * steps].astype(jnp.bfloat16)
    rest = res_buf[:, lanes]
    for r in range(requests):
        own_ref[r] = rest[r * steps : (r + 1) * steps]


def feed(
    capacity, steps, used, slices, router_ref, gate_ref, up_ref, down_ref, near_ref, far_ref,
    out_ref, tokens,
):
    half = near_ref.shape[0]
    count = 2 * half
    width = gate_ref.shape[1]
    experts = router_ref.shape[0]
    seq_size, _, requests, _, feature = out_ref.shape
    seq = lax.axis_index("seq")
    tp = lax.axis_index("tp")
    columns = count * ROWS
    core = within(tp, 2)
    for d in range(half):
        chip = over(tp, 2) ^ d
        for ref, which in ((near_ref, core), (far_ref, 1 - core)):
            start = pl.multiple_of((2 * chip + which) * ROWS, ROWS)
            tokens[pl.ds(start, ROWS), :] = ref[d]
    ids = jnp.zeros((8, columns), jnp.float32)
    for p in range(count):
        ids = ids + tokens[p * ROWS : (p + 1) * ROWS, :columns].astype(jnp.float32)[8:]
    place = used - 8
    first = ids[place : place + 1]
    second = ids[place + 1 : place + 2]
    mine = over(seq * count + tp, slices)
    mine_f = mine.astype(jnp.float32)
    hit = jnp.where((first == mine_f) | (second == mine_f), 1.0, 0.0)
    other = jnp.where(first == mine_f, second, first)
    earlier = (iota((columns, columns), 0) < iota((columns, columns), 1)) & (
        within(iota((columns, columns), 0), steps) == within(iota((columns, columns), 1), steps)
    )
    slot = jnp.dot(
        jnp.broadcast_to(hit, (ROWS, columns)).astype(jnp.bfloat16),
        jnp.where(earlier, 1.0, 0.0).astype(jnp.bfloat16),
        preferred_element_type=jnp.float32,
    )[:1]
    rows = -(-steps * capacity // ROWS) * ROWS
    row = iota((rows, columns), 0)
    choose = (
        (hit > 0.5)
        & (slot == within(row, capacity).astype(jnp.float32))
        & (within(iota((rows, columns), 1), steps) == over(row, capacity))
    )
    select = jnp.where(choose, 1.0, 0.0)
    rival = jnp.sum(select * other, axis=1, keepdims=True)
    select = select.astype(jnp.bfloat16)
    buffer = jnp.dot(select, tokens[...], preferred_element_type=jnp.float32).astype(jnp.bfloat16)
    logits = lax.dot_general(buffer, router_ref[...], NT, preferred_element_type=jnp.float32)
    index = iota((rows, experts), 1)
    ahead = jnp.sum(jnp.where(index == mine, logits, 0.0), axis=1, keepdims=True)
    behind = jnp.sum(
        jnp.where(index.astype(jnp.float32) == rival, logits, 0.0), axis=1, keepdims=True
    )
    share = 1.0 / (1.0 + jnp.exp(behind - ahead))
    gate = lax.dot_general(buffer, gate_ref[...], NT, preferred_element_type=jnp.float32)
    upward = lax.dot_general(buffer, up_ref[...], NT, preferred_element_type=jnp.float32)
    inner = (jax.nn.gelu(gate) * upward).astype(jnp.bfloat16)
    produced = jnp.dot(inner, down_ref[...], preferred_element_type=jnp.float32)
    shared = (produced * share).astype(jnp.bfloat16)
    term = lax.dot_general(select, shared, TN, preferred_element_type=jnp.float32)
    for s in range(seq_size):
        for p in range(count):
            for r in range(requests):
                start = p * ROWS + r * steps
                out_ref[s, p, r] = term[
                    start : start + steps, s * feature : (s + 1) * feature
                ].astype(jnp.bfloat16)


def limit(mebibytes):
    return pltpu.CompilerParams(vmem_limit_bytes=mebibytes * 1024 * 1024)


def stage(count, *refs):
    sources, copies, sems = refs[1 : 1 + count], refs[1 + count : 1 + 2 * count], refs[-1]
    moves = [
        pltpu.make_async_copy(source, copy, sems.at[i])
        for i, (source, copy) in enumerate(zip(sources, copies))
    ]
    for move in moves:
        move.start()
    for move in moves:
        move.wait()


def staged(after, *arrays, result=None):
    anywhere = pl.BlockSpec(memory_space=pl.ANY)
    inputs = [pltpu.with_memory_space_constraint(x, pltpu.HBM) for x in arrays]
    shapes = [pltpu.VMEM(x.shape, x.dtype) for x in arrays]
    if result is not None:
        inputs.append(result)
        shapes.append(pltpu.HBM(result.shape, result.dtype))
    count = len(inputs)
    size = sum(2 * x.size for x in arrays)
    return pl.pallas_call(
        functools.partial(stage, count),
        out_shape=tuple(shapes),
        in_specs=[anywhere] * (1 + count),
        out_specs=(anywhere,) * count,
        scratch_shapes=[pltpu.SemaphoreType.DMA((count,))],
        compiler_params=limit(4),
        cost_estimate=pl.CostEstimate(flops=0, bytes_accessed=2 * size, transcendentals=0),
        name="stage",
    )(after, *inputs)


def body(
    hidden_in,
    new_query,
    new_key,
    new_value,
    key_cache,
    value_cache,
    lengths,
    out_weight,
    norm_gain,
    router_weight,
    expert_ids,
    gate_weight,
    up_weight,
    down_weight,
):
    requests, steps, width = hidden_in.shape
    block = key_cache.shape[1]
    seq_size = lax.axis_size("seq")
    tp_size = lax.axis_size("tp")
    feature = width // seq_size
    experts = router_weight.shape[1]
    topk = expert_ids.shape[2]
    capacity = (5 * requests * tp_size * topk + 4 * experts - 1) // (4 * experts)
    slices = seq_size * tp_size // experts
    vmem = pl.BlockSpec(memory_space=pltpu.VMEM)
    smem = pl.BlockSpec(memory_space=pltpu.SMEM)
    hbm = pl.BlockSpec(memory_space=pltpu.HBM)

    small = pltpu.VMEM((requests, steps, width), jnp.bfloat16)
    partial = pltpu.VMEM((requests, steps, width + LANES), jnp.bfloat16)
    part, fresh = pl.pallas_call(
        attend,
        out_shape=(partial, partial),
        in_specs=[hbm] * 6,
        out_specs=(vmem, vmem),
        scratch_shapes=[
            pltpu.SMEM((requests,), jnp.int32),
            small,
            small,
            small,
            pltpu.VMEM((requests, ROWS, width), jnp.bfloat16),
            pltpu.VMEM((requests, block, width), jnp.bfloat16),
            pltpu.VMEM((requests, block, width), jnp.bfloat16),
            pltpu.SemaphoreType.DMA((2, requests)),
            pltpu.SemaphoreType.DMA((4,)),
        ],
        compiler_params=limit(24),
        name="attend",
    )(
        *[
            pltpu.with_memory_space_constraint(x, pltpu.HBM)
            for x in (lengths, new_query, new_key, new_value, key_cache, value_cache)
        ]
    )

    def swapped(x, axis, size, d):
        return lax.ppermute(x, axis, [(i, i ^ d) for i in range(size)])

    out_weight, gate_weight = staged(part, out_weight, gate_weight)
    parts = [fresh, part] + [swapped(part, "seq", seq_size, d) for d in range(1, seq_size)]
    attn_out, own_residual, packed = pl.pallas_call(
        functools.partial(project, seq_size + 1, tp_size * ROWS),
        out_shape=(
            pltpu.VMEM((requests, steps, feature), jnp.bfloat16),
            jax.ShapeDtypeStruct((requests, steps, feature), jnp.float32),
            jax.ShapeDtypeStruct((ROWS, width), jnp.bfloat16),
        ),
        in_specs=[smem] + [vmem] * (4 + seq_size),
        out_specs=(vmem, vmem, vmem),
        scratch_shapes=[
            pltpu.VMEM((ROWS, width), jnp.float32),
            pltpu.VMEM((ROWS, width), jnp.float32),
        ],
        compiler_params=limit(8),
        name="project",
    )(expert_ids.transpose(0, 2, 1), hidden_in, norm_gain.reshape(1, width), out_weight, *parts)
    up_weight, down_weight, attn_out = staged(packed, up_weight, down_weight, result=attn_out)
    near = jnp.stack(
        [packed] + [swapped(packed, "tp", tp_size, 2 * d) for d in range(1, tp_size // 2)]
    )
    near, up_weight, down_weight = lax.optimization_barrier((near, up_weight, down_weight))
    far = swapped(near, "tp", tp_size, 1)
    terms = pl.pallas_call(
        functools.partial(feed, capacity, steps, requests * steps, slices),
        out_shape=pltpu.VMEM((seq_size, tp_size, requests, steps, feature), jnp.bfloat16),
        in_specs=[vmem] * 6,
        out_specs=vmem,
        scratch_shapes=[pltpu.VMEM((tp_size * ROWS, width), jnp.bfloat16)],
        compiler_params=limit(16),
        name="feed",
    )(router_weight.T, gate_weight, up_weight, down_weight, near, far)
    terms = terms.reshape(seq_size * tp_size, requests, steps, feature)
    arrived = lax.all_to_all(terms, ("seq", "tp"), 0, 0, tiled=True)
    mixture = jnp.sum(arrived.astype(jnp.float32), axis=0)
    return (attn_out, (own_residual + mixture).astype(jnp.bfloat16))


def solution(mesh):
    return jax.shard_map(
        body,
        mesh=mesh,
        in_specs=(
            P("tp", None, None),
            P("tp", None, None),
            P("tp", None, None),
            P("tp", None, None),
            P("tp", "seq", None),
            P("tp", "seq", None),
            P("tp"),
            P(),
            P(),
            P(),
            P("tp", None, None),
            P(("seq", "tp"), None),
            P(("seq", "tp"), None),
            P(("seq", "tp"), None),
        ),
        out_specs=(P("tp", None, "seq"), P("tp", None, "seq")),
        check_vma=False,
    )
```

```python
import functools

import jax
import jax.numpy as jnp
from jax import lax
from jax.experimental import pallas as pl
from jax.experimental.pallas import tpu as pltpu
from jax.sharding import PartitionSpec as P

HEADS = 16
SHORT = 128
ROWS = 16
LANES = 128
masked_score = -1e30
norm_epsilon = 1e-06
NT = (((1,), (1,)), ((), ()))
TN = (((0,), (0,)), ((), ()))


def iota(shape, dim):
    return lax.broadcasted_iota(jnp.int32, shape, dim)


def over(x, n):
    if n & (n - 1) == 0:
        return lax.shift_right_logical(x, jnp.int32(n.bit_length() - 1))
    return x // n


def within(x, n):
    if n & (n - 1) == 0:
        return x & (n - 1)
    return x % n


def three_parts(x):
    hi = x.astype(jnp.bfloat16).astype(jnp.float32)
    mid = (x - hi).astype(jnp.bfloat16).astype(jnp.float32)
    return hi, mid, x - hi - mid


def tiled(x, times):
    return jnp.concatenate([x] * times, axis=0)


def attend(
    lens_hbm, q_hbm, nk_hbm, nv_hbm, k_hbm, v_hbm, out_ref, fresh_ref,
    lens, q_ref, nk_ref, nv_ref, query_ref, kbuf, vbuf, sems, small_sems,
):
    requests, block, width = k_hbm.shape
    steps = q_ref.shape[1]
    head = width // HEADS
    scale = head ** (-0.5)
    group = 256 // head
    chunks = width // 256
    rows = group * steps
    seq = lax.axis_index("seq")
    small = [
        pltpu.make_async_copy(src, dst, small_sems.at[i])
        for i, (src, dst) in enumerate(
            ((lens_hbm, lens), (q_hbm, q_ref), (nk_hbm, nk_ref), (nv_hbm, nv_ref))
        )
    ]
    for move in small:
        move.start()
    small[0].wait()

    def left(r):
        return lens[r] - seq * block

    def is_full(r):
        return left(r) >= block

    def is_short(r):
        return (left(r) > 0) & (left(r) < block)

    def move(which, r, piece):
        src, dst = ((k_hbm, kbuf), (v_hbm, vbuf))[which]
        part = pl.ds(*piece)
        return pltpu.make_async_copy(
            src.at[r, part], dst.at[r, part], sems.at[which, r, 1 if piece[0] else 0]
        )

    half = block // 2
    kinds = ((is_short, ((0, SHORT),)), (is_full, ((0, half), (half, half))))
    for kind, pieces in kinds:
        for r in range(requests):

            @pl.when(kind(r))
            def _():
                for which in range(2):
                    for piece in pieces:
                        move(which, r, piece).start()

    for move_small in small[1:]:
        move_small.wait()
    diag = over(iota((rows, 256), 0), steps) == over(iota((rows, 256), 1), head)
    diag_all = jnp.concatenate([diag] * chunks, axis=1)
    all_rows = chunks * rows

    def columns(c):
        return slice(c * 256, (c + 1) * 256)

    def against(query, keys):
        return jnp.concatenate(
            [
                lax.dot_general(
                    query[:, columns(c)], keys(c), NT, preferred_element_type=jnp.float32
                )
                for c in range(chunks)
            ],
            axis=0,
        )

    def summary(top, total):
        shape = (all_rows, LANES)
        part = over(iota(shape, 1), HEADS)
        spread = jnp.zeros(shape, jnp.float32)
        for place, value in enumerate(three_parts(top) + three_parts(total)):
            spread = jnp.where(part == place, value, spread)
        spread = jnp.where(
            within(iota(shape, 1), HEADS) == over(iota(shape, 0), steps), spread, 0.0
        )
        pick = within(iota((ROWS, all_rows), 1), steps) == iota((ROWS, all_rows), 0)
        gathered = jnp.dot(
            jnp.where(pick, 1.0, 0.0).astype(jnp.bfloat16),
            spread.astype(jnp.bfloat16),
            preferred_element_type=jnp.float32,
        )
        return gathered[:steps].astype(jnp.bfloat16)

    def own_head(mixed):
        mixed = jnp.where(diag, mixed, 0.0)
        half = mixed[: 2 * steps]
        for g in range(1, group // 2):
            half = half + mixed[2 * steps * g : 2 * steps * (g + 1)]
        return (half[:steps] + half[steps:]).astype(jnp.bfloat16)

    def largest(x):
        return jnp.max(x, axis=1, keepdims=True)

    def summed(x):
        return jnp.sum(x, axis=1, keepdims=True)

    def weighted(weight, values):
        return [
            jnp.dot(
                weight[c * rows : (c + 1) * rows], values(c), preferred_element_type=jnp.float32
            )
            for c in range(chunks)
        ]

    for r in range(requests):
        query = jnp.where(diag_all, tiled(q_ref[r].astype(jnp.float32) * scale, group), 0.0)
        query = query.astype(jnp.bfloat16)
        query_ref[r] = query
        keys = tiled(nk_ref[r].astype(jnp.float32), group).astype(jnp.bfloat16)
        values = tiled(nv_ref[r].astype(jnp.float32), group).astype(jnp.bfloat16)
        score = against(query, lambda c: keys[:, columns(c)])
        usable = iota(score.shape, 1) <= within(iota(score.shape, 0), steps)
        score = jnp.where(usable, score, masked_score)
        top = largest(score)
        weight = jnp.where(usable, jnp.exp(score - top), 0.0)
        fresh_ref[r, :, width:] = summary(top, summed(weight))
        mixed = weighted(weight.astype(jnp.bfloat16), lambda c: values[:, columns(c)])
        for c in range(chunks):
            fresh_ref[r, :, columns(c)] = own_head(mixed[c])

    @pl.loop(0, requests)
    def _(r):
        @pl.when(left(r) <= 0)
        def _():
            shape = (steps, LANES)
            hi, mid, low = three_parts(jnp.full(shape, masked_score, jnp.float32))
            part = over(iota(shape, 1), HEADS)
            empty = jnp.where(part == 0, hi, jnp.where(part == 1, mid, low))
            out_ref[r, :, width:] = jnp.where(part < 3, empty, 0.0).astype(jnp.bfloat16)
            out_ref[r, :, :width] = jnp.zeros((steps, width), jnp.bfloat16)

    def one(r, pieces):
        query = query_ref[r]
        scores = []
        for piece in pieces:
            move(0, r, piece).wait()
            score = against(query, lambda c: kbuf[r, pl.ds(*piece), columns(c)])
            if len(pieces) == 1:
                usable = iota(score.shape, 1) < left(r)
                score = jnp.where(usable, score, masked_score)
            scores.append(score)
        top = functools.reduce(jnp.maximum, [largest(score) for score in scores])
        weights = [jnp.exp(score - top) for score in scores]
        if len(pieces) == 1:
            weights[0] = jnp.where(usable, weights[0], 0.0)
        total = functools.reduce(jnp.add, [summed(weight) for weight in weights])
        mixed = [0.0] * chunks
        for piece, weight in zip(pieces, weights):
            weight = weight.astype(jnp.bfloat16)
            move(1, r, piece).wait()
            values = weighted(weight, lambda c: vbuf[r, pl.ds(*piece), columns(c)])
            mixed = [former + value for former, value in zip(mixed, values)]
        out_ref[r, :, width:] = summary(top, total)
        for c in range(chunks):
            out_ref[r, :, columns(c)] = own_head(mixed[c])

    for kind, pieces in kinds:

        @pl.loop(0, requests)
        def _(r):
            @pl.when(kind(r))
            def _():
                one(r, pieces)


def project(count, columns, ids_ref, hidden_ref, gain_ref, weight_ref, *refs):
    parts = refs[:count]
    attn_ref, own_ref, send_ref, attn_buf, res_buf = refs[count:]
    requests, steps, width = hidden_ref.shape
    feature = attn_ref.shape[2]
    head = width // HEADS
    seq = lax.axis_index("seq")
    tp = lax.axis_index("tp")

    def moved(x, amount):
        return pltpu.roll(x, LANES - amount, 1)

    def rows_of(ref, lanes):
        pieces = [ref[r, :, lanes].astype(jnp.float32) for r in range(requests)]
        blank = jnp.zeros((ROWS - requests * steps, pieces[0].shape[1]), jnp.float32)
        return jnp.concatenate(pieces + [blank], axis=0)

    tops, totals = [], []
    for ref in parts:
        x = rows_of(ref, slice(width, width + LANES))
        tops.append(x + moved(x, HEADS) + moved(x, 2 * HEADS))
        totals.append(moved(x, 3 * HEADS) + moved(x, 4 * HEADS) + moved(x, 5 * HEADS))
    overall = functools.reduce(jnp.maximum, tops)
    factors = [jnp.exp(top - overall) for top in tops]
    total = functools.reduce(jnp.add, [f * t for f, t in zip(factors, totals)])
    real = (iota(total.shape, 1) < HEADS) & (iota(total.shape, 0) < requests * steps)
    inverse = jnp.where(real, 1.0 / jnp.where(real, total, 1.0), 0.0)
    ratio = jnp.concatenate([jnp.where(real, f, 0.0) * inverse for f in factors], axis=0)
    expand = jnp.where(
        (within(iota((4 * HEADS, width), 0), HEADS) == over(iota((4 * HEADS, width), 1), head))
        & (iota((4 * HEADS, width), 0) < 3 * HEADS),
        1.0,
        0.0,
    ).astype(jnp.bfloat16)
    hi, mid, low = three_parts(ratio)
    packed = hi + pltpu.roll(mid, HEADS, 1) + pltpu.roll(low, 2 * HEADS, 1)
    packed = packed.astype(jnp.bfloat16)[:, : 4 * HEADS]
    wide = jnp.dot(packed, expand, preferred_element_type=jnp.float32)
    context = jnp.zeros((ROWS, width), jnp.float32)
    for b, ref in enumerate(parts):
        context = context + wide[b * ROWS : (b + 1) * ROWS] * rows_of(ref, slice(0, width))
    attention = jnp.dot(
        context.astype(jnp.bfloat16), weight_ref[...], preferred_element_type=jnp.float32
    )
    residual = rows_of(hidden_ref, slice(0, width)) + attention
    normed = (
        residual
        * lax.rsqrt(jnp.mean(residual * residual, axis=1, keepdims=True) + norm_epsilon)
        * gain_ref[...]
    )
    row = iota((ROWS, columns), 0)
    lane = iota((ROWS, columns), 1) - tp * ROWS
    extra = jnp.where((lane >= 0) & (lane < ROWS), -1.0, 0.0)
    for i in range(requests * steps):
        first, second = [
            ids_ref[i // steps, k, i % steps].astype(jnp.float32) for k in range(2)
        ]
        extra = jnp.where(lane == i, jnp.where(row == requests * steps, first, second), extra)
    tail = row >= requests * steps
    message = jnp.concatenate(
        [jnp.where(tail, extra, normed[:, :columns]), normed[:, columns:]], axis=1
    ).astype(jnp.bfloat16)
    send_ref[...] = message
    attn_buf[...] = attention
    res_buf[...] = residual
    lanes = pl.ds(pl.multiple_of(seq * feature, feature), feature)
    mine = attn_buf[:, lanes]
    for r in range(requests):
        attn_ref[r] = mine[r * steps : (r + 1) * steps].astype(jnp.bfloat16)
    rest = res_buf[:, lanes]
    for r in range(requests):
        own_ref[r] = rest[r * steps : (r + 1) * steps]


def feed(
    capacity, steps, used, slices, router_ref, gate_ref, up_ref, down_ref, near_ref, far_ref,
    out_ref, tokens,
):
    half = near_ref.shape[0]
    count = 2 * half
    width = gate_ref.shape[1]
    experts = router_ref.shape[0]
    _, seq_size, requests, _, feature = out_ref.shape
    seq = lax.axis_index("seq")
    tp = lax.axis_index("tp")
    columns = count * ROWS
    core = within(tp, 2)
    for d in range(half):
        chip = over(tp, 2) ^ d
        for ref, which in ((near_ref, core), (far_ref, 1 - core)):
            start = pl.multiple_of((2 * chip + which) * ROWS, ROWS)
            tokens[pl.ds(start, ROWS), :] = ref[d]
    ids = jnp.zeros((8, columns), jnp.float32)
    for p in range(count):
        ids = ids + tokens[p * ROWS : (p + 1) * ROWS, :columns].astype(jnp.float32)[8:]
    place = used - 8
    first = ids[place : place + 1]
    second = ids[place + 1 : place + 2]
    mine = over(seq * count + tp, slices)
    mine_f = mine.astype(jnp.float32)
    hit = jnp.where((first == mine_f) | (second == mine_f), 1.0, 0.0)
    other = jnp.where(first == mine_f, second, first)
    earlier = (iota((columns, columns), 0) < iota((columns, columns), 1)) & (
        within(iota((columns, columns), 0), steps) == within(iota((columns, columns), 1), steps)
    )
    slot = jnp.dot(
        jnp.broadcast_to(hit, (ROWS, columns)).astype(jnp.bfloat16),
        jnp.where(earlier, 1.0, 0.0).astype(jnp.bfloat16),
        preferred_element_type=jnp.float32,
    )[:1]
    rows = -(-steps * capacity // ROWS) * ROWS
    row = iota((rows, columns), 0)
    choose = (
        (hit > 0.5)
        & (slot == within(row, capacity).astype(jnp.float32))
        & (within(iota((rows, columns), 1), steps) == over(row, capacity))
    )
    select = jnp.where(choose, 1.0, 0.0)
    rival = jnp.sum(select * other, axis=1, keepdims=True)
    select = select.astype(jnp.bfloat16)
    buffer = jnp.dot(select, tokens[...], preferred_element_type=jnp.float32).astype(jnp.bfloat16)
    logits = lax.dot_general(buffer, router_ref[...], NT, preferred_element_type=jnp.float32)
    index = iota((rows, experts), 1)
    ahead = jnp.sum(jnp.where(index == mine, logits, 0.0), axis=1, keepdims=True)
    behind = jnp.sum(
        jnp.where(index.astype(jnp.float32) == rival, logits, 0.0), axis=1, keepdims=True
    )
    share = 1.0 / (1.0 + jnp.exp(behind - ahead))
    gate = lax.dot_general(buffer, gate_ref[...], NT, preferred_element_type=jnp.float32)
    upward = lax.dot_general(buffer, up_ref[...], NT, preferred_element_type=jnp.float32)
    inner = (jax.nn.gelu(gate) * upward).astype(jnp.bfloat16)
    produced = jnp.dot(inner, down_ref[...], preferred_element_type=jnp.float32)
    shared = (produced * share).astype(jnp.bfloat16)
    term = lax.dot_general(select, shared, TN, preferred_element_type=jnp.float32)
    for s in range(seq_size):
        for p in range(count):
            for r in range(requests):
                start = p * ROWS + r * steps
                out_ref[p, s, r] = term[
                    start : start + steps, s * feature : (s + 1) * feature
                ].astype(jnp.bfloat16)


def limit(mebibytes):
    return pltpu.CompilerParams(vmem_limit_bytes=mebibytes * 1024 * 1024)


def stage(count, *refs):
    sources, copies, sems = refs[1 : 1 + count], refs[1 + count : 1 + 2 * count], refs[-1]
    moves = [
        pltpu.make_async_copy(source, copy, sems.at[i])
        for i, (source, copy) in enumerate(zip(sources, copies))
    ]
    for move in moves:
        move.start()
    for move in moves:
        move.wait()


def staged(after, *arrays, result=None):
    anywhere = pl.BlockSpec(memory_space=pl.ANY)
    inputs = [pltpu.with_memory_space_constraint(x, pltpu.HBM) for x in arrays]
    shapes = [pltpu.VMEM(x.shape, x.dtype) for x in arrays]
    if result is not None:
        inputs.append(result)
        shapes.append(pltpu.HBM(result.shape, result.dtype))
    count = len(inputs)
    size = sum(2 * x.size for x in arrays)
    return pl.pallas_call(
        functools.partial(stage, count),
        out_shape=tuple(shapes),
        in_specs=[anywhere] * (1 + count),
        out_specs=(anywhere,) * count,
        scratch_shapes=[pltpu.SemaphoreType.DMA((count,))],
        compiler_params=limit(4),
        cost_estimate=pl.CostEstimate(flops=0, bytes_accessed=2 * size, transcendentals=0),
        name="stage",
    )(after, *inputs)


def body(
    hidden_in,
    new_query,
    new_key,
    new_value,
    key_cache,
    value_cache,
    lengths,
    out_weight,
    norm_gain,
    router_weight,
    expert_ids,
    gate_weight,
    up_weight,
    down_weight,
):
    requests, steps, width = hidden_in.shape
    block = key_cache.shape[1]
    seq_size = lax.axis_size("seq")
    tp_size = lax.axis_size("tp")
    feature = width // seq_size
    experts = router_weight.shape[1]
    topk = expert_ids.shape[2]
    capacity = (5 * requests * tp_size * topk + 4 * experts - 1) // (4 * experts)
    slices = seq_size * tp_size // experts
    vmem = pl.BlockSpec(memory_space=pltpu.VMEM)
    smem = pl.BlockSpec(memory_space=pltpu.SMEM)
    hbm = pl.BlockSpec(memory_space=pltpu.HBM)

    small = pltpu.VMEM((requests, steps, width), jnp.bfloat16)
    partial = pltpu.VMEM((requests, steps, width + LANES), jnp.bfloat16)
    part, fresh = pl.pallas_call(
        attend,
        out_shape=(partial, partial),
        in_specs=[hbm] * 6,
        out_specs=(vmem, vmem),
        scratch_shapes=[
            pltpu.SMEM((requests,), jnp.int32),
            small,
            small,
            small,
            pltpu.VMEM((requests, ROWS, width), jnp.bfloat16),
            pltpu.VMEM((requests, block, width), jnp.bfloat16),
            pltpu.VMEM((requests, block, width), jnp.bfloat16),
            pltpu.SemaphoreType.DMA((2, requests, 2)),
            pltpu.SemaphoreType.DMA((4,)),
        ],
        compiler_params=limit(24),
        name="attend",
    )(
        *[
            pltpu.with_memory_space_constraint(x, pltpu.HBM)
            for x in (lengths, new_query, new_key, new_value, key_cache, value_cache)
        ]
    )

    def swapped(x, axis, size, d):
        return lax.ppermute(x, axis, [(i, i ^ d) for i in range(size)])

    out_weight, gate_weight = staged(part, out_weight, gate_weight)
    parts = [fresh, part] + [swapped(part, "seq", seq_size, d) for d in range(1, seq_size)]
    attn_out, own_residual, packed = pl.pallas_call(
        functools.partial(project, seq_size + 1, tp_size * ROWS),
        out_shape=(
            pltpu.VMEM((requests, steps, feature), jnp.bfloat16),
            jax.ShapeDtypeStruct((requests, steps, feature), jnp.float32),
            jax.ShapeDtypeStruct((ROWS, width), jnp.bfloat16),
        ),
        in_specs=[smem] + [vmem] * (4 + seq_size),
        out_specs=(vmem, vmem, vmem),
        scratch_shapes=[
            pltpu.VMEM((ROWS, width), jnp.float32),
            pltpu.VMEM((ROWS, width), jnp.float32),
        ],
        compiler_params=limit(8),
        name="project",
    )(expert_ids.transpose(0, 2, 1), hidden_in, norm_gain.reshape(1, width), out_weight, *parts)
    up_weight, down_weight, attn_out = staged(packed, up_weight, down_weight, result=attn_out)
    near = jnp.stack(
        [packed] + [swapped(packed, "tp", tp_size, 2 * d) for d in range(1, tp_size // 2)]
    )
    near, up_weight, down_weight = lax.optimization_barrier((near, up_weight, down_weight))
    far = swapped(near, "tp", tp_size, 1)
    terms = pl.pallas_call(
        functools.partial(feed, capacity, steps, requests * steps, slices),
        out_shape=pltpu.VMEM((tp_size, seq_size, requests, steps, feature), jnp.bfloat16),
        in_specs=[vmem] * 6,
        out_specs=vmem,
        scratch_shapes=[pltpu.VMEM((tp_size * ROWS, width), jnp.bfloat16)],
        compiler_params=limit(16),
        name="feed",
    )(router_weight.T, gate_weight, up_weight, down_weight, near, far)
    terms = terms.reshape(seq_size * tp_size, requests, steps, feature)
    arrived = lax.all_to_all(terms, ("tp", "seq"), 0, 0, tiled=True)
    mixture = jnp.sum(arrived.astype(jnp.float32), axis=0)
    return (attn_out, (own_residual + mixture).astype(jnp.bfloat16))


def solution(mesh):
    return jax.shard_map(
        body,
        mesh=mesh,
        in_specs=(
            P("tp", None, None),
            P("tp", None, None),
            P("tp", None, None),
            P("tp", None, None),
            P("tp", "seq", None),
            P("tp", "seq", None),
            P("tp"),
            P(),
            P(),
            P(),
            P("tp", None, None),
            P(("seq", "tp"), None),
            P(("seq", "tp"), None),
            P(("seq", "tp"), None),
        ),
        out_specs=(P("tp", None, "seq"), P("tp", None, "seq")),
        check_vma=False,
    )
```

```python
import functools

import jax
import jax.numpy as jnp
from jax import lax
from jax.experimental import pallas as pl
from jax.experimental.pallas import tpu as pltpu
from jax.sharding import PartitionSpec as P

HEADS = 16
SHORT = 128
ROWS = 16
LANES = 128
masked_score = -1e30
norm_epsilon = 1e-06
NT = (((1,), (1,)), ((), ()))
TN = (((0,), (0,)), ((), ()))


def iota(shape, dim):
    return lax.broadcasted_iota(jnp.int32, shape, dim)


def over(x, n):
    if n & (n - 1) == 0:
        return lax.shift_right_logical(x, jnp.int32(n.bit_length() - 1))
    return x // n


def within(x, n):
    if n & (n - 1) == 0:
        return x & (n - 1)
    return x % n


def three_parts(x):
    hi = x.astype(jnp.bfloat16).astype(jnp.float32)
    mid = (x - hi).astype(jnp.bfloat16).astype(jnp.float32)
    return hi, mid, x - hi - mid


def tiled(x, times):
    return jnp.concatenate([x] * times, axis=0)


def attend(
    lens_hbm, q_hbm, nk_hbm, nv_hbm, k_hbm, v_hbm, out_ref, fresh_ref,
    lens, q_ref, nk_ref, nv_ref, query_ref, kbuf, vbuf, sems, small_sems,
):
    requests, block, width = k_hbm.shape
    steps = q_ref.shape[1]
    head = width // HEADS
    scale = head ** (-0.5)
    group = 256 // head
    chunks = width // 256
    rows = group * steps
    seq = lax.axis_index("seq")
    small = [
        pltpu.make_async_copy(src, dst, small_sems.at[i])
        for i, (src, dst) in enumerate(
            ((lens_hbm, lens), (q_hbm, q_ref), (nk_hbm, nk_ref), (nv_hbm, nv_ref))
        )
    ]
    for move in small:
        move.start()
    small[0].wait()

    def left(r):
        return lens[r] - seq * block

    def is_full(r):
        return left(r) >= block

    def is_short(r):
        return (left(r) > 0) & (left(r) < block)

    def move(which, r, count):
        src, dst = ((k_hbm, kbuf), (v_hbm, vbuf))[which]
        part = pl.ds(0, count)
        return pltpu.make_async_copy(src.at[r, part], dst.at[r, part], sems.at[which, r])

    for kind, count in ((is_short, SHORT), (is_full, block)):
        for r in range(requests):

            @pl.when(kind(r))
            def _():
                for which in range(2):
                    move(which, r, count).start()

    for move_small in small[1:]:
        move_small.wait()
    diag = over(iota((rows, 256), 0), steps) == over(iota((rows, 256), 1), head)
    diag_all = jnp.concatenate([diag] * chunks, axis=1)
    all_rows = chunks * rows

    def columns(c):
        return slice(c * 256, (c + 1) * 256)

    def against(query, keys):
        return jnp.concatenate(
            [
                lax.dot_general(
                    query[:, columns(c)], keys(c), NT, preferred_element_type=jnp.float32
                )
                for c in range(chunks)
            ],
            axis=0,
        )

    def summary(top, total):
        shape = (all_rows, LANES)
        part = over(iota(shape, 1), HEADS)
        spread = jnp.zeros(shape, jnp.float32)
        for place, value in enumerate(three_parts(top) + three_parts(total)):
            spread = jnp.where(part == place, value, spread)
        spread = jnp.where(
            within(iota(shape, 1), HEADS) == over(iota(shape, 0), steps), spread, 0.0
        )
        pick = within(iota((ROWS, all_rows), 1), steps) == iota((ROWS, all_rows), 0)
        gathered = jnp.dot(
            jnp.where(pick, 1.0, 0.0).astype(jnp.bfloat16),
            spread.astype(jnp.bfloat16),
            preferred_element_type=jnp.float32,
        )
        return gathered[:steps].astype(jnp.bfloat16)

    def own_head(mixed):
        mixed = jnp.where(diag, mixed, 0.0)
        half = mixed[: 2 * steps]
        for g in range(1, group // 2):
            half = half + mixed[2 * steps * g : 2 * steps * (g + 1)]
        return (half[:steps] + half[steps:]).astype(jnp.bfloat16)

    def largest(x):
        return jnp.max(x, axis=1, keepdims=True)

    def summed(x):
        return jnp.sum(x, axis=1, keepdims=True)

    def weighted(weight, values):
        return [
            own_head(
                jnp.dot(
                    weight[c * rows : (c + 1) * rows],
                    values(c),
                    preferred_element_type=jnp.float32,
                )
            )
            for c in range(chunks)
        ]

    for r in range(requests):
        query = jnp.where(diag_all, tiled(q_ref[r].astype(jnp.float32) * scale, group), 0.0)
        query = query.astype(jnp.bfloat16)
        query_ref[r] = query
        keys = tiled(nk_ref[r].astype(jnp.float32), group).astype(jnp.bfloat16)
        values = tiled(nv_ref[r].astype(jnp.float32), group).astype(jnp.bfloat16)
        score = against(query, lambda c: keys[:, columns(c)])
        usable = iota(score.shape, 1) <= within(iota(score.shape, 0), steps)
        score = jnp.where(usable, score, masked_score)
        top = largest(score)
        weight = jnp.where(usable, jnp.exp(score - top), 0.0)
        fresh_ref[r, :, width:] = summary(top, summed(weight))
        mixed = weighted(weight.astype(jnp.bfloat16), lambda c: values[:, columns(c)])
        for c in range(chunks):
            fresh_ref[r, :, columns(c)] = mixed[c]

    @pl.loop(0, requests)
    def _(r):
        @pl.when(left(r) <= 0)
        def _():
            shape = (steps, LANES)
            hi, mid, low = three_parts(jnp.full(shape, masked_score, jnp.float32))
            part = over(iota(shape, 1), HEADS)
            empty = jnp.where(part == 0, hi, jnp.where(part == 1, mid, low))
            out_ref[r, :, width:] = jnp.where(part < 3, empty, 0.0).astype(jnp.bfloat16)
            out_ref[r, :, :width] = jnp.zeros((steps, width), jnp.bfloat16)

    def one(r, count):
        part = pl.ds(0, count)
        move(0, r, count).wait()
        query = query_ref[r]
        score = against(query, lambda c: kbuf[r, part, columns(c)])
        if count < block:
            usable = iota(score.shape, 1) < left(r)
            score = jnp.where(usable, score, masked_score)
        top = largest(score)
        weight = jnp.exp(score - top)
        if count < block:
            weight = jnp.where(usable, weight, 0.0)
        total = summed(weight)
        weight = weight.astype(jnp.bfloat16)
        move(1, r, count).wait()
        mixed = weighted(weight, lambda c: vbuf[r, part, columns(c)])
        out_ref[r, :, width:] = summary(top, total)
        for c in range(chunks):
            out_ref[r, :, columns(c)] = mixed[c]

    for kind, count in ((is_short, SHORT), (is_full, block)):

        @pl.loop(0, requests)
        def _(r):
            @pl.when(kind(r))
            def _():
                one(r, count)


def project(count, columns, cut, ids_ref, hidden_ref, gain_ref, weight_ref, gate_hbm, *refs):
    parts = refs[:count]
    attn_ref, own_ref, send_ref, gate_ref, attn_buf, res_buf, sem = refs[count:]
    gate_move = pltpu.make_async_copy(gate_hbm.at[pl.ds(cut, gate_ref.shape[0])], gate_ref, sem)
    gate_move.start()
    requests, steps, width = hidden_ref.shape
    feature = attn_ref.shape[2]
    head = width // HEADS
    seq = lax.axis_index("seq")
    tp = lax.axis_index("tp")

    def moved(x, amount):
        return pltpu.roll(x, LANES - amount, 1)

    def rows_of(ref, lanes):
        pieces = [ref[r, :, lanes].astype(jnp.float32) for r in range(requests)]
        blank = jnp.zeros((ROWS - requests * steps, pieces[0].shape[1]), jnp.float32)
        return jnp.concatenate(pieces + [blank], axis=0)

    tops, totals = [], []
    for ref in parts:
        x = rows_of(ref, slice(width, width + LANES))
        tops.append(x + moved(x, HEADS) + moved(x, 2 * HEADS))
        totals.append(moved(x, 3 * HEADS) + moved(x, 4 * HEADS) + moved(x, 5 * HEADS))
    overall = functools.reduce(jnp.maximum, tops)
    factors = [jnp.exp(top - overall) for top in tops]
    total = functools.reduce(jnp.add, [f * t for f, t in zip(factors, totals)])
    real = (iota(total.shape, 1) < HEADS) & (iota(total.shape, 0) < requests * steps)
    inverse = jnp.where(real, 1.0 / jnp.where(real, total, 1.0), 0.0)
    ratio = jnp.concatenate([jnp.where(real, f, 0.0) * inverse for f in factors], axis=0)
    expand = jnp.where(
        (within(iota((4 * HEADS, width), 0), HEADS) == over(iota((4 * HEADS, width), 1), head))
        & (iota((4 * HEADS, width), 0) < 3 * HEADS),
        1.0,
        0.0,
    ).astype(jnp.bfloat16)
    hi, mid, low = three_parts(ratio)
    packed = hi + pltpu.roll(mid, HEADS, 1) + pltpu.roll(low, 2 * HEADS, 1)
    packed = packed.astype(jnp.bfloat16)[:, : 4 * HEADS]
    wide = jnp.dot(packed, expand, preferred_element_type=jnp.float32)
    context = jnp.zeros((ROWS, width), jnp.float32)
    for b, ref in enumerate(parts):
        context = context + wide[b * ROWS : (b + 1) * ROWS] * rows_of(ref, slice(0, width))
    attention = jnp.dot(
        context.astype(jnp.bfloat16), weight_ref[...], preferred_element_type=jnp.float32
    )
    residual = rows_of(hidden_ref, slice(0, width)) + attention
    normed = (
        residual
        * lax.rsqrt(jnp.mean(residual * residual, axis=1, keepdims=True) + norm_epsilon)
        * gain_ref[...]
    )
    row = iota((ROWS, columns), 0)
    lane = iota((ROWS, columns), 1) - tp * ROWS
    extra = jnp.where((lane >= 0) & (lane < ROWS), -1.0, 0.0)
    for i in range(requests * steps):
        first, second = [
            ids_ref[i // steps, k, i % steps].astype(jnp.float32) for k in range(2)
        ]
        extra = jnp.where(lane == i, jnp.where(row == requests * steps, first, second), extra)
    tail = row >= requests * steps
    message = jnp.concatenate(
        [jnp.where(tail, extra, normed[:, :columns]), normed[:, columns:]], axis=1
    ).astype(jnp.bfloat16)
    send_ref[...] = message
    attn_buf[...] = attention
    res_buf[...] = residual
    lanes = pl.ds(pl.multiple_of(seq * feature, feature), feature)
    mine = attn_buf[:, lanes]
    for r in range(requests):
        attn_ref[r] = mine[r * steps : (r + 1) * steps].astype(jnp.bfloat16)
    rest = res_buf[:, lanes]
    for r in range(requests):
        own_ref[r] = rest[r * steps : (r + 1) * steps]
    gate_move.wait()


def feed(
    capacity, steps, used, slices, router_ref, gate_one, gate_two, up_one, up_hbm, down_hbm,
    near_ref, far_ref, out_ref, tokens, up_two, down_ref, sems,
):
    cut, width = gate_one.shape
    up_move = pltpu.make_async_copy(
        up_hbm.at[pl.ds(cut, up_two.shape[0])], up_two, sems.at[0]
    )
    down_move = pltpu.make_async_copy(down_hbm, down_ref, sems.at[1])
    up_move.start()
    down_move.start()
    half = near_ref.shape[0]
    count = 2 * half
    experts = router_ref.shape[0]
    seq_size, _, requests, _, feature = out_ref.shape
    seq = lax.axis_index("seq")
    tp = lax.axis_index("tp")
    columns = count * ROWS
    core = within(tp, 2)
    for d in range(half):
        chip = over(tp, 2) ^ d
        for ref, which in ((near_ref, core), (far_ref, 1 - core)):
            start = pl.multiple_of((2 * chip + which) * ROWS, ROWS)
            tokens[pl.ds(start, ROWS), :] = ref[d]
    ids = jnp.zeros((8, columns), jnp.float32)
    for p in range(count):
        ids = ids + tokens[p * ROWS : (p + 1) * ROWS, :columns].astype(jnp.float32)[8:]
    place = used - 8
    first = ids[place : place + 1]
    second = ids[place + 1 : place + 2]
    mine = over(seq * count + tp, slices)
    mine_f = mine.astype(jnp.float32)
    hit = jnp.where((first == mine_f) | (second == mine_f), 1.0, 0.0)
    other = jnp.where(first == mine_f, second, first)
    earlier = (iota((columns, columns), 0) < iota((columns, columns), 1)) & (
        within(iota((columns, columns), 0), steps) == within(iota((columns, columns), 1), steps)
    )
    slot = jnp.dot(
        jnp.broadcast_to(hit, (ROWS, columns)).astype(jnp.bfloat16),
        jnp.where(earlier, 1.0, 0.0).astype(jnp.bfloat16),
        preferred_element_type=jnp.float32,
    )[:1]
    rows = -(-steps * capacity // ROWS) * ROWS
    row = iota((rows, columns), 0)
    choose = (
        (hit > 0.5)
        & (slot == within(row, capacity).astype(jnp.float32))
        & (within(iota((rows, columns), 1), steps) == over(row, capacity))
    )
    select = jnp.where(choose, 1.0, 0.0)
    rival = jnp.sum(select * other, axis=1, keepdims=True)
    select = select.astype(jnp.bfloat16)
    buffer = jnp.dot(select, tokens[...], preferred_element_type=jnp.float32).astype(jnp.bfloat16)
    logits = lax.dot_general(buffer, router_ref[...], NT, preferred_element_type=jnp.float32)
    index = iota((rows, experts), 1)
    ahead = jnp.sum(jnp.where(index == mine, logits, 0.0), axis=1, keepdims=True)
    behind = jnp.sum(
        jnp.where(index.astype(jnp.float32) == rival, logits, 0.0), axis=1, keepdims=True
    )
    share = 1.0 / (1.0 + jnp.exp(behind - ahead))

    def across(ref):
        return lax.dot_general(buffer, ref[...], NT, preferred_element_type=jnp.float32)

    inner_one = (jax.nn.gelu(across(gate_one)) * across(up_one)).astype(jnp.bfloat16)
    activated = jax.nn.gelu(across(gate_two))
    up_move.wait()
    inner_two = (activated * across(up_two)).astype(jnp.bfloat16)
    down_move.wait()
    produced = jnp.dot(
        inner_one, down_ref[:cut, :], preferred_element_type=jnp.float32
    ) + jnp.dot(inner_two, down_ref[cut:, :], preferred_element_type=jnp.float32)
    shared = (produced * share).astype(jnp.bfloat16)
    term = lax.dot_general(select, shared, TN, preferred_element_type=jnp.float32)
    for s in range(seq_size):
        for p in range(count):
            for r in range(requests):
                start = p * ROWS + r * steps
                out_ref[s, p, r] = term[
                    start : start + steps, s * feature : (s + 1) * feature
                ].astype(jnp.bfloat16)


def limit(mebibytes):
    return pltpu.CompilerParams(vmem_limit_bytes=mebibytes * 1024 * 1024)


def stage(count, *refs):
    sources, copies, sems = refs[1 : 1 + count], refs[1 + count : 1 + 2 * count], refs[-1]
    moves = [
        pltpu.make_async_copy(source.at[pl.ds(0, copy.shape[0])], copy, sems.at[i])
        for i, (source, copy) in enumerate(zip(sources, copies))
    ]
    for move in moves:
        move.start()
    for move in moves:
        move.wait()


def staged(after, cuts, arrays, result=None):
    anywhere = pl.BlockSpec(memory_space=pl.ANY)
    inputs = [pltpu.with_memory_space_constraint(x, pltpu.HBM) for x in arrays]
    shapes = [pltpu.VMEM((cut,) + x.shape[1:], x.dtype) for cut, x in zip(cuts, arrays)]
    if result is not None:
        inputs.append(result)
        shapes.append(pltpu.HBM(result.shape, result.dtype))
    count = len(inputs)
    size = sum(2 * cut * x.shape[1] for cut, x in zip(cuts, arrays))
    return pl.pallas_call(
        functools.partial(stage, count),
        out_shape=tuple(shapes),
        in_specs=[anywhere] * (1 + count),
        out_specs=(anywhere,) * count,
        scratch_shapes=[pltpu.SemaphoreType.DMA((count,))],
        compiler_params=limit(4),
        cost_estimate=pl.CostEstimate(flops=0, bytes_accessed=2 * size, transcendentals=0),
        name="stage",
    )(after, *inputs)


def body(
    hidden_in,
    new_query,
    new_key,
    new_value,
    key_cache,
    value_cache,
    lengths,
    out_weight,
    norm_gain,
    router_weight,
    expert_ids,
    gate_weight,
    up_weight,
    down_weight,
):
    requests, steps, width = hidden_in.shape
    block = key_cache.shape[1]
    seq_size = lax.axis_size("seq")
    tp_size = lax.axis_size("tp")
    feature = width // seq_size
    experts = router_weight.shape[1]
    topk = expert_ids.shape[2]
    capacity = (5 * requests * tp_size * topk + 4 * experts - 1) // (4 * experts)
    slices = seq_size * tp_size // experts
    vmem = pl.BlockSpec(memory_space=pltpu.VMEM)
    smem = pl.BlockSpec(memory_space=pltpu.SMEM)
    hbm = pl.BlockSpec(memory_space=pltpu.HBM)

    small = pltpu.VMEM((requests, steps, width), jnp.bfloat16)
    partial = pltpu.VMEM((requests, steps, width + LANES), jnp.bfloat16)
    part, fresh = pl.pallas_call(
        attend,
        out_shape=(partial, partial),
        in_specs=[hbm] * 6,
        out_specs=(vmem, vmem),
        scratch_shapes=[
            pltpu.SMEM((requests,), jnp.int32),
            small,
            small,
            small,
            pltpu.VMEM((requests, ROWS, width), jnp.bfloat16),
            pltpu.VMEM((requests, block, width), jnp.bfloat16),
            pltpu.VMEM((requests, block, width), jnp.bfloat16),
            pltpu.SemaphoreType.DMA((2, requests)),
            pltpu.SemaphoreType.DMA((4,)),
        ],
        compiler_params=limit(24),
        name="attend",
    )(
        *[
            pltpu.with_memory_space_constraint(x, pltpu.HBM)
            for x in (lengths, new_query, new_key, new_value, key_cache, value_cache)
        ]
    )

    def swapped(x, axis, size, d):
        return lax.ppermute(x, axis, [(i, i ^ d) for i in range(size)])

    hidden_units = gate_weight.shape[0]
    cut = -(-hidden_units // (2 * LANES)) * LANES
    gate_weight, up_weight, down_weight = [
        pltpu.with_memory_space_constraint(x, pltpu.HBM)
        for x in (gate_weight, up_weight, down_weight)
    ]
    out_weight, gate_one = staged(part, (width, cut), (out_weight, gate_weight))
    parts = [fresh, part] + [swapped(part, "seq", seq_size, d) for d in range(1, seq_size)]
    attn_out, own_residual, packed, gate_two = pl.pallas_call(
        functools.partial(project, seq_size + 1, tp_size * ROWS, cut),
        out_shape=(
            pltpu.VMEM((requests, steps, feature), jnp.bfloat16),
            jax.ShapeDtypeStruct((requests, steps, feature), jnp.float32),
            pltpu.VMEM((ROWS, width), jnp.bfloat16),
            pltpu.VMEM((hidden_units - cut, width), jnp.bfloat16),
        ),
        in_specs=[smem] + [vmem] * 3 + [hbm] + [vmem] * (1 + seq_size),
        out_specs=(vmem, vmem, vmem, pl.BlockSpec(memory_space=pl.ANY)),
        scratch_shapes=[
            pltpu.VMEM((ROWS, width), jnp.float32),
            pltpu.VMEM((ROWS, width), jnp.float32),
            pltpu.SemaphoreType.DMA,
        ],
        compiler_params=limit(8),
        name="project",
    )(
        expert_ids.transpose(0, 2, 1),
        hidden_in,
        norm_gain.reshape(1, width),
        out_weight,
        gate_weight,
        *parts,
    )
    near = jnp.stack(
        [packed] + [swapped(packed, "tp", tp_size, 2 * d) for d in range(1, tp_size // 2)]
    )
    up_one, attn_out = staged(near, (cut,), (up_weight,), result=attn_out)
    far = swapped(near, "tp", tp_size, 1)
    terms = pl.pallas_call(
        functools.partial(feed, capacity, steps, requests * steps, slices),
        out_shape=pltpu.VMEM((seq_size, tp_size, requests, steps, feature), jnp.bfloat16),
        in_specs=[vmem] * 4 + [hbm] * 2 + [vmem] * 2,
        out_specs=vmem,
        scratch_shapes=[
            pltpu.VMEM((tp_size * ROWS, width), jnp.bfloat16),
            pltpu.VMEM((hidden_units - cut, width), jnp.bfloat16),
            pltpu.VMEM((hidden_units, width), jnp.bfloat16),
            pltpu.SemaphoreType.DMA((2,)),
        ],
        compiler_params=limit(16),
        name="feed",
    )(router_weight.T, gate_one, gate_two, up_one, up_weight, down_weight, near, far)
    terms = terms.reshape(seq_size * tp_size, requests, steps, feature)
    arrived = lax.all_to_all(terms, ("seq", "tp"), 0, 0, tiled=True)
    mixture = jnp.sum(arrived.astype(jnp.float32), axis=0)
    return (attn_out, (own_residual + mixture).astype(jnp.bfloat16))


def solution(mesh):
    return jax.shard_map(
        body,
        mesh=mesh,
        in_specs=(
            P("tp", None, None),
            P("tp", None, None),
            P("tp", None, None),
            P("tp", None, None),
            P("tp", "seq", None),
            P("tp", "seq", None),
            P("tp"),
            P(),
            P(),
            P(),
            P("tp", None, None),
            P(("seq", "tp"), None),
            P(("seq", "tp"), None),
            P(("seq", "tp"), None),
        ),
        out_specs=(P("tp", None, "seq"), P("tp", None, "seq")),
        check_vma=False,
    )
```

```python
import functools

import jax
import jax.numpy as jnp
from jax import lax
from jax.experimental import pallas as pl
from jax.experimental.pallas import tpu as pltpu
from jax.sharding import PartitionSpec as P

HEADS = 16
SHORT = 128
ROWS = 16
LANES = 128
masked_score = -1e30
norm_epsilon = 1e-06
NT = (((1,), (1,)), ((), ()))
TN = (((0,), (0,)), ((), ()))


def iota(shape, dim):
    return lax.broadcasted_iota(jnp.int32, shape, dim)


def over(x, n):
    if n & (n - 1) == 0:
        return lax.shift_right_logical(x, jnp.int32(n.bit_length() - 1))
    return x // n


def within(x, n):
    if n & (n - 1) == 0:
        return x & (n - 1)
    return x % n


def three_parts(x):
    hi = x.astype(jnp.bfloat16).astype(jnp.float32)
    mid = (x - hi).astype(jnp.bfloat16).astype(jnp.float32)
    return hi, mid, x - hi - mid


def tiled(x, times):
    return jnp.concatenate([x] * times, axis=0)


def attend(
    lens_hbm, q_hbm, nk_hbm, nv_hbm, k_hbm, v_hbm, out_ref, fresh_ref,
    lens, q_ref, nk_ref, nv_ref, query_ref, kbuf, vbuf, sems, small_sems,
):
    requests, block, width = k_hbm.shape
    steps = q_ref.shape[1]
    head = width // HEADS
    scale = head ** (-0.5)
    group = 256 // head
    chunks = width // 256
    rows = group * steps
    seq = lax.axis_index("seq")
    small = [
        pltpu.make_async_copy(src, dst, small_sems.at[i])
        for i, (src, dst) in enumerate(
            ((lens_hbm, lens), (q_hbm, q_ref), (nk_hbm, nk_ref), (nv_hbm, nv_ref))
        )
    ]
    for move in small:
        move.start()
    small[0].wait()

    def left(r):
        return lens[r] - seq * block

    def is_full(r):
        return left(r) >= block

    def is_short(r):
        return (left(r) > 0) & (left(r) < block)

    def move(which, r, count):
        src, dst = ((k_hbm, kbuf), (v_hbm, vbuf))[which]
        part = pl.ds(0, count)
        return pltpu.make_async_copy(src.at[r, part], dst.at[r, part], sems.at[which, r])

    for kind, count in ((is_short, SHORT), (is_full, block)):
        for r in range(requests):

            @pl.when(kind(r))
            def _():
                for which in range(2):
                    move(which, r, count).start()

    for move_small in small[1:]:
        move_small.wait()
    diag = over(iota((rows, 256), 0), steps) == over(iota((rows, 256), 1), head)
    diag_all = jnp.concatenate([diag] * chunks, axis=1)
    all_rows = chunks * rows

    def columns(c):
        return slice(c * 256, (c + 1) * 256)

    def against(query, keys):
        return jnp.concatenate(
            [
                lax.dot_general(
                    query[:, columns(c)], keys(c), NT, preferred_element_type=jnp.float32
                )
                for c in range(chunks)
            ],
            axis=0,
        )

    def summary(top, total):
        shape = (all_rows, LANES)
        part = over(iota(shape, 1), HEADS)
        spread = jnp.zeros(shape, jnp.float32)
        for place, value in enumerate(three_parts(top) + three_parts(total)):
            spread = jnp.where(part == place, value, spread)
        spread = jnp.where(
            within(iota(shape, 1), HEADS) == over(iota(shape, 0), steps), spread, 0.0
        )
        pick = within(iota((ROWS, all_rows), 1), steps) == iota((ROWS, all_rows), 0)
        gathered = jnp.dot(
            jnp.where(pick, 1.0, 0.0).astype(jnp.bfloat16),
            spread.astype(jnp.bfloat16),
            preferred_element_type=jnp.float32,
        )
        return gathered[:steps].astype(jnp.bfloat16)

    def own_head(mixed):
        mixed = jnp.where(diag, mixed, 0.0)
        half = mixed[: 2 * steps]
        for g in range(1, group // 2):
            half = half + mixed[2 * steps * g : 2 * steps * (g + 1)]
        return (half[:steps] + half[steps:]).astype(jnp.bfloat16)

    def largest(x):
        return jnp.max(x, axis=1, keepdims=True)

    def summed(x):
        return jnp.sum(x, axis=1, keepdims=True)

    def weighted(weight, values):
        return [
            own_head(
                jnp.dot(
                    weight[c * rows : (c + 1) * rows],
                    values(c),
                    preferred_element_type=jnp.float32,
                )
            )
            for c in range(chunks)
        ]

    for r in range(requests):
        query = jnp.where(diag_all, tiled(q_ref[r].astype(jnp.float32) * scale, group), 0.0)
        query = query.astype(jnp.bfloat16)
        query_ref[r] = query
        keys = tiled(nk_ref[r].astype(jnp.float32), group).astype(jnp.bfloat16)
        values = tiled(nv_ref[r].astype(jnp.float32), group).astype(jnp.bfloat16)
        score = against(query, lambda c: keys[:, columns(c)])
        usable = iota(score.shape, 1) <= within(iota(score.shape, 0), steps)
        score = jnp.where(usable, score, masked_score)
        top = largest(score)
        weight = jnp.where(usable, jnp.exp(score - top), 0.0)
        fresh_ref[r, :, width:] = summary(top, summed(weight))
        mixed = weighted(weight.astype(jnp.bfloat16), lambda c: values[:, columns(c)])
        for c in range(chunks):
            fresh_ref[r, :, columns(c)] = mixed[c]

    @pl.loop(0, requests)
    def _(r):
        @pl.when(left(r) <= 0)
        def _():
            shape = (steps, LANES)
            hi, mid, low = three_parts(jnp.full(shape, masked_score, jnp.float32))
            part = over(iota(shape, 1), HEADS)
            empty = jnp.where(part == 0, hi, jnp.where(part == 1, mid, low))
            out_ref[r, :, width:] = jnp.where(part < 3, empty, 0.0).astype(jnp.bfloat16)
            out_ref[r, :, :width] = jnp.zeros((steps, width), jnp.bfloat16)

    def one(r, count):
        part = pl.ds(0, count)
        move(0, r, count).wait()
        query = query_ref[r]
        score = against(query, lambda c: kbuf[r, part, columns(c)])
        if count < block:
            usable = iota(score.shape, 1) < left(r)
            score = jnp.where(usable, score, masked_score)
        top = largest(score)
        weight = jnp.exp(score - top)
        if count < block:
            weight = jnp.where(usable, weight, 0.0)
        total = summed(weight)
        weight = weight.astype(jnp.bfloat16)
        move(1, r, count).wait()
        mixed = weighted(weight, lambda c: vbuf[r, part, columns(c)])
        out_ref[r, :, width:] = summary(top, total)
        for c in range(chunks):
            out_ref[r, :, columns(c)] = mixed[c]

    for kind, count in ((is_short, SHORT), (is_full, block)):

        @pl.loop(0, requests)
        def _(r):
            @pl.when(kind(r))
            def _():
                one(r, count)


def project(count, ids_ref, hidden_ref, gain_ref, weight_ref, *refs):
    parts = refs[:count]
    attn_ref, own_ref, send_ref, attn_buf, res_buf = refs[count:]
    requests, steps, width = hidden_ref.shape
    feature = attn_ref.shape[2]
    head = width // HEADS
    seq = lax.axis_index("seq")

    def moved(x, amount):
        return pltpu.roll(x, LANES - amount, 1)

    def rows_of(ref, lanes):
        pieces = [ref[r, :, lanes].astype(jnp.float32) for r in range(requests)]
        blank = jnp.zeros((ROWS - requests * steps, pieces[0].shape[1]), jnp.float32)
        return jnp.concatenate(pieces + [blank], axis=0)

    tops, totals = [], []
    for ref in parts:
        x = rows_of(ref, slice(width, width + LANES))
        tops.append(x + moved(x, HEADS) + moved(x, 2 * HEADS))
        totals.append(moved(x, 3 * HEADS) + moved(x, 4 * HEADS) + moved(x, 5 * HEADS))
    overall = functools.reduce(jnp.maximum, tops)
    factors = [jnp.exp(top - overall) for top in tops]
    total = functools.reduce(jnp.add, [f * t for f, t in zip(factors, totals)])
    real = (iota(total.shape, 1) < HEADS) & (iota(total.shape, 0) < requests * steps)
    inverse = jnp.where(real, 1.0 / jnp.where(real, total, 1.0), 0.0)
    ratio = jnp.concatenate([jnp.where(real, f, 0.0) * inverse for f in factors], axis=0)
    expand = jnp.where(
        (within(iota((4 * HEADS, width), 0), HEADS) == over(iota((4 * HEADS, width), 1), head))
        & (iota((4 * HEADS, width), 0) < 3 * HEADS),
        1.0,
        0.0,
    ).astype(jnp.bfloat16)
    hi, mid, low = three_parts(ratio)
    packed = hi + pltpu.roll(mid, HEADS, 1) + pltpu.roll(low, 2 * HEADS, 1)
    packed = packed.astype(jnp.bfloat16)[:, : 4 * HEADS]
    wide = jnp.dot(packed, expand, preferred_element_type=jnp.float32)
    context = jnp.zeros((ROWS, width), jnp.float32)
    for b, ref in enumerate(parts):
        context = context + wide[b * ROWS : (b + 1) * ROWS] * rows_of(ref, slice(0, width))
    attention = jnp.dot(
        context.astype(jnp.bfloat16), weight_ref[...], preferred_element_type=jnp.float32
    )
    residual = rows_of(hidden_ref, slice(0, width)) + attention
    normed = (
        residual
        * lax.rsqrt(jnp.mean(residual * residual, axis=1, keepdims=True) + norm_epsilon)
        * gain_ref[...]
    )
    row = iota((ROWS, LANES), 0)
    lane = iota((ROWS, LANES), 1)
    extra = jnp.zeros((ROWS, LANES), jnp.float32)
    for i in range(requests * steps):
        for k in range(2):
            number = ids_ref[i // steps, k, i % steps].astype(jnp.float32)
            extra = jnp.where((row == i) & (lane == k), number, extra)
    for r in range(requests):
        part = slice(r * steps, (r + 1) * steps)
        send_ref[r, :, :width] = normed[part].astype(jnp.bfloat16)
        send_ref[r, :, width:] = extra[part].astype(jnp.bfloat16)
    attn_buf[...] = attention
    res_buf[...] = residual
    lanes = pl.ds(pl.multiple_of(seq * feature, feature), feature)
    mine = attn_buf[:, lanes]
    for r in range(requests):
        attn_ref[r] = mine[r * steps : (r + 1) * steps].astype(jnp.bfloat16)
    rest = res_buf[:, lanes]
    for r in range(requests):
        own_ref[r] = rest[r * steps : (r + 1) * steps]


def feed(
    capacity, steps, used, slices, router_ref, gate_ref, up_ref, down_ref, near_ref, far_ref,
    out_ref, tokens,
):
    half = near_ref.shape[0]
    count = 2 * half
    width = gate_ref.shape[1]
    experts = router_ref.shape[0]
    seq_size, _, requests, _, feature = out_ref.shape
    seq = lax.axis_index("seq")
    tp = lax.axis_index("tp")
    columns = count * ROWS
    core = within(tp, 2)
    for d in range(half):
        chip = over(tp, 2) ^ d
        for ref, which in ((near_ref, core), (far_ref, 1 - core)):
            start = pl.multiple_of((2 * chip + which) * ROWS, ROWS)
            pieces = [ref[d, r].astype(jnp.float32) for r in range(requests)]
            blank = jnp.zeros((ROWS - used, pieces[0].shape[1]), jnp.float32)
            rows_of = jnp.concatenate(pieces + [blank], axis=0)
            tokens[pl.ds(start, ROWS), :] = rows_of.astype(jnp.bfloat16)
    turn = iota((ROWS, LANES), 0) == iota((ROWS, LANES), 1)
    ids = lax.dot_general(
        jnp.where(turn, 1.0, 0.0).astype(jnp.bfloat16),
        tokens[:, width:],
        NT,
        preferred_element_type=jnp.float32,
    )
    first = ids[:1]
    second = ids[1:2]
    real = within(iota((1, columns), 1), ROWS) < used
    mine = over(seq * count + tp, slices)
    mine_f = mine.astype(jnp.float32)
    hit = jnp.where(((first == mine_f) | (second == mine_f)) & real, 1.0, 0.0)
    other = jnp.where(first == mine_f, second, first)
    earlier = (iota((columns, columns), 0) < iota((columns, columns), 1)) & (
        within(iota((columns, columns), 0), steps) == within(iota((columns, columns), 1), steps)
    )
    slot = jnp.dot(
        jnp.broadcast_to(hit, (ROWS, columns)).astype(jnp.bfloat16),
        jnp.where(earlier, 1.0, 0.0).astype(jnp.bfloat16),
        preferred_element_type=jnp.float32,
    )[:1]
    rows = -(-steps * capacity // ROWS) * ROWS
    row = iota((rows, columns), 0)
    choose = (
        (hit > 0.5)
        & (slot == within(row, capacity).astype(jnp.float32))
        & (within(iota((rows, columns), 1), steps) == over(row, capacity))
    )
    select = jnp.where(choose, 1.0, 0.0)
    rival = jnp.sum(select * other, axis=1, keepdims=True)
    select = select.astype(jnp.bfloat16)
    buffer = jnp.dot(select, tokens[:, :width], preferred_element_type=jnp.float32).astype(jnp.bfloat16)
    logits = lax.dot_general(buffer, router_ref[...], NT, preferred_element_type=jnp.float32)
    index = iota((rows, experts), 1)
    ahead = jnp.sum(jnp.where(index == mine, logits, 0.0), axis=1, keepdims=True)
    behind = jnp.sum(
        jnp.where(index.astype(jnp.float32) == rival, logits, 0.0), axis=1, keepdims=True
    )
    share = 1.0 / (1.0 + jnp.exp(behind - ahead))
    gate = lax.dot_general(buffer, gate_ref[...], NT, preferred_element_type=jnp.float32)
    upward = lax.dot_general(buffer, up_ref[...], NT, preferred_element_type=jnp.float32)
    inner = (jax.nn.gelu(gate) * upward).astype(jnp.bfloat16)
    produced = jnp.dot(inner, down_ref[...], preferred_element_type=jnp.float32)
    shared = (produced * share).astype(jnp.bfloat16)
    term = lax.dot_general(select, shared, TN, preferred_element_type=jnp.float32)
    for s in range(seq_size):
        for p in range(count):
            for r in range(requests):
                start = p * ROWS + r * steps
                out_ref[s, p, r] = term[
                    start : start + steps, s * feature : (s + 1) * feature
                ].astype(jnp.bfloat16)


def limit(mebibytes):
    return pltpu.CompilerParams(vmem_limit_bytes=mebibytes * 1024 * 1024)


def stage(count, *refs):
    sources, copies, sems = refs[1 : 1 + count], refs[1 + count : 1 + 2 * count], refs[-1]
    moves = [
        pltpu.make_async_copy(source, copy, sems.at[i])
        for i, (source, copy) in enumerate(zip(sources, copies))
    ]
    for move in moves:
        move.start()
    for move in moves:
        move.wait()


def staged(after, *arrays, result=None):
    anywhere = pl.BlockSpec(memory_space=pl.ANY)
    inputs = [pltpu.with_memory_space_constraint(x, pltpu.HBM) for x in arrays]
    shapes = [pltpu.VMEM(x.shape, x.dtype) for x in arrays]
    if result is not None:
        inputs.append(result)
        shapes.append(pltpu.HBM(result.shape, result.dtype))
    count = len(inputs)
    size = sum(2 * x.size for x in arrays)
    return pl.pallas_call(
        functools.partial(stage, count),
        out_shape=tuple(shapes),
        in_specs=[anywhere] * (1 + count),
        out_specs=(anywhere,) * count,
        scratch_shapes=[pltpu.SemaphoreType.DMA((count,))],
        compiler_params=limit(4),
        cost_estimate=pl.CostEstimate(flops=0, bytes_accessed=2 * size, transcendentals=0),
        name="stage",
    )(after, *inputs)


def body(
    hidden_in,
    new_query,
    new_key,
    new_value,
    key_cache,
    value_cache,
    lengths,
    out_weight,
    norm_gain,
    router_weight,
    expert_ids,
    gate_weight,
    up_weight,
    down_weight,
):
    requests, steps, width = hidden_in.shape
    block = key_cache.shape[1]
    seq_size = lax.axis_size("seq")
    tp_size = lax.axis_size("tp")
    feature = width // seq_size
    experts = router_weight.shape[1]
    topk = expert_ids.shape[2]
    capacity = (5 * requests * tp_size * topk + 4 * experts - 1) // (4 * experts)
    slices = seq_size * tp_size // experts
    vmem = pl.BlockSpec(memory_space=pltpu.VMEM)
    smem = pl.BlockSpec(memory_space=pltpu.SMEM)
    hbm = pl.BlockSpec(memory_space=pltpu.HBM)

    small = pltpu.VMEM((requests, steps, width), jnp.bfloat16)
    partial = pltpu.VMEM((requests, steps, width + LANES), jnp.bfloat16)
    part, fresh = pl.pallas_call(
        attend,
        out_shape=(partial, partial),
        in_specs=[hbm] * 6,
        out_specs=(vmem, vmem),
        scratch_shapes=[
            pltpu.SMEM((requests,), jnp.int32),
            small,
            small,
            small,
            pltpu.VMEM((requests, ROWS, width), jnp.bfloat16),
            pltpu.VMEM((requests, block, width), jnp.bfloat16),
            pltpu.VMEM((requests, block, width), jnp.bfloat16),
            pltpu.SemaphoreType.DMA((2, requests)),
            pltpu.SemaphoreType.DMA((4,)),
        ],
        compiler_params=limit(24),
        name="attend",
    )(
        *[
            pltpu.with_memory_space_constraint(x, pltpu.HBM)
            for x in (lengths, new_query, new_key, new_value, key_cache, value_cache)
        ]
    )

    def swapped(x, axis, size, d):
        return lax.ppermute(x, axis, [(i, i ^ d) for i in range(size)])

    out_weight, gate_weight = staged(part, out_weight, gate_weight)
    parts = [fresh, part] + [swapped(part, "seq", seq_size, d) for d in range(1, seq_size)]
    attn_out, own_residual, packed = pl.pallas_call(
        functools.partial(project, seq_size + 1),
        out_shape=(
            pltpu.VMEM((requests, steps, feature), jnp.bfloat16),
            jax.ShapeDtypeStruct((requests, steps, feature), jnp.float32),
            partial,
        ),
        in_specs=[smem] + [vmem] * (4 + seq_size),
        out_specs=(vmem, vmem, vmem),
        scratch_shapes=[
            pltpu.VMEM((ROWS, width), jnp.float32),
            pltpu.VMEM((ROWS, width), jnp.float32),
        ],
        compiler_params=limit(8),
        name="project",
    )(expert_ids.transpose(0, 2, 1), hidden_in, norm_gain.reshape(1, width), out_weight, *parts)
    up_weight, down_weight, attn_out = staged(packed, up_weight, down_weight, result=attn_out)
    near = jnp.stack(
        [packed] + [swapped(packed, "tp", tp_size, 2 * d) for d in range(1, tp_size // 2)]
    )
    near, up_weight, down_weight = lax.optimization_barrier((near, up_weight, down_weight))
    far = swapped(near, "tp", tp_size, 1)
    terms = pl.pallas_call(
        functools.partial(feed, capacity, steps, requests * steps, slices),
        out_shape=pltpu.VMEM((seq_size, tp_size, requests, steps, feature), jnp.bfloat16),
        in_specs=[vmem] * 6,
        out_specs=vmem,
        scratch_shapes=[pltpu.VMEM((tp_size * ROWS, width + LANES), jnp.bfloat16)],
        compiler_params=limit(16),
        name="feed",
    )(router_weight.T, gate_weight, up_weight, down_weight, near, far)
    terms = terms.reshape(seq_size * tp_size, requests, steps, feature)
    arrived = lax.all_to_all(terms, ("seq", "tp"), 0, 0, tiled=True)
    mixture = jnp.sum(arrived.astype(jnp.float32), axis=0)
    return (attn_out, (own_residual + mixture).astype(jnp.bfloat16))


def solution(mesh):
    return jax.shard_map(
        body,
        mesh=mesh,
        in_specs=(
            P("tp", None, None),
            P("tp", None, None),
            P("tp", None, None),
            P("tp", None, None),
            P("tp", "seq", None),
            P("tp", "seq", None),
            P("tp"),
            P(),
            P(),
            P(),
            P("tp", None, None),
            P(("seq", "tp"), None),
            P(("seq", "tp"), None),
            P(("seq", "tp"), None),
        ),
        out_specs=(P("tp", None, "seq"), P("tp", None, "seq")),
        check_vma=False,
    )
```

```python
import functools

import jax
import jax.numpy as jnp
from jax import lax
from jax.experimental import pallas as pl
from jax.experimental.pallas import tpu as pltpu
from jax.sharding import PartitionSpec as P

HEADS = 16
SHORT = 128
ROWS = 16
LANES = 128
masked_score = -1e30
norm_epsilon = 1e-06
NT = (((1,), (1,)), ((), ()))
TN = (((0,), (0,)), ((), ()))


def iota(shape, dim):
    return lax.broadcasted_iota(jnp.int32, shape, dim)


def over(x, n):
    if n & (n - 1) == 0:
        return lax.shift_right_logical(x, jnp.int32(n.bit_length() - 1))
    return x // n


def within(x, n):
    if n & (n - 1) == 0:
        return x & (n - 1)
    return x % n


def three_parts(x):
    hi = x.astype(jnp.bfloat16).astype(jnp.float32)
    mid = (x - hi).astype(jnp.bfloat16).astype(jnp.float32)
    return hi, mid, x - hi - mid


def tiled(x, times):
    return jnp.concatenate([x] * times, axis=0)


def attend(
    lens_hbm, q_hbm, nk_hbm, nv_hbm, k_hbm, v_hbm, out_ref, fresh_ref,
    lens, q_ref, nk_ref, nv_ref, query_ref, kbuf, vbuf, sems, small_sems,
):
    requests, block, width = k_hbm.shape
    steps = q_ref.shape[1]
    head = width // HEADS
    scale = head ** (-0.5)
    group = 256 // head
    chunks = width // 256
    rows = group * steps
    seq = lax.axis_index("seq")
    small = [
        pltpu.make_async_copy(src, dst, small_sems.at[i])
        for i, (src, dst) in enumerate(
            ((lens_hbm, lens), (q_hbm, q_ref), (nk_hbm, nk_ref), (nv_hbm, nv_ref))
        )
    ]
    for move in small:
        move.start()
    small[0].wait()

    def left(r):
        return lens[r] - seq * block

    def is_full(r):
        return left(r) >= block

    def is_short(r):
        return (left(r) > 0) & (left(r) < block)

    def move(which, r, count):
        src, dst = ((k_hbm, kbuf), (v_hbm, vbuf))[which]
        part = pl.ds(0, count)
        return pltpu.make_async_copy(src.at[r, part], dst.at[r, part], sems.at[which, r])

    for kind, count in ((is_short, SHORT), (is_full, block)):
        for r in range(requests):

            @pl.when(kind(r))
            def _():
                for which in range(2):
                    move(which, r, count).start()

    for move_small in small[1:]:
        move_small.wait()
    diag = over(iota((rows, 256), 0), steps) == over(iota((rows, 256), 1), head)
    diag_all = jnp.concatenate([diag] * chunks, axis=1)
    all_rows = chunks * rows

    def columns(c):
        return slice(c * 256, (c + 1) * 256)

    def against(query, keys):
        return jnp.concatenate(
            [
                lax.dot_general(
                    query[:, columns(c)], keys(c), NT, preferred_element_type=jnp.float32
                )
                for c in range(chunks)
            ],
            axis=0,
        )

    def summary(top, total):
        shape = (all_rows, LANES)
        part = over(iota(shape, 1), HEADS)
        spread = jnp.zeros(shape, jnp.float32)
        for place, value in enumerate(three_parts(top) + three_parts(total)):
            spread = jnp.where(part == place, value, spread)
        spread = jnp.where(
            within(iota(shape, 1), HEADS) == over(iota(shape, 0), steps), spread, 0.0
        )
        pick = within(iota((ROWS, all_rows), 1), steps) == iota((ROWS, all_rows), 0)
        gathered = jnp.dot(
            jnp.where(pick, 1.0, 0.0).astype(jnp.bfloat16),
            spread.astype(jnp.bfloat16),
            preferred_element_type=jnp.float32,
        )
        return gathered[:steps].astype(jnp.bfloat16)

    def own_head(mixed):
        mixed = jnp.where(diag, mixed, 0.0)
        half = mixed[: 2 * steps]
        for g in range(1, group // 2):
            half = half + mixed[2 * steps * g : 2 * steps * (g + 1)]
        return (half[:steps] + half[steps:]).astype(jnp.bfloat16)

    def largest(x):
        return jnp.max(x, axis=1, keepdims=True)

    def summed(x):
        return jnp.sum(x, axis=1, keepdims=True)

    def weighted(weight, values):
        return [
            own_head(
                jnp.dot(
                    weight[c * rows : (c + 1) * rows],
                    values(c),
                    preferred_element_type=jnp.float32,
                )
            )
            for c in range(chunks)
        ]

    for r in range(requests):
        query = jnp.where(diag_all, tiled(q_ref[r].astype(jnp.float32) * scale, group), 0.0)
        query = query.astype(jnp.bfloat16)
        query_ref[r] = query
        keys = tiled(nk_ref[r].astype(jnp.float32), group).astype(jnp.bfloat16)
        values = tiled(nv_ref[r].astype(jnp.float32), group).astype(jnp.bfloat16)
        score = against(query, lambda c: keys[:, columns(c)])
        usable = iota(score.shape, 1) <= within(iota(score.shape, 0), steps)
        score = jnp.where(usable, score, masked_score)
        top = largest(score)
        weight = jnp.where(usable, jnp.exp(score - top), 0.0)
        fresh_ref[r, :, width:] = summary(top, summed(weight))
        mixed = weighted(weight.astype(jnp.bfloat16), lambda c: values[:, columns(c)])
        for c in range(chunks):
            fresh_ref[r, :, columns(c)] = mixed[c]

    @pl.loop(0, requests)
    def _(r):
        @pl.when(left(r) <= 0)
        def _():
            shape = (steps, LANES)
            hi, mid, low = three_parts(jnp.full(shape, masked_score, jnp.float32))
            part = over(iota(shape, 1), HEADS)
            empty = jnp.where(part == 0, hi, jnp.where(part == 1, mid, low))
            out_ref[r, :, width:] = jnp.where(part < 3, empty, 0.0).astype(jnp.bfloat16)
            out_ref[r, :, :width] = jnp.zeros((steps, width), jnp.bfloat16)

    def one(r, count):
        part = pl.ds(0, count)
        move(0, r, count).wait()
        query = query_ref[r]
        score = against(query, lambda c: kbuf[r, part, columns(c)])
        if count < block:
            usable = iota(score.shape, 1) < left(r)
            score = jnp.where(usable, score, masked_score)
        top = largest(score)
        weight = jnp.exp(score - top)
        if count < block:
            weight = jnp.where(usable, weight, 0.0)
        total = summed(weight)
        weight = weight.astype(jnp.bfloat16)
        move(1, r, count).wait()
        mixed = weighted(weight, lambda c: vbuf[r, part, columns(c)])
        out_ref[r, :, width:] = summary(top, total)
        for c in range(chunks):
            out_ref[r, :, columns(c)] = mixed[c]

    for kind, count in ((is_short, SHORT), (is_full, block)):

        @pl.loop(0, requests)
        def _(r):
            @pl.when(kind(r))
            def _():
                one(r, count)


def project(count, columns, ids_ref, hidden_ref, gain_ref, weight_ref, expand_ref, *refs):
    parts = refs[:count]
    send_ref, attn_ref, res_ref = refs[count:]
    requests, steps, width = hidden_ref.shape
    tp = lax.axis_index("tp")

    def moved(x, amount):
        return pltpu.roll(x, LANES - amount, 1)

    def rows_of(ref, lanes):
        pieces = [ref[r, :, lanes].astype(jnp.float32) for r in range(requests)]
        blank = jnp.zeros((ROWS - requests * steps, pieces[0].shape[1]), jnp.float32)
        return jnp.concatenate(pieces + [blank], axis=0)

    tops, totals = [], []
    for ref in parts:
        x = rows_of(ref, slice(width, width + LANES))
        tops.append(x + moved(x, HEADS) + moved(x, 2 * HEADS))
        totals.append(moved(x, 3 * HEADS) + moved(x, 4 * HEADS) + moved(x, 5 * HEADS))
    overall = functools.reduce(jnp.maximum, tops)
    factors = [jnp.exp(top - overall) for top in tops]
    total = functools.reduce(jnp.add, [f * t for f, t in zip(factors, totals)])
    real = (iota(total.shape, 1) < HEADS) & (iota(total.shape, 0) < requests * steps)
    inverse = jnp.where(real, 1.0 / jnp.where(real, total, 1.0), 0.0)
    ratio = jnp.concatenate([jnp.where(real, f, 0.0) * inverse for f in factors], axis=0)
    hi, mid, low = three_parts(ratio)
    packed = hi + pltpu.roll(mid, HEADS, 1) + pltpu.roll(low, 2 * HEADS, 1)
    packed = packed.astype(jnp.bfloat16)[:, : 4 * HEADS]
    wide = jnp.dot(packed, expand_ref[...], preferred_element_type=jnp.float32)
    context = jnp.zeros((ROWS, width), jnp.float32)
    for b, ref in enumerate(parts):
        context = context + wide[b * ROWS : (b + 1) * ROWS] * rows_of(ref, slice(0, width))
    attention = jnp.dot(
        context.astype(jnp.bfloat16), weight_ref[...], preferred_element_type=jnp.float32
    )
    residual = rows_of(hidden_ref, slice(0, width)) + attention
    normed = (
        residual
        * lax.rsqrt(jnp.mean(residual * residual, axis=1, keepdims=True) + norm_epsilon)
        * gain_ref[...]
    )
    row = iota((ROWS, columns), 0)
    lane = iota((ROWS, columns), 1) - tp * ROWS
    extra = jnp.where((lane >= 0) & (lane < ROWS), -1.0, 0.0)
    for i in range(requests * steps):
        first, second = [
            ids_ref[i // steps, k, i % steps].astype(jnp.float32) for k in range(2)
        ]
        extra = jnp.where(lane == i, jnp.where(row == requests * steps, first, second), extra)
    tail = row >= requests * steps
    message = jnp.concatenate(
        [jnp.where(tail, extra, normed[:, :columns]), normed[:, columns:]], axis=1
    ).astype(jnp.bfloat16)
    send_ref[...] = message
    attn_ref[...] = attention
    res_ref[...] = residual


def feed(
    capacity, steps, used, slices, router_ref, gate_ref, up_ref, down_ref, near_ref, far_ref,
    out_ref, tokens,
):
    half = near_ref.shape[0]
    count = 2 * half
    width = gate_ref.shape[1]
    experts = router_ref.shape[0]
    seq_size, _, requests, _, feature = out_ref.shape
    seq = lax.axis_index("seq")
    tp = lax.axis_index("tp")
    columns = count * ROWS
    core = within(tp, 2)
    for d in range(half):
        chip = over(tp, 2) ^ d
        for ref, which in ((near_ref, core), (far_ref, 1 - core)):
            start = pl.multiple_of((2 * chip + which) * ROWS, ROWS)
            tokens[pl.ds(start, ROWS), :] = ref[d]
    ids = jnp.zeros((8, columns), jnp.float32)
    for p in range(count):
        ids = ids + tokens[p * ROWS : (p + 1) * ROWS, :columns].astype(jnp.float32)[8:]
    place = used - 8
    first = ids[place : place + 1]
    second = ids[place + 1 : place + 2]
    mine = over(seq * count + tp, slices)
    mine_f = mine.astype(jnp.float32)
    hit = jnp.where((first == mine_f) | (second == mine_f), 1.0, 0.0)
    other = jnp.where(first == mine_f, second, first)
    earlier = (iota((columns, columns), 0) < iota((columns, columns), 1)) & (
        within(iota((columns, columns), 0), steps) == within(iota((columns, columns), 1), steps)
    )
    slot = jnp.dot(
        jnp.broadcast_to(hit, (ROWS, columns)).astype(jnp.bfloat16),
        jnp.where(earlier, 1.0, 0.0).astype(jnp.bfloat16),
        preferred_element_type=jnp.float32,
    )[:1]
    rows = -(-steps * capacity // ROWS) * ROWS
    row = iota((rows, columns), 0)
    choose = (
        (hit > 0.5)
        & (slot == within(row, capacity).astype(jnp.float32))
        & (within(iota((rows, columns), 1), steps) == over(row, capacity))
    )
    select = jnp.where(choose, 1.0, 0.0)
    rival = jnp.sum(select * other, axis=1, keepdims=True)
    select = select.astype(jnp.bfloat16)
    buffer = jnp.dot(select, tokens[...], preferred_element_type=jnp.float32).astype(jnp.bfloat16)
    logits = lax.dot_general(buffer, router_ref[...], NT, preferred_element_type=jnp.float32)
    index = iota((rows, experts), 1)
    ahead = jnp.sum(jnp.where(index == mine, logits, 0.0), axis=1, keepdims=True)
    behind = jnp.sum(
        jnp.where(index.astype(jnp.float32) == rival, logits, 0.0), axis=1, keepdims=True
    )
    share = 1.0 / (1.0 + jnp.exp(behind - ahead))
    gate = lax.dot_general(buffer, gate_ref[...], NT, preferred_element_type=jnp.float32)
    upward = lax.dot_general(buffer, up_ref[...], NT, preferred_element_type=jnp.float32)
    inner = (jax.nn.gelu(gate) * upward).astype(jnp.bfloat16)
    produced = jnp.dot(inner, down_ref[...], preferred_element_type=jnp.float32)
    shared = (produced * share).astype(jnp.bfloat16)
    term = lax.dot_general(select, shared, TN, preferred_element_type=jnp.float32)
    for s in range(seq_size):
        for p in range(count):
            for r in range(requests):
                start = p * ROWS + r * steps
                out_ref[s, p, r] = term[
                    start : start + steps, s * feature : (s + 1) * feature
                ].astype(jnp.bfloat16)


def limit(mebibytes):
    return pltpu.CompilerParams(vmem_limit_bytes=mebibytes * 1024 * 1024)


def stage(count, beside, extras, *refs):
    sources, rest = refs[:count], refs[count:]
    inputs, copies = rest[:extras], rest[extras : extras + count]
    sems, others = rest[-1], rest[extras + count : -1]
    moves = [
        pltpu.make_async_copy(source, copy, sems.at[i])
        for i, (source, copy) in enumerate(zip(sources, copies))
    ]
    for move in moves:
        move.start()
    beside(inputs, others, sems.at[count])
    for move in moves:
        move.wait()


def spread_heads(inputs, others, sem):
    expand_ref = others[0]
    shape = expand_ref.shape
    head = shape[1] // HEADS
    row = iota(shape, 0)
    same = (within(row, HEADS) == over(iota(shape, 1), head)) & (row < 3 * HEADS)
    expand_ref[...] = jnp.where(same, 1.0, 0.0).astype(jnp.bfloat16)


def own_features(inputs, others, sem):
    attn_ref, res_ref = inputs
    attn_hbm, own_ref, attn_buf = others
    requests, steps, feature = own_ref.shape
    seq = lax.axis_index("seq")
    lanes = pl.ds(pl.multiple_of(seq * feature, feature), feature)
    attention, residual = attn_ref[:, lanes], res_ref[:, lanes]
    for r in range(requests):
        part = slice(r * steps, (r + 1) * steps)
        attn_buf[r] = attention[part].astype(jnp.bfloat16)
        own_ref[r] = residual[part]
    move = pltpu.make_async_copy(attn_buf, attn_hbm, sem)
    move.start()
    move.wait()


def staged(beside, arrays, extras, shapes, specs, scratch=()):
    anywhere = pl.BlockSpec(memory_space=pl.ANY)
    vmem = pl.BlockSpec(memory_space=pltpu.VMEM)
    count = len(arrays)
    size = sum(2 * x.size for x in arrays)
    return pl.pallas_call(
        functools.partial(stage, count, beside, len(extras)),
        out_shape=tuple(pltpu.VMEM(x.shape, x.dtype) for x in arrays) + tuple(shapes),
        in_specs=[anywhere] * count + [vmem] * len(extras),
        out_specs=(anywhere,) * count + tuple(specs),
        scratch_shapes=list(scratch) + [pltpu.SemaphoreType.DMA((count + 1,))],
        compiler_params=limit(4),
        cost_estimate=pl.CostEstimate(flops=0, bytes_accessed=2 * size, transcendentals=0),
        name="stage",
    )(*[pltpu.with_memory_space_constraint(x, pltpu.HBM) for x in arrays], *extras)


def body(
    hidden_in,
    new_query,
    new_key,
    new_value,
    key_cache,
    value_cache,
    lengths,
    out_weight,
    norm_gain,
    router_weight,
    expert_ids,
    gate_weight,
    up_weight,
    down_weight,
):
    requests, steps, width = hidden_in.shape
    block = key_cache.shape[1]
    seq_size = lax.axis_size("seq")
    tp_size = lax.axis_size("tp")
    feature = width // seq_size
    experts = router_weight.shape[1]
    topk = expert_ids.shape[2]
    capacity = (5 * requests * tp_size * topk + 4 * experts - 1) // (4 * experts)
    slices = seq_size * tp_size // experts
    vmem = pl.BlockSpec(memory_space=pltpu.VMEM)
    smem = pl.BlockSpec(memory_space=pltpu.SMEM)
    hbm = pl.BlockSpec(memory_space=pltpu.HBM)

    small = pltpu.VMEM((requests, steps, width), jnp.bfloat16)
    partial = pltpu.VMEM((requests, steps, width + LANES), jnp.bfloat16)
    part, fresh = pl.pallas_call(
        attend,
        out_shape=(partial, partial),
        in_specs=[hbm] * 6,
        out_specs=(vmem, vmem),
        scratch_shapes=[
            pltpu.SMEM((requests,), jnp.int32),
            small,
            small,
            small,
            pltpu.VMEM((requests, ROWS, width), jnp.bfloat16),
            pltpu.VMEM((requests, block, width), jnp.bfloat16),
            pltpu.VMEM((requests, block, width), jnp.bfloat16),
            pltpu.SemaphoreType.DMA((2, requests)),
            pltpu.SemaphoreType.DMA((4,)),
        ],
        compiler_params=limit(24),
        name="attend",
    )(
        *[
            pltpu.with_memory_space_constraint(x, pltpu.HBM)
            for x in (lengths, new_query, new_key, new_value, key_cache, value_cache)
        ]
    )

    def swapped(x, axis, size, d):
        return lax.ppermute(x, axis, [(i, i ^ d) for i in range(size)])

    out_weight, gate_weight, expand = staged(
        spread_heads,
        (out_weight, gate_weight),
        (part,),
        (pltpu.VMEM((4 * HEADS, width), jnp.bfloat16),),
        (vmem,),
    )
    parts = [fresh, part] + [swapped(part, "seq", seq_size, d) for d in range(1, seq_size)]
    row_sums = pltpu.VMEM((ROWS, width), jnp.float32)
    packed, attention, residual = pl.pallas_call(
        functools.partial(project, seq_size + 1, tp_size * ROWS),
        out_shape=(pltpu.VMEM((ROWS, width), jnp.bfloat16), row_sums, row_sums),
        in_specs=[smem] + [vmem] * (5 + seq_size),
        out_specs=(vmem, vmem, vmem),
        compiler_params=limit(8),
        name="project",
    )(
        expert_ids.transpose(0, 2, 1),
        hidden_in,
        norm_gain.reshape(1, width),
        out_weight,
        expand,
        *parts,
    )
    own = (requests, steps, feature)
    up_weight, down_weight, attn_out, own_residual = staged(
        own_features,
        (up_weight, down_weight),
        (attention, residual),
        (pltpu.HBM(own, jnp.bfloat16), pltpu.VMEM(own, jnp.float32)),
        (pl.BlockSpec(memory_space=pl.ANY), vmem),
        (pltpu.VMEM(own, jnp.bfloat16),),
    )
    near = jnp.stack(
        [packed] + [swapped(packed, "tp", tp_size, 2 * d) for d in range(1, tp_size // 2)]
    )
    near, up_weight, down_weight = lax.optimization_barrier((near, up_weight, down_weight))
    far = swapped(near, "tp", tp_size, 1)
    terms = pl.pallas_call(
        functools.partial(feed, capacity, steps, requests * steps, slices),
        out_shape=pltpu.VMEM((seq_size, tp_size, requests, steps, feature), jnp.bfloat16),
        in_specs=[vmem] * 6,
        out_specs=vmem,
        scratch_shapes=[pltpu.VMEM((tp_size * ROWS, width), jnp.bfloat16)],
        compiler_params=limit(16),
        name="feed",
    )(router_weight.T, gate_weight, up_weight, down_weight, near, far)
    terms = terms.reshape(seq_size * tp_size, requests, steps, feature)
    arrived = lax.all_to_all(terms, ("seq", "tp"), 0, 0, tiled=True)
    mixture = jnp.sum(arrived.astype(jnp.float32), axis=0)
    return (attn_out, (own_residual + mixture).astype(jnp.bfloat16))


def solution(mesh):
    return jax.shard_map(
        body,
        mesh=mesh,
        in_specs=(
            P("tp", None, None),
            P("tp", None, None),
            P("tp", None, None),
            P("tp", None, None),
            P("tp", "seq", None),
            P("tp", "seq", None),
            P("tp"),
            P(),
            P(),
            P(),
            P("tp", None, None),
            P(("seq", "tp"), None),
            P(("seq", "tp"), None),
            P(("seq", "tp"), None),
        ),
        out_specs=(P("tp", None, "seq"), P("tp", None, "seq")),
        check_vma=False,
    )
```

```python
import functools

import jax
import jax.numpy as jnp
from jax import lax
from jax.experimental import pallas as pl
from jax.experimental.pallas import tpu as pltpu
from jax.sharding import PartitionSpec as P

HEADS = 16
SHORT = 128
ROWS = 16
LANES = 128
masked_score = -1e30
norm_epsilon = 1e-06
NT = (((1,), (1,)), ((), ()))
TN = (((0,), (0,)), ((), ()))


def iota(shape, dim):
    return lax.broadcasted_iota(jnp.int32, shape, dim)


def over(x, n):
    if n & (n - 1) == 0:
        return lax.shift_right_logical(x, jnp.int32(n.bit_length() - 1))
    return x // n


def within(x, n):
    if n & (n - 1) == 0:
        return x & (n - 1)
    return x % n


def three_parts(x):
    hi = x.astype(jnp.bfloat16).astype(jnp.float32)
    mid = (x - hi).astype(jnp.bfloat16).astype(jnp.float32)
    return hi, mid, x - hi - mid


def tiled(x, times):
    return jnp.concatenate([x] * times, axis=0)


def attend(
    lens_hbm, q_hbm, nk_hbm, nv_hbm, k_hbm, v_hbm, out_ref, fresh_ref,
    lens, q_ref, nk_ref, nv_ref, query_ref, kbuf, vbuf, sems, small_sems,
):
    requests, block, width = k_hbm.shape
    steps = q_ref.shape[1]
    head = width // HEADS
    scale = head ** (-0.5)
    group = 256 // head
    chunks = width // 256
    rows = group * steps
    seq = lax.axis_index("seq")
    small = [
        pltpu.make_async_copy(src, dst, small_sems.at[i])
        for i, (src, dst) in enumerate(
            ((lens_hbm, lens), (q_hbm, q_ref), (nk_hbm, nk_ref), (nv_hbm, nv_ref))
        )
    ]
    for move in small:
        move.start()
    small[0].wait()

    def left(r):
        return lens[r] - seq * block

    def is_full(r):
        return left(r) >= block

    def is_short(r):
        return (left(r) > 0) & (left(r) < block)

    def move(which, r, count):
        src, dst = ((k_hbm, kbuf), (v_hbm, vbuf))[which]
        part = pl.ds(0, count)
        return pltpu.make_async_copy(src.at[r, part], dst.at[r, part], sems.at[which, r])

    for kind, count in ((is_short, SHORT), (is_full, block)):
        for r in range(requests):

            @pl.when(kind(r))
            def _():
                for which in range(2):
                    move(which, r, count).start()

    for move_small in small[1:]:
        move_small.wait()
    diag = over(iota((rows, 256), 0), steps) == over(iota((rows, 256), 1), head)
    diag_all = jnp.concatenate([diag] * chunks, axis=1)
    all_rows = chunks * rows

    def columns(c):
        return slice(c * 256, (c + 1) * 256)

    def against(query, keys):
        return jnp.concatenate(
            [
                lax.dot_general(
                    query[:, columns(c)], keys(c), NT, preferred_element_type=jnp.float32
                )
                for c in range(chunks)
            ],
            axis=0,
        )

    def summary(top, total):
        shape = (all_rows, LANES)
        part = over(iota(shape, 1), HEADS)
        spread = jnp.zeros(shape, jnp.float32)
        for place, value in enumerate(three_parts(top) + three_parts(total)):
            spread = jnp.where(part == place, value, spread)
        spread = jnp.where(
            within(iota(shape, 1), HEADS) == over(iota(shape, 0), steps), spread, 0.0
        )
        pick = within(iota((ROWS, all_rows), 1), steps) == iota((ROWS, all_rows), 0)
        gathered = jnp.dot(
            jnp.where(pick, 1.0, 0.0).astype(jnp.bfloat16),
            spread.astype(jnp.bfloat16),
            preferred_element_type=jnp.float32,
        )
        return gathered[:steps].astype(jnp.bfloat16)

    def own_head(mixed):
        mixed = jnp.where(diag, mixed, 0.0)
        half = mixed[: 2 * steps]
        for g in range(1, group // 2):
            half = half + mixed[2 * steps * g : 2 * steps * (g + 1)]
        return (half[:steps] + half[steps:]).astype(jnp.bfloat16)

    def largest(x):
        return jnp.max(x, axis=1, keepdims=True)

    def summed(x):
        return jnp.sum(x, axis=1, keepdims=True)

    def weighted(weight, values):
        return [
            own_head(
                jnp.dot(
                    weight[c * rows : (c + 1) * rows],
                    values(c),
                    preferred_element_type=jnp.float32,
                )
            )
            for c in range(chunks)
        ]

    for r in range(requests):
        query = jnp.where(diag_all, tiled(q_ref[r].astype(jnp.float32) * scale, group), 0.0)
        query = query.astype(jnp.bfloat16)
        query_ref[r] = query
        keys = tiled(nk_ref[r].astype(jnp.float32), group).astype(jnp.bfloat16)
        values = tiled(nv_ref[r].astype(jnp.float32), group).astype(jnp.bfloat16)
        score = against(query, lambda c: keys[:, columns(c)])
        usable = iota(score.shape, 1) <= within(iota(score.shape, 0), steps)
        score = jnp.where(usable, score, masked_score)
        top = largest(score)
        weight = jnp.where(usable, jnp.exp(score - top), 0.0)
        fresh_ref[r, :, width:] = summary(top, summed(weight))
        mixed = weighted(weight.astype(jnp.bfloat16), lambda c: values[:, columns(c)])
        for c in range(chunks):
            fresh_ref[r, :, columns(c)] = mixed[c]

    @pl.loop(0, requests)
    def _(r):
        @pl.when(left(r) <= 0)
        def _():
            shape = (steps, LANES)
            hi, mid, low = three_parts(jnp.full(shape, masked_score, jnp.float32))
            part = over(iota(shape, 1), HEADS)
            empty = jnp.where(part == 0, hi, jnp.where(part == 1, mid, low))
            out_ref[r, :, width:] = jnp.where(part < 3, empty, 0.0).astype(jnp.bfloat16)
            out_ref[r, :, :width] = jnp.zeros((steps, width), jnp.bfloat16)

    def one(r, count):
        part = pl.ds(0, count)
        move(0, r, count).wait()
        query = query_ref[r]
        score = against(query, lambda c: kbuf[r, part, columns(c)])
        if count < block:
            usable = iota(score.shape, 1) < left(r)
            score = jnp.where(usable, score, masked_score)
        top = largest(score)
        weight = jnp.exp(score - top)
        if count < block:
            weight = jnp.where(usable, weight, 0.0)
        total = summed(weight)
        weight = weight.astype(jnp.bfloat16)
        move(1, r, count).wait()
        mixed = weighted(weight, lambda c: vbuf[r, part, columns(c)])
        out_ref[r, :, width:] = summary(top, total)
        for c in range(chunks):
            out_ref[r, :, columns(c)] = mixed[c]

    for kind, count in ((is_short, SHORT), (is_full, block)):

        @pl.loop(0, requests)
        def _(r):
            @pl.when(kind(r))
            def _():
                one(r, count)


def project(count, extra_ref, hidden_ref, gain_ref, weight_ref, expand_ref, *refs):
    parts = refs[:count]
    send_ref, attn_ref, res_ref = refs[count:]
    requests, steps, width = hidden_ref.shape

    def moved(x, amount):
        return pltpu.roll(x, LANES - amount, 1)

    def rows_of(ref, lanes):
        pieces = [ref[r, :, lanes].astype(jnp.float32) for r in range(requests)]
        blank = jnp.zeros((ROWS - requests * steps, pieces[0].shape[1]), jnp.float32)
        return jnp.concatenate(pieces + [blank], axis=0)

    tops, totals = [], []
    for ref in parts:
        x = rows_of(ref, slice(width, width + LANES))
        tops.append(x + moved(x, HEADS) + moved(x, 2 * HEADS))
        totals.append(moved(x, 3 * HEADS) + moved(x, 4 * HEADS) + moved(x, 5 * HEADS))
    overall = functools.reduce(jnp.maximum, tops)
    factors = [jnp.exp(top - overall) for top in tops]
    total = functools.reduce(jnp.add, [f * t for f, t in zip(factors, totals)])
    real = (iota(total.shape, 1) < HEADS) & (iota(total.shape, 0) < requests * steps)
    inverse = jnp.where(real, 1.0 / jnp.where(real, total, 1.0), 0.0)
    ratio = jnp.concatenate([jnp.where(real, f, 0.0) * inverse for f in factors], axis=0)
    hi, mid, low = three_parts(ratio)
    packed = hi + pltpu.roll(mid, HEADS, 1) + pltpu.roll(low, 2 * HEADS, 1)
    packed = packed.astype(jnp.bfloat16)[:, : 4 * HEADS]
    wide = jnp.dot(packed, expand_ref[...], preferred_element_type=jnp.float32)
    context = jnp.zeros((ROWS, width), jnp.float32)
    for b, ref in enumerate(parts):
        context = context + wide[b * ROWS : (b + 1) * ROWS] * rows_of(ref, slice(0, width))
    attention = jnp.dot(
        context.astype(jnp.bfloat16), weight_ref[...], preferred_element_type=jnp.float32
    )
    residual = rows_of(hidden_ref, slice(0, width)) + attention
    normed = (
        residual
        * lax.rsqrt(jnp.mean(residual * residual, axis=1, keepdims=True) + norm_epsilon)
        * gain_ref[...]
    )
    columns = extra_ref.shape[1]
    row = iota((ROWS, columns), 0)
    tail = row >= requests * steps
    message = jnp.concatenate(
        [jnp.where(tail, extra_ref[...], normed[:, :columns]), normed[:, columns:]], axis=1
    ).astype(jnp.bfloat16)
    send_ref[...] = message
    attn_ref[...] = attention
    res_ref[...] = residual


def feed(
    capacity, steps, used, slices, router_ref, gate_ref, up_ref, down_ref, near_ref, far_ref,
    out_ref, tokens,
):
    half = near_ref.shape[0]
    count = 2 * half
    width = gate_ref.shape[1]
    experts = router_ref.shape[0]
    seq_size, _, requests, _, feature = out_ref.shape
    seq = lax.axis_index("seq")
    tp = lax.axis_index("tp")
    columns = count * ROWS
    core = within(tp, 2)
    for d in range(half):
        chip = over(tp, 2) ^ d
        for ref, which in ((near_ref, core), (far_ref, 1 - core)):
            start = pl.multiple_of((2 * chip + which) * ROWS, ROWS)
            tokens[pl.ds(start, ROWS), :] = ref[d]
    ids = jnp.zeros((8, columns), jnp.float32)
    for p in range(count):
        ids = ids + tokens[p * ROWS : (p + 1) * ROWS, :columns].astype(jnp.float32)[8:]
    place = used - 8
    first = ids[place : place + 1]
    second = ids[place + 1 : place + 2]
    mine = over(seq * count + tp, slices)
    mine_f = mine.astype(jnp.float32)
    hit = jnp.where((first == mine_f) | (second == mine_f), 1.0, 0.0)
    other = jnp.where(first == mine_f, second, first)
    earlier = (iota((columns, columns), 0) < iota((columns, columns), 1)) & (
        within(iota((columns, columns), 0), steps) == within(iota((columns, columns), 1), steps)
    )
    slot = jnp.dot(
        jnp.broadcast_to(hit, (ROWS, columns)).astype(jnp.bfloat16),
        jnp.where(earlier, 1.0, 0.0).astype(jnp.bfloat16),
        preferred_element_type=jnp.float32,
    )[:1]
    rows = -(-steps * capacity // ROWS) * ROWS
    row = iota((rows, columns), 0)
    choose = (
        (hit > 0.5)
        & (slot == within(row, capacity).astype(jnp.float32))
        & (within(iota((rows, columns), 1), steps) == over(row, capacity))
    )
    select = jnp.where(choose, 1.0, 0.0)
    rival = jnp.sum(select * other, axis=1, keepdims=True)
    select = select.astype(jnp.bfloat16)
    buffer = jnp.dot(select, tokens[...], preferred_element_type=jnp.float32).astype(jnp.bfloat16)
    logits = lax.dot_general(buffer, router_ref[...], NT, preferred_element_type=jnp.float32)
    index = iota((rows, experts), 1)
    ahead = jnp.sum(jnp.where(index == mine, logits, 0.0), axis=1, keepdims=True)
    behind = jnp.sum(
        jnp.where(index.astype(jnp.float32) == rival, logits, 0.0), axis=1, keepdims=True
    )
    share = 1.0 / (1.0 + jnp.exp(behind - ahead))
    gate = lax.dot_general(buffer, gate_ref[...], NT, preferred_element_type=jnp.float32)
    upward = lax.dot_general(buffer, up_ref[...], NT, preferred_element_type=jnp.float32)
    inner = (jax.nn.gelu(gate) * upward).astype(jnp.bfloat16)
    produced = jnp.dot(inner, down_ref[...], preferred_element_type=jnp.float32)
    shared = (produced * share).astype(jnp.bfloat16)
    term = lax.dot_general(select, shared, TN, preferred_element_type=jnp.float32)
    for s in range(seq_size):
        for p in range(count):
            for r in range(requests):
                start = p * ROWS + r * steps
                out_ref[s, p, r] = term[
                    start : start + steps, s * feature : (s + 1) * feature
                ].astype(jnp.bfloat16)


def limit(mebibytes):
    return pltpu.CompilerParams(vmem_limit_bytes=mebibytes * 1024 * 1024)


def stage(count, beside, extras, *refs):
    sources, rest = refs[:count], refs[count:]
    inputs, copies = rest[:extras], rest[extras : extras + count]
    sems, others = rest[-1], rest[extras + count : -1]
    moves = [
        pltpu.make_async_copy(source, copy, sems.at[i])
        for i, (source, copy) in enumerate(zip(sources, copies))
    ]
    for move in moves:
        move.start()
    beside(inputs, others, sems.at[count])
    for move in moves:
        move.wait()


def spread_constants(inputs, others, sem):
    ids_ref = inputs[1]
    expand_ref, extra_ref = others
    requests, _, steps = ids_ref.shape
    columns = extra_ref.shape[1]
    tp = lax.axis_index("tp")
    row = iota((ROWS, columns), 0)
    lane = iota((ROWS, columns), 1) - tp * ROWS
    extra = jnp.where((lane >= 0) & (lane < ROWS), -1.0, 0.0)
    for i in range(requests * steps):
        first, second = [
            ids_ref[i // steps, k, i % steps].astype(jnp.float32) for k in range(2)
        ]
        extra = jnp.where(lane == i, jnp.where(row == requests * steps, first, second), extra)
    extra_ref[...] = extra
    shape = expand_ref.shape
    head = shape[1] // HEADS
    group = iota(shape, 0)
    same = (within(group, HEADS) == over(iota(shape, 1), head)) & (group < 3 * HEADS)
    expand_ref[...] = jnp.where(same, 1.0, 0.0).astype(jnp.bfloat16)


def own_features(inputs, others, sem):
    attn_ref, res_ref = inputs
    attn_hbm, own_ref, attn_buf = others
    requests, steps, feature = own_ref.shape
    seq = lax.axis_index("seq")
    lanes = pl.ds(pl.multiple_of(seq * feature, feature), feature)
    attention, residual = attn_ref[:, lanes], res_ref[:, lanes]
    for r in range(requests):
        part = slice(r * steps, (r + 1) * steps)
        attn_buf[r] = attention[part].astype(jnp.bfloat16)
        own_ref[r] = residual[part]
    move = pltpu.make_async_copy(attn_buf, attn_hbm, sem)
    move.start()
    move.wait()


def staged(beside, arrays, extras, shapes, specs, scratch=()):
    anywhere = pl.BlockSpec(memory_space=pl.ANY)
    count = len(arrays)
    size = sum(2 * x.size for x in arrays)
    return pl.pallas_call(
        functools.partial(stage, count, beside, len(extras)),
        out_shape=tuple(pltpu.VMEM(x.shape, x.dtype) for x in arrays) + tuple(shapes),
        in_specs=[anywhere] * count + [spec for _, spec in extras],
        out_specs=(anywhere,) * count + tuple(specs),
        scratch_shapes=list(scratch) + [pltpu.SemaphoreType.DMA((count + 1,))],
        compiler_params=limit(4),
        cost_estimate=pl.CostEstimate(flops=0, bytes_accessed=2 * size, transcendentals=0),
        name="stage",
    )(*[pltpu.with_memory_space_constraint(x, pltpu.HBM) for x in arrays], *[x for x, _ in extras])


def body(
    hidden_in,
    new_query,
    new_key,
    new_value,
    key_cache,
    value_cache,
    lengths,
    out_weight,
    norm_gain,
    router_weight,
    expert_ids,
    gate_weight,
    up_weight,
    down_weight,
):
    requests, steps, width = hidden_in.shape
    block = key_cache.shape[1]
    seq_size = lax.axis_size("seq")
    tp_size = lax.axis_size("tp")
    feature = width // seq_size
    experts = router_weight.shape[1]
    topk = expert_ids.shape[2]
    capacity = (5 * requests * tp_size * topk + 4 * experts - 1) // (4 * experts)
    slices = seq_size * tp_size // experts
    vmem = pl.BlockSpec(memory_space=pltpu.VMEM)
    smem = pl.BlockSpec(memory_space=pltpu.SMEM)
    hbm = pl.BlockSpec(memory_space=pltpu.HBM)

    small = pltpu.VMEM((requests, steps, width), jnp.bfloat16)
    partial = pltpu.VMEM((requests, steps, width + LANES), jnp.bfloat16)
    part, fresh = pl.pallas_call(
        attend,
        out_shape=(partial, partial),
        in_specs=[hbm] * 6,
        out_specs=(vmem, vmem),
        scratch_shapes=[
            pltpu.SMEM((requests,), jnp.int32),
            small,
            small,
            small,
            pltpu.VMEM((requests, ROWS, width), jnp.bfloat16),
            pltpu.VMEM((requests, block, width), jnp.bfloat16),
            pltpu.VMEM((requests, block, width), jnp.bfloat16),
            pltpu.SemaphoreType.DMA((2, requests)),
            pltpu.SemaphoreType.DMA((4,)),
        ],
        compiler_params=limit(24),
        name="attend",
    )(
        *[
            pltpu.with_memory_space_constraint(x, pltpu.HBM)
            for x in (lengths, new_query, new_key, new_value, key_cache, value_cache)
        ]
    )

    def swapped(x, axis, size, d):
        return lax.ppermute(x, axis, [(i, i ^ d) for i in range(size)])

    out_weight, gate_weight, expand, extra = staged(
        spread_constants,
        (out_weight, gate_weight),
        ((part, vmem), (expert_ids.transpose(0, 2, 1), smem)),
        (
            pltpu.VMEM((4 * HEADS, width), jnp.bfloat16),
            pltpu.VMEM((ROWS, tp_size * ROWS), jnp.float32),
        ),
        (vmem, vmem),
    )
    parts = [fresh, part] + [swapped(part, "seq", seq_size, d) for d in range(1, seq_size)]
    row_sums = pltpu.VMEM((ROWS, width), jnp.float32)
    packed, attention, residual = pl.pallas_call(
        functools.partial(project, seq_size + 1),
        out_shape=(pltpu.VMEM((ROWS, width), jnp.bfloat16), row_sums, row_sums),
        in_specs=[vmem] * (6 + seq_size),
        out_specs=(vmem, vmem, vmem),
        compiler_params=limit(8),
        name="project",
    )(
        extra,
        hidden_in,
        norm_gain.reshape(1, width),
        out_weight,
        expand,
        *parts,
    )
    own = (requests, steps, feature)
    up_weight, down_weight, attn_out, own_residual = staged(
        own_features,
        (up_weight, down_weight),
        ((attention, vmem), (residual, vmem)),
        (pltpu.HBM(own, jnp.bfloat16), pltpu.VMEM(own, jnp.float32)),
        (pl.BlockSpec(memory_space=pl.ANY), vmem),
        (pltpu.VMEM(own, jnp.bfloat16),),
    )
    near = jnp.stack(
        [packed] + [swapped(packed, "tp", tp_size, 2 * d) for d in range(1, tp_size // 2)]
    )
    near, up_weight, down_weight = lax.optimization_barrier((near, up_weight, down_weight))
    far = swapped(near, "tp", tp_size, 1)
    terms = pl.pallas_call(
        functools.partial(feed, capacity, steps, requests * steps, slices),
        out_shape=pltpu.VMEM((seq_size, tp_size, requests, steps, feature), jnp.bfloat16),
        in_specs=[vmem] * 6,
        out_specs=vmem,
        scratch_shapes=[pltpu.VMEM((tp_size * ROWS, width), jnp.bfloat16)],
        compiler_params=limit(16),
        name="feed",
    )(router_weight.T, gate_weight, up_weight, down_weight, near, far)
    terms = terms.reshape(seq_size * tp_size, requests, steps, feature)
    arrived = lax.all_to_all(terms, ("seq", "tp"), 0, 0, tiled=True)
    mixture = jnp.sum(arrived.astype(jnp.float32), axis=0)
    return (attn_out, (own_residual + mixture).astype(jnp.bfloat16))


def solution(mesh):
    return jax.shard_map(
        body,
        mesh=mesh,
        in_specs=(
            P("tp", None, None),
            P("tp", None, None),
            P("tp", None, None),
            P("tp", None, None),
            P("tp", "seq", None),
            P("tp", "seq", None),
            P("tp"),
            P(),
            P(),
            P(),
            P("tp", None, None),
            P(("seq", "tp"), None),
            P(("seq", "tp"), None),
            P(("seq", "tp"), None),
        ),
        out_specs=(P("tp", None, "seq"), P("tp", None, "seq")),
        check_vma=False,
    )
```

```python
import functools

import jax
import jax.numpy as jnp
from jax import lax
from jax.experimental import pallas as pl
from jax.experimental.pallas import tpu as pltpu
from jax.sharding import PartitionSpec as P

HEADS = 16
SHORT = 128
ROWS = 16
LANES = 128
masked_score = -1e30
norm_epsilon = 1e-06
NT = (((1,), (1,)), ((), ()))
TN = (((0,), (0,)), ((), ()))


def iota(shape, dim):
    return lax.broadcasted_iota(jnp.int32, shape, dim)


def over(x, n):
    if n & (n - 1) == 0:
        return lax.shift_right_logical(x, jnp.int32(n.bit_length() - 1))
    return x // n


def within(x, n):
    if n & (n - 1) == 0:
        return x & (n - 1)
    return x % n


def three_parts(x):
    hi = x.astype(jnp.bfloat16).astype(jnp.float32)
    mid = (x - hi).astype(jnp.bfloat16).astype(jnp.float32)
    return hi, mid, x - hi - mid


def tiled(x, times):
    return jnp.concatenate([x] * times, axis=0)


def attend(
    lens_hbm, q_hbm, nk_hbm, nv_hbm, k_hbm, v_hbm, out_ref, fresh_ref,
    lens, q_ref, nk_ref, nv_ref, query_ref, kbuf, vbuf, sems, small_sems,
):
    requests, block, width = k_hbm.shape
    steps = q_ref.shape[1]
    head = width // HEADS
    scale = head ** (-0.5)
    group = 256 // head
    chunks = width // 256
    rows = group * steps
    seq = lax.axis_index("seq")
    small = [
        pltpu.make_async_copy(src, dst, small_sems.at[i])
        for i, (src, dst) in enumerate(
            ((lens_hbm, lens), (q_hbm, q_ref), (nk_hbm, nk_ref), (nv_hbm, nv_ref))
        )
    ]
    for move in small:
        move.start()
    small[0].wait()

    def left(r):
        return lens[r] - seq * block

    def is_full(r):
        return left(r) >= block

    def is_short(r):
        return (left(r) > 0) & (left(r) < block)

    def move(which, r, count):
        src, dst = ((k_hbm, kbuf), (v_hbm, vbuf))[which]
        part = pl.ds(0, count)
        return pltpu.make_async_copy(src.at[r, part], dst.at[r, part], sems.at[which, r])

    for kind, count in ((is_short, SHORT), (is_full, block)):
        for r in range(requests):

            @pl.when(kind(r))
            def _():
                for which in range(2):
                    move(which, r, count).start()

    for move_small in small[1:]:
        move_small.wait()
    diag = over(iota((rows, 256), 0), steps) == over(iota((rows, 256), 1), head)
    diag_all = jnp.concatenate([diag] * chunks, axis=1)
    all_rows = chunks * rows

    def columns(c):
        return slice(c * 256, (c + 1) * 256)

    def against(query, keys):
        return jnp.concatenate(
            [
                lax.dot_general(
                    query[:, columns(c)], keys(c), NT, preferred_element_type=jnp.float32
                )
                for c in range(chunks)
            ],
            axis=0,
        )

    def summary(top, total):
        shape = (all_rows, LANES)
        part = over(iota(shape, 1), HEADS)
        spread = jnp.zeros(shape, jnp.float32)
        for place, value in enumerate(three_parts(top) + three_parts(total)):
            spread = jnp.where(part == place, value, spread)
        spread = jnp.where(
            within(iota(shape, 1), HEADS) == over(iota(shape, 0), steps), spread, 0.0
        )
        pick = within(iota((ROWS, all_rows), 1), steps) == iota((ROWS, all_rows), 0)
        gathered = jnp.dot(
            jnp.where(pick, 1.0, 0.0).astype(jnp.bfloat16),
            spread.astype(jnp.bfloat16),
            preferred_element_type=jnp.float32,
        )
        return gathered[:steps].astype(jnp.bfloat16)

    def own_head(mixed):
        mixed = jnp.where(diag, mixed, 0.0)
        half = mixed[: 2 * steps]
        for g in range(1, group // 2):
            half = half + mixed[2 * steps * g : 2 * steps * (g + 1)]
        return (half[:steps] + half[steps:]).astype(jnp.bfloat16)

    def largest(x):
        return jnp.max(x, axis=1, keepdims=True)

    def summed(x):
        return jnp.sum(x, axis=1, keepdims=True)

    def weighted(weight, values):
        return [
            own_head(
                jnp.dot(
                    weight[c * rows : (c + 1) * rows],
                    values(c),
                    preferred_element_type=jnp.float32,
                )
            )
            for c in range(chunks)
        ]

    for r in range(requests):
        query = jnp.where(diag_all, tiled(q_ref[r].astype(jnp.float32) * scale, group), 0.0)
        query = query.astype(jnp.bfloat16)
        query_ref[r] = query
        keys = tiled(nk_ref[r].astype(jnp.float32), group).astype(jnp.bfloat16)
        values = tiled(nv_ref[r].astype(jnp.float32), group).astype(jnp.bfloat16)
        score = against(query, lambda c: keys[:, columns(c)])
        usable = iota(score.shape, 1) <= within(iota(score.shape, 0), steps)
        score = jnp.where(usable, score, masked_score)
        top = largest(score)
        weight = jnp.where(usable, jnp.exp(score - top), 0.0)
        fresh_ref[r, :, width:] = summary(top, summed(weight))
        mixed = weighted(weight.astype(jnp.bfloat16), lambda c: values[:, columns(c)])
        for c in range(chunks):
            fresh_ref[r, :, columns(c)] = mixed[c]

    @pl.loop(0, requests)
    def _(r):
        @pl.when(left(r) <= 0)
        def _():
            shape = (steps, LANES)
            hi, mid, low = three_parts(jnp.full(shape, masked_score, jnp.float32))
            part = over(iota(shape, 1), HEADS)
            empty = jnp.where(part == 0, hi, jnp.where(part == 1, mid, low))
            out_ref[r, :, width:] = jnp.where(part < 3, empty, 0.0).astype(jnp.bfloat16)
            out_ref[r, :, :width] = jnp.zeros((steps, width), jnp.bfloat16)

    def one(r, count):
        part = pl.ds(0, count)
        move(0, r, count).wait()
        query = query_ref[r]
        score = against(query, lambda c: kbuf[r, part, columns(c)])
        if count < block:
            usable = iota(score.shape, 1) < left(r)
            score = jnp.where(usable, score, masked_score)
        top = largest(score)
        weight = jnp.exp(score - top)
        if count < block:
            weight = jnp.where(usable, weight, 0.0)
        total = summed(weight)
        weight = weight.astype(jnp.bfloat16)
        move(1, r, count).wait()
        mixed = weighted(weight, lambda c: vbuf[r, part, columns(c)])
        out_ref[r, :, width:] = summary(top, total)
        for c in range(chunks):
            out_ref[r, :, columns(c)] = mixed[c]

    for kind, count in ((is_short, SHORT), (is_full, block)):

        @pl.loop(0, requests)
        def _(r):
            @pl.when(kind(r))
            def _():
                one(r, count)


def project(count, extra_ref, hidden_ref, gain_ref, weight_ref, expand_ref, *refs):
    parts = refs[:count]
    send_ref, attn_ref, res_ref = refs[count:]
    requests, steps, width = hidden_ref.shape

    def moved(x, amount):
        return pltpu.roll(x, LANES - amount, 1)

    def rows_of(ref, lanes):
        pieces = [ref[r, :, lanes].astype(jnp.float32) for r in range(requests)]
        blank = jnp.zeros((ROWS - requests * steps, pieces[0].shape[1]), jnp.float32)
        return jnp.concatenate(pieces + [blank], axis=0)

    tops, totals = [], []
    for ref in parts:
        x = rows_of(ref, slice(width, width + LANES))
        tops.append(x + moved(x, HEADS) + moved(x, 2 * HEADS))
        totals.append(moved(x, 3 * HEADS) + moved(x, 4 * HEADS) + moved(x, 5 * HEADS))
    overall = functools.reduce(jnp.maximum, tops)
    factors = [jnp.exp(top - overall) for top in tops]
    total = functools.reduce(jnp.add, [f * t for f, t in zip(factors, totals)])
    real = (iota(total.shape, 1) < HEADS) & (iota(total.shape, 0) < requests * steps)
    inverse = jnp.where(real, 1.0 / jnp.where(real, total, 1.0), 0.0)
    ratio = jnp.concatenate([jnp.where(real, f, 0.0) * inverse for f in factors], axis=0)
    hi, mid, low = three_parts(ratio)
    packed = hi + pltpu.roll(mid, HEADS, 1) + pltpu.roll(low, 2 * HEADS, 1)
    packed = packed.astype(jnp.bfloat16)[:, : 4 * HEADS]
    wide = jnp.dot(packed, expand_ref[...], preferred_element_type=jnp.float32)
    context = jnp.zeros((ROWS, width), jnp.float32)
    for b, ref in enumerate(parts):
        context = context + wide[b * ROWS : (b + 1) * ROWS] * rows_of(ref, slice(0, width))
    attention = jnp.dot(
        context.astype(jnp.bfloat16), weight_ref[...], preferred_element_type=jnp.float32
    )
    residual = rows_of(hidden_ref, slice(0, width)) + attention
    normed = (
        residual
        * lax.rsqrt(jnp.mean(residual * residual, axis=1, keepdims=True) + norm_epsilon)
        * gain_ref[...]
    )
    columns = extra_ref.shape[1]
    row = iota((ROWS, columns), 0)
    tail = row >= requests * steps
    message = jnp.concatenate(
        [jnp.where(tail, extra_ref[...], normed[:, :columns]), normed[:, columns:]], axis=1
    ).astype(jnp.bfloat16)
    send_ref[...] = message
    attn_ref[...] = attention
    res_ref[...] = residual


def feed(
    capacity, steps, used, slices, router_ref, gate_ref, up_ref, down_ref, near_ref, far_ref,
    out_ref, tokens,
):
    half = near_ref.shape[0]
    count = 2 * half
    width = gate_ref.shape[1]
    experts = router_ref.shape[0]
    seq_size, _, requests, _, feature = out_ref.shape
    seq = lax.axis_index("seq")
    tp = lax.axis_index("tp")
    columns = count * ROWS
    core = within(tp, 2)
    for d in range(half):
        chip = over(tp, 2) ^ d
        for ref, which in ((near_ref, core), (far_ref, 1 - core)):
            start = pl.multiple_of((2 * chip + which) * ROWS, ROWS)
            tokens[pl.ds(start, ROWS), :] = ref[d]
    ids = jnp.zeros((8, columns), jnp.float32)
    for p in range(count):
        ids = ids + tokens[p * ROWS : (p + 1) * ROWS, :columns].astype(jnp.float32)[8:]
    place = used - 8
    first = ids[place : place + 1]
    second = ids[place + 1 : place + 2]
    mine = over(seq * count + tp, slices)
    mine_f = mine.astype(jnp.float32)
    hit = jnp.where((first == mine_f) | (second == mine_f), 1.0, 0.0)
    other = jnp.where(first == mine_f, second, first)
    earlier = (iota((columns, columns), 0) < iota((columns, columns), 1)) & (
        within(iota((columns, columns), 0), steps) == within(iota((columns, columns), 1), steps)
    )
    slot = jnp.dot(
        jnp.broadcast_to(hit, (ROWS, columns)).astype(jnp.bfloat16),
        jnp.where(earlier, 1.0, 0.0).astype(jnp.bfloat16),
        preferred_element_type=jnp.float32,
    )[:1]
    rows = -(-steps * capacity // ROWS) * ROWS
    row = iota((rows, columns), 0)
    choose = (
        (hit > 0.5)
        & (slot == within(row, capacity).astype(jnp.float32))
        & (within(iota((rows, columns), 1), steps) == over(row, capacity))
    )
    select = jnp.where(choose, 1.0, 0.0)
    rival = jnp.sum(select * other, axis=1, keepdims=True)
    select = select.astype(jnp.bfloat16)
    buffer = jnp.dot(select, tokens[...], preferred_element_type=jnp.float32).astype(jnp.bfloat16)
    logits = lax.dot_general(buffer, router_ref[...], NT, preferred_element_type=jnp.float32)
    index = iota((rows, experts), 1)
    ahead = jnp.sum(jnp.where(index == mine, logits, 0.0), axis=1, keepdims=True)
    behind = jnp.sum(
        jnp.where(index.astype(jnp.float32) == rival, logits, 0.0), axis=1, keepdims=True
    )
    share = 1.0 / (1.0 + jnp.exp(behind - ahead))
    gate = lax.dot_general(buffer, gate_ref[...], NT, preferred_element_type=jnp.float32)
    upward = lax.dot_general(buffer, up_ref[...], NT, preferred_element_type=jnp.float32)
    inner = (jax.nn.gelu(gate) * upward).astype(jnp.bfloat16)
    produced = jnp.dot(inner, down_ref[...], preferred_element_type=jnp.float32)
    shared = (produced * share).astype(jnp.bfloat16)
    term = lax.dot_general(select, shared, TN, preferred_element_type=jnp.float32)
    for s in range(seq_size):
        for p in range(count):
            for r in range(requests):
                start = p * ROWS + r * steps
                out_ref[s, p, r] = term[
                    start : start + steps, s * feature : (s + 1) * feature
                ].astype(jnp.bfloat16)


def limit(mebibytes):
    return pltpu.CompilerParams(vmem_limit_bytes=mebibytes * 1024 * 1024)


def stage(count, beside, extras, *refs):
    sources, rest = refs[:count], refs[count:]
    inputs, copies = rest[:extras], rest[extras : extras + count]
    sems, others = rest[-1], rest[extras + count : -1]
    moves = [
        pltpu.make_async_copy(source, copy, sems.at[i])
        for i, (source, copy) in enumerate(zip(sources, copies))
    ]
    for move in moves:
        move.start()
    beside(inputs, others, sems.at[count])
    for move in moves:
        move.wait()


def spread_constants(inputs, others, sem):
    expand_ref, extra_ref, ids_ref = others
    move = pltpu.make_async_copy(inputs[1], ids_ref, sem)
    move.start()
    shape = expand_ref.shape
    head = shape[1] // HEADS
    group = iota(shape, 0)
    same = (within(group, HEADS) == over(iota(shape, 1), head)) & (group < 3 * HEADS)
    expand_ref[...] = jnp.where(same, 1.0, 0.0).astype(jnp.bfloat16)
    move.wait()
    requests, _, steps = ids_ref.shape
    columns = extra_ref.shape[1]
    tp = lax.axis_index("tp")
    row = iota((ROWS, columns), 0)
    lane = iota((ROWS, columns), 1) - tp * ROWS
    extra = jnp.where((lane >= 0) & (lane < ROWS), -1.0, 0.0)
    for i in range(requests * steps):
        first, second = [
            ids_ref[i // steps, k, i % steps].astype(jnp.float32) for k in range(2)
        ]
        extra = jnp.where(lane == i, jnp.where(row == requests * steps, first, second), extra)
    extra_ref[...] = extra


def own_features(inputs, others, sem):
    attn_ref, res_ref = inputs
    attn_hbm, own_ref, attn_buf = others
    requests, steps, feature = own_ref.shape
    seq = lax.axis_index("seq")
    lanes = pl.ds(pl.multiple_of(seq * feature, feature), feature)
    attention, residual = attn_ref[:, lanes], res_ref[:, lanes]
    for r in range(requests):
        part = slice(r * steps, (r + 1) * steps)
        attn_buf[r] = attention[part].astype(jnp.bfloat16)
        own_ref[r] = residual[part]
    move = pltpu.make_async_copy(attn_buf, attn_hbm, sem)
    move.start()
    move.wait()


def staged(beside, arrays, extras, shapes, specs, scratch=()):
    anywhere = pl.BlockSpec(memory_space=pl.ANY)
    count = len(arrays)
    size = sum(2 * x.size for x in arrays)
    return pl.pallas_call(
        functools.partial(stage, count, beside, len(extras)),
        out_shape=tuple(pltpu.VMEM(x.shape, x.dtype) for x in arrays) + tuple(shapes),
        in_specs=[anywhere] * count + [spec for _, spec in extras],
        out_specs=(anywhere,) * count + tuple(specs),
        scratch_shapes=list(scratch) + [pltpu.SemaphoreType.DMA((count + 1,))],
        compiler_params=limit(4),
        cost_estimate=pl.CostEstimate(flops=0, bytes_accessed=2 * size, transcendentals=0),
        name="stage",
    )(*[pltpu.with_memory_space_constraint(x, pltpu.HBM) for x in arrays], *[x for x, _ in extras])


def body(
    hidden_in,
    new_query,
    new_key,
    new_value,
    key_cache,
    value_cache,
    lengths,
    out_weight,
    norm_gain,
    router_weight,
    expert_ids,
    gate_weight,
    up_weight,
    down_weight,
):
    requests, steps, width = hidden_in.shape
    block = key_cache.shape[1]
    seq_size = lax.axis_size("seq")
    tp_size = lax.axis_size("tp")
    feature = width // seq_size
    experts = router_weight.shape[1]
    topk = expert_ids.shape[2]
    capacity = (5 * requests * tp_size * topk + 4 * experts - 1) // (4 * experts)
    slices = seq_size * tp_size // experts
    vmem = pl.BlockSpec(memory_space=pltpu.VMEM)
    hbm = pl.BlockSpec(memory_space=pltpu.HBM)

    small = pltpu.VMEM((requests, steps, width), jnp.bfloat16)
    partial = pltpu.VMEM((requests, steps, width + LANES), jnp.bfloat16)
    part, fresh = pl.pallas_call(
        attend,
        out_shape=(partial, partial),
        in_specs=[hbm] * 6,
        out_specs=(vmem, vmem),
        scratch_shapes=[
            pltpu.SMEM((requests,), jnp.int32),
            small,
            small,
            small,
            pltpu.VMEM((requests, ROWS, width), jnp.bfloat16),
            pltpu.VMEM((requests, block, width), jnp.bfloat16),
            pltpu.VMEM((requests, block, width), jnp.bfloat16),
            pltpu.SemaphoreType.DMA((2, requests)),
            pltpu.SemaphoreType.DMA((4,)),
        ],
        compiler_params=limit(24),
        name="attend",
    )(
        *[
            pltpu.with_memory_space_constraint(x, pltpu.HBM)
            for x in (lengths, new_query, new_key, new_value, key_cache, value_cache)
        ]
    )

    def swapped(x, axis, size, d):
        return lax.ppermute(x, axis, [(i, i ^ d) for i in range(size)])

    ids = expert_ids.transpose(0, 2, 1)
    out_weight, gate_weight, expand, extra = staged(
        spread_constants,
        (out_weight, gate_weight),
        ((part, vmem), (pltpu.with_memory_space_constraint(ids, pltpu.HBM), hbm)),
        (
            pltpu.VMEM((4 * HEADS, width), jnp.bfloat16),
            pltpu.VMEM((ROWS, tp_size * ROWS), jnp.float32),
        ),
        (vmem, vmem),
        (pltpu.SMEM(ids.shape, jnp.int32),),
    )
    parts = [fresh, part] + [swapped(part, "seq", seq_size, d) for d in range(1, seq_size)]
    row_sums = pltpu.VMEM((ROWS, width), jnp.float32)
    packed, attention, residual = pl.pallas_call(
        functools.partial(project, seq_size + 1),
        out_shape=(pltpu.VMEM((ROWS, width), jnp.bfloat16), row_sums, row_sums),
        in_specs=[vmem] * (6 + seq_size),
        out_specs=(vmem, vmem, vmem),
        compiler_params=limit(8),
        name="project",
    )(
        extra,
        hidden_in,
        norm_gain.reshape(1, width),
        out_weight,
        expand,
        *parts,
    )
    own = (requests, steps, feature)
    up_weight, down_weight, attn_out, own_residual = staged(
        own_features,
        (up_weight, down_weight),
        ((attention, vmem), (residual, vmem)),
        (pltpu.HBM(own, jnp.bfloat16), pltpu.VMEM(own, jnp.float32)),
        (pl.BlockSpec(memory_space=pl.ANY), vmem),
        (pltpu.VMEM(own, jnp.bfloat16),),
    )
    near = jnp.stack(
        [packed] + [swapped(packed, "tp", tp_size, 2 * d) for d in range(1, tp_size // 2)]
    )
    near, up_weight, down_weight = lax.optimization_barrier((near, up_weight, down_weight))
    far = swapped(near, "tp", tp_size, 1)
    terms = pl.pallas_call(
        functools.partial(feed, capacity, steps, requests * steps, slices),
        out_shape=pltpu.VMEM((seq_size, tp_size, requests, steps, feature), jnp.bfloat16),
        in_specs=[vmem] * 6,
        out_specs=vmem,
        scratch_shapes=[pltpu.VMEM((tp_size * ROWS, width), jnp.bfloat16)],
        compiler_params=limit(16),
        name="feed",
    )(router_weight.T, gate_weight, up_weight, down_weight, near, far)
    terms = terms.reshape(seq_size * tp_size, requests, steps, feature)
    arrived = lax.all_to_all(terms, ("seq", "tp"), 0, 0, tiled=True)
    mixture = jnp.sum(arrived.astype(jnp.float32), axis=0)
    return (attn_out, (own_residual + mixture).astype(jnp.bfloat16))


def solution(mesh):
    return jax.shard_map(
        body,
        mesh=mesh,
        in_specs=(
            P("tp", None, None),
            P("tp", None, None),
            P("tp", None, None),
            P("tp", None, None),
            P("tp", "seq", None),
            P("tp", "seq", None),
            P("tp"),
            P(),
            P(),
            P(),
            P("tp", None, None),
            P(("seq", "tp"), None),
            P(("seq", "tp"), None),
            P(("seq", "tp"), None),
        ),
        out_specs=(P("tp", None, "seq"), P("tp", None, "seq")),
        check_vma=False,
    )
```

```python
import functools

import jax
import jax.numpy as jnp
from jax import lax
from jax.experimental import pallas as pl
from jax.experimental.pallas import tpu as pltpu
from jax.sharding import PartitionSpec as P

HEADS = 16
SHORT = 128
ROWS = 16
LANES = 128
masked_score = -1e30
norm_epsilon = 1e-06
NT = (((1,), (1,)), ((), ()))
TN = (((0,), (0,)), ((), ()))


def iota(shape, dim):
    return lax.broadcasted_iota(jnp.int32, shape, dim)


def over(x, n):
    if n & (n - 1) == 0:
        return lax.shift_right_logical(x, jnp.int32(n.bit_length() - 1))
    return x // n


def within(x, n):
    if n & (n - 1) == 0:
        return x & (n - 1)
    return x % n


def three_parts(x):
    hi = x.astype(jnp.bfloat16).astype(jnp.float32)
    mid = (x - hi).astype(jnp.bfloat16).astype(jnp.float32)
    return hi, mid, x - hi - mid


def tiled(x, times):
    return jnp.concatenate([x] * times, axis=0)


def attend(
    lens_hbm, q_hbm, nk_hbm, nv_hbm, k_hbm, v_hbm, out_ref, fresh_ref,
    lens, q_ref, nk_ref, nv_ref, query_ref, kbuf, vbuf, sems, small_sems,
):
    requests, block, width = k_hbm.shape
    steps = q_ref.shape[1]
    head = width // HEADS
    scale = head ** (-0.5)
    group = 256 // head
    chunks = width // 256
    rows = group * steps
    seq = lax.axis_index("seq")
    small = [
        pltpu.make_async_copy(src, dst, small_sems.at[i])
        for i, (src, dst) in enumerate(
            ((lens_hbm, lens), (q_hbm, q_ref), (nk_hbm, nk_ref), (nv_hbm, nv_ref))
        )
    ]
    for move in small:
        move.start()
    small[0].wait()

    def left(r):
        return lens[r] - seq * block

    def is_full(r):
        return left(r) >= block

    def is_short(r):
        return (left(r) > 0) & (left(r) < block)

    def move(which, r, count):
        src, dst = ((k_hbm, kbuf), (v_hbm, vbuf))[which]
        part = pl.ds(0, count)
        return pltpu.make_async_copy(src.at[r, part], dst.at[r, part], sems.at[which, r])

    for kind, count in ((is_short, SHORT), (is_full, block)):
        for r in range(requests):

            @pl.when(kind(r))
            def _():
                for which in range(2):
                    move(which, r, count).start()

    for move_small in small[1:]:
        move_small.wait()
    diag = over(iota((rows, 256), 0), steps) == over(iota((rows, 256), 1), head)
    diag_all = jnp.concatenate([diag] * chunks, axis=1)
    all_rows = chunks * rows

    def columns(c):
        return slice(c * 256, (c + 1) * 256)

    def against(query, keys):
        return jnp.concatenate(
            [
                lax.dot_general(
                    query[:, columns(c)], keys(c), NT, preferred_element_type=jnp.float32
                )
                for c in range(chunks)
            ],
            axis=0,
        )

    def summary(top, total):
        shape = (all_rows, LANES)
        part = over(iota(shape, 1), HEADS)
        spread = jnp.zeros(shape, jnp.float32)
        for place, value in enumerate(three_parts(top) + three_parts(total)):
            spread = jnp.where(part == place, value, spread)
        spread = jnp.where(
            within(iota(shape, 1), HEADS) == over(iota(shape, 0), steps), spread, 0.0
        )
        pick = within(iota((ROWS, all_rows), 1), steps) == iota((ROWS, all_rows), 0)
        gathered = jnp.dot(
            jnp.where(pick, 1.0, 0.0).astype(jnp.bfloat16),
            spread.astype(jnp.bfloat16),
            preferred_element_type=jnp.float32,
        )
        return gathered[:steps].astype(jnp.bfloat16)

    def own_head(mixed):
        mixed = jnp.where(diag, mixed, 0.0)
        half = mixed[: 2 * steps]
        for g in range(1, group // 2):
            half = half + mixed[2 * steps * g : 2 * steps * (g + 1)]
        return (half[:steps] + half[steps:]).astype(jnp.bfloat16)

    def largest(x):
        return jnp.max(x, axis=1, keepdims=True)

    def summed(x):
        return jnp.sum(x, axis=1, keepdims=True)

    def weighted(weight, values):
        return [
            own_head(
                jnp.dot(
                    weight[c * rows : (c + 1) * rows],
                    values(c),
                    preferred_element_type=jnp.float32,
                )
            )
            for c in range(chunks)
        ]

    for r in range(requests):
        query = jnp.where(diag_all, tiled(q_ref[r].astype(jnp.float32) * scale, group), 0.0)
        query = query.astype(jnp.bfloat16)
        query_ref[r] = query
        keys = tiled(nk_ref[r].astype(jnp.float32), group).astype(jnp.bfloat16)
        values = tiled(nv_ref[r].astype(jnp.float32), group).astype(jnp.bfloat16)
        score = against(query, lambda c: keys[:, columns(c)])
        usable = iota(score.shape, 1) <= within(iota(score.shape, 0), steps)
        score = jnp.where(usable, score, masked_score)
        top = largest(score)
        weight = jnp.where(usable, jnp.exp(score - top), 0.0)
        fresh_ref[r, :, width:] = summary(top, summed(weight))
        mixed = weighted(weight.astype(jnp.bfloat16), lambda c: values[:, columns(c)])
        for c in range(chunks):
            fresh_ref[r, :, columns(c)] = mixed[c]

    @pl.loop(0, requests)
    def _(r):
        @pl.when(left(r) <= 0)
        def _():
            shape = (steps, LANES)
            hi, mid, low = three_parts(jnp.full(shape, masked_score, jnp.float32))
            part = over(iota(shape, 1), HEADS)
            empty = jnp.where(part == 0, hi, jnp.where(part == 1, mid, low))
            out_ref[r, :, width:] = jnp.where(part < 3, empty, 0.0).astype(jnp.bfloat16)
            out_ref[r, :, :width] = jnp.zeros((steps, width), jnp.bfloat16)

    def one(r, count):
        part = pl.ds(0, count)
        move(0, r, count).wait()
        query = query_ref[r]
        score = against(query, lambda c: kbuf[r, part, columns(c)])
        if count < block:
            usable = iota(score.shape, 1) < left(r)
            score = jnp.where(usable, score, masked_score)
        top = largest(score)
        weight = jnp.exp(score - top)
        if count < block:
            weight = jnp.where(usable, weight, 0.0)
        total = summed(weight)
        weight = weight.astype(jnp.bfloat16)
        move(1, r, count).wait()
        mixed = weighted(weight, lambda c: vbuf[r, part, columns(c)])
        out_ref[r, :, width:] = summary(top, total)
        for c in range(chunks):
            out_ref[r, :, columns(c)] = mixed[c]

    for kind, count in ((is_short, SHORT), (is_full, block)):

        @pl.loop(0, requests)
        def _(r):
            @pl.when(kind(r))
            def _():
                one(r, count)


def project(count, extra_ref, hidden_ref, gain_ref, weight_ref, expand_ref, *refs):
    parts = refs[:count]
    send_ref, attn_ref, res_ref = refs[count:]
    requests, steps, width = hidden_ref.shape

    def moved(x, amount):
        return pltpu.roll(x, LANES - amount, 1)

    def rows_of(ref, lanes):
        pieces = [ref[r, :, lanes].astype(jnp.float32) for r in range(requests)]
        blank = jnp.zeros((ROWS - requests * steps, pieces[0].shape[1]), jnp.float32)
        return jnp.concatenate(pieces + [blank], axis=0)

    tops, totals = [], []
    for ref in parts:
        x = rows_of(ref, slice(width, width + LANES))
        tops.append(x + moved(x, HEADS) + moved(x, 2 * HEADS))
        totals.append(moved(x, 3 * HEADS) + moved(x, 4 * HEADS) + moved(x, 5 * HEADS))
    overall = functools.reduce(jnp.maximum, tops)
    factors = [jnp.exp(top - overall) for top in tops]
    total = functools.reduce(jnp.add, [f * t for f, t in zip(factors, totals)])
    real = (iota(total.shape, 1) < HEADS) & (iota(total.shape, 0) < requests * steps)
    inverse = jnp.where(real, 1.0 / jnp.where(real, total, 1.0), 0.0)
    ratio = jnp.concatenate([jnp.where(real, f, 0.0) * inverse for f in factors], axis=0)
    hi, mid, low = three_parts(ratio)
    packed = hi + pltpu.roll(mid, HEADS, 1) + pltpu.roll(low, 2 * HEADS, 1)
    packed = packed.astype(jnp.bfloat16)[:, : 4 * HEADS]
    wide = jnp.dot(packed, expand_ref[...], preferred_element_type=jnp.float32)
    context = jnp.zeros((ROWS, width), jnp.float32)
    for b, ref in enumerate(parts):
        context = context + wide[b * ROWS : (b + 1) * ROWS] * rows_of(ref, slice(0, width))
    attention = jnp.dot(
        context.astype(jnp.bfloat16), weight_ref[...], preferred_element_type=jnp.float32
    )
    residual = rows_of(hidden_ref, slice(0, width)) + attention
    normed = (
        residual
        * lax.rsqrt(jnp.mean(residual * residual, axis=1, keepdims=True) + norm_epsilon)
        * gain_ref[...]
    )
    columns = extra_ref.shape[1]
    row = iota((ROWS, columns), 0)
    tail = row >= requests * steps
    message = jnp.concatenate(
        [jnp.where(tail, extra_ref[...], normed[:, :columns]), normed[:, columns:]], axis=1
    ).astype(jnp.bfloat16)
    send_ref[...] = message
    attn_ref[...] = attention
    res_ref[...] = residual


def feed(
    capacity, steps, used, slices, router_ref, gate_ref, up_ref, down_ref, near_ref, far_ref,
    out_ref, tokens,
):
    half = near_ref.shape[0]
    count = 2 * half
    width = gate_ref.shape[1]
    experts = router_ref.shape[0]
    seq_size, _, requests, _, feature = out_ref.shape
    seq = lax.axis_index("seq")
    tp = lax.axis_index("tp")
    columns = count * ROWS
    core = within(tp, 2)
    for d in range(half):
        chip = within(over(tp, 2) + (half - d), half)
        for ref, which in ((near_ref, core), (far_ref, 1 - core)):
            start = pl.multiple_of((2 * chip + which) * ROWS, ROWS)
            tokens[pl.ds(start, ROWS), :] = ref[d]
    ids = jnp.zeros((8, columns), jnp.float32)
    for p in range(count):
        ids = ids + tokens[p * ROWS : (p + 1) * ROWS, :columns].astype(jnp.float32)[8:]
    place = used - 8
    first = ids[place : place + 1]
    second = ids[place + 1 : place + 2]
    mine = over(seq * count + tp, slices)
    mine_f = mine.astype(jnp.float32)
    hit = jnp.where((first == mine_f) | (second == mine_f), 1.0, 0.0)
    other = jnp.where(first == mine_f, second, first)
    earlier = (iota((columns, columns), 0) < iota((columns, columns), 1)) & (
        within(iota((columns, columns), 0), steps) == within(iota((columns, columns), 1), steps)
    )
    slot = jnp.dot(
        jnp.broadcast_to(hit, (ROWS, columns)).astype(jnp.bfloat16),
        jnp.where(earlier, 1.0, 0.0).astype(jnp.bfloat16),
        preferred_element_type=jnp.float32,
    )[:1]
    rows = -(-steps * capacity // ROWS) * ROWS
    row = iota((rows, columns), 0)
    choose = (
        (hit > 0.5)
        & (slot == within(row, capacity).astype(jnp.float32))
        & (within(iota((rows, columns), 1), steps) == over(row, capacity))
    )
    select = jnp.where(choose, 1.0, 0.0)
    rival = jnp.sum(select * other, axis=1, keepdims=True)
    select = select.astype(jnp.bfloat16)
    buffer = jnp.dot(select, tokens[...], preferred_element_type=jnp.float32).astype(jnp.bfloat16)
    logits = lax.dot_general(buffer, router_ref[...], NT, preferred_element_type=jnp.float32)
    index = iota((rows, experts), 1)
    ahead = jnp.sum(jnp.where(index == mine, logits, 0.0), axis=1, keepdims=True)
    behind = jnp.sum(
        jnp.where(index.astype(jnp.float32) == rival, logits, 0.0), axis=1, keepdims=True
    )
    share = 1.0 / (1.0 + jnp.exp(behind - ahead))
    gate = lax.dot_general(buffer, gate_ref[...], NT, preferred_element_type=jnp.float32)
    upward = lax.dot_general(buffer, up_ref[...], NT, preferred_element_type=jnp.float32)
    inner = (jax.nn.gelu(gate) * upward).astype(jnp.bfloat16)
    produced = jnp.dot(inner, down_ref[...], preferred_element_type=jnp.float32)
    shared = (produced * share).astype(jnp.bfloat16)
    term = lax.dot_general(select, shared, TN, preferred_element_type=jnp.float32)
    for s in range(seq_size):
        for p in range(count):
            for r in range(requests):
                start = p * ROWS + r * steps
                out_ref[s, p, r] = term[
                    start : start + steps, s * feature : (s + 1) * feature
                ].astype(jnp.bfloat16)


def limit(mebibytes):
    return pltpu.CompilerParams(vmem_limit_bytes=mebibytes * 1024 * 1024)


def stage(count, beside, extras, *refs):
    sources, rest = refs[:count], refs[count:]
    inputs, copies = rest[:extras], rest[extras : extras + count]
    sems, others = rest[-1], rest[extras + count : -1]
    moves = [
        pltpu.make_async_copy(source, copy, sems.at[i])
        for i, (source, copy) in enumerate(zip(sources, copies))
    ]
    for move in moves:
        move.start()
    beside(inputs, others, sems.at[count])
    for move in moves:
        move.wait()


def spread_constants(inputs, others, sem):
    expand_ref, extra_ref, ids_ref = others
    move = pltpu.make_async_copy(inputs[1], ids_ref, sem)
    move.start()
    shape = expand_ref.shape
    head = shape[1] // HEADS
    group = iota(shape, 0)
    same = (within(group, HEADS) == over(iota(shape, 1), head)) & (group < 3 * HEADS)
    expand_ref[...] = jnp.where(same, 1.0, 0.0).astype(jnp.bfloat16)
    move.wait()
    requests, _, steps = ids_ref.shape
    columns = extra_ref.shape[1]
    tp = lax.axis_index("tp")
    row = iota((ROWS, columns), 0)
    lane = iota((ROWS, columns), 1) - tp * ROWS
    extra = jnp.where((lane >= 0) & (lane < ROWS), -1.0, 0.0)
    for i in range(requests * steps):
        first, second = [
            ids_ref[i // steps, k, i % steps].astype(jnp.float32) for k in range(2)
        ]
        extra = jnp.where(lane == i, jnp.where(row == requests * steps, first, second), extra)
    extra_ref[...] = extra


def own_features(inputs, others, sem):
    attn_ref, res_ref = inputs
    attn_hbm, own_ref, attn_buf = others
    requests, steps, feature = own_ref.shape
    seq = lax.axis_index("seq")
    lanes = pl.ds(pl.multiple_of(seq * feature, feature), feature)
    attention, residual = attn_ref[:, lanes], res_ref[:, lanes]
    for r in range(requests):
        part = slice(r * steps, (r + 1) * steps)
        attn_buf[r] = attention[part].astype(jnp.bfloat16)
        own_ref[r] = residual[part]
    move = pltpu.make_async_copy(attn_buf, attn_hbm, sem)
    move.start()
    move.wait()


def staged(beside, arrays, extras, shapes, specs, scratch=()):
    anywhere = pl.BlockSpec(memory_space=pl.ANY)
    count = len(arrays)
    size = sum(2 * x.size for x in arrays)
    return pl.pallas_call(
        functools.partial(stage, count, beside, len(extras)),
        out_shape=tuple(pltpu.VMEM(x.shape, x.dtype) for x in arrays) + tuple(shapes),
        in_specs=[anywhere] * count + [spec for _, spec in extras],
        out_specs=(anywhere,) * count + tuple(specs),
        scratch_shapes=list(scratch) + [pltpu.SemaphoreType.DMA((count + 1,))],
        compiler_params=limit(4),
        cost_estimate=pl.CostEstimate(flops=0, bytes_accessed=2 * size, transcendentals=0),
        name="stage",
    )(*[pltpu.with_memory_space_constraint(x, pltpu.HBM) for x in arrays], *[x for x, _ in extras])


def body(
    hidden_in,
    new_query,
    new_key,
    new_value,
    key_cache,
    value_cache,
    lengths,
    out_weight,
    norm_gain,
    router_weight,
    expert_ids,
    gate_weight,
    up_weight,
    down_weight,
):
    requests, steps, width = hidden_in.shape
    block = key_cache.shape[1]
    seq_size = lax.axis_size("seq")
    tp_size = lax.axis_size("tp")
    feature = width // seq_size
    experts = router_weight.shape[1]
    topk = expert_ids.shape[2]
    capacity = (5 * requests * tp_size * topk + 4 * experts - 1) // (4 * experts)
    slices = seq_size * tp_size // experts
    vmem = pl.BlockSpec(memory_space=pltpu.VMEM)
    hbm = pl.BlockSpec(memory_space=pltpu.HBM)

    small = pltpu.VMEM((requests, steps, width), jnp.bfloat16)
    partial = pltpu.VMEM((requests, steps, width + LANES), jnp.bfloat16)
    part, fresh = pl.pallas_call(
        attend,
        out_shape=(partial, partial),
        in_specs=[hbm] * 6,
        out_specs=(vmem, vmem),
        scratch_shapes=[
            pltpu.SMEM((requests,), jnp.int32),
            small,
            small,
            small,
            pltpu.VMEM((requests, ROWS, width), jnp.bfloat16),
            pltpu.VMEM((requests, block, width), jnp.bfloat16),
            pltpu.VMEM((requests, block, width), jnp.bfloat16),
            pltpu.SemaphoreType.DMA((2, requests)),
            pltpu.SemaphoreType.DMA((4,)),
        ],
        compiler_params=limit(24),
        name="attend",
    )(
        *[
            pltpu.with_memory_space_constraint(x, pltpu.HBM)
            for x in (lengths, new_query, new_key, new_value, key_cache, value_cache)
        ]
    )

    def swapped(x, axis, size, d):
        return lax.ppermute(x, axis, [(i, i ^ d) for i in range(size)])

    ids = expert_ids.transpose(0, 2, 1)
    out_weight, gate_weight, expand, extra = staged(
        spread_constants,
        (out_weight, gate_weight),
        ((part, vmem), (pltpu.with_memory_space_constraint(ids, pltpu.HBM), hbm)),
        (
            pltpu.VMEM((4 * HEADS, width), jnp.bfloat16),
            pltpu.VMEM((ROWS, tp_size * ROWS), jnp.float32),
        ),
        (vmem, vmem),
        (pltpu.SMEM(ids.shape, jnp.int32),),
    )
    def shifted(x, axis, size, d):
        return lax.ppermute(x, axis, [(i, (i + d) % size) for i in range(size)])

    parts = [fresh, part] + [swapped(part, "seq", seq_size, d) for d in range(1, seq_size)]
    row_sums = pltpu.VMEM((ROWS, width), jnp.float32)
    packed, attention, residual = pl.pallas_call(
        functools.partial(project, seq_size + 1),
        out_shape=(pltpu.VMEM((ROWS, width), jnp.bfloat16), row_sums, row_sums),
        in_specs=[vmem] * (6 + seq_size),
        out_specs=(vmem, vmem, vmem),
        compiler_params=limit(8),
        name="project",
    )(
        extra,
        hidden_in,
        norm_gain.reshape(1, width),
        out_weight,
        expand,
        *parts,
    )
    own = (requests, steps, feature)
    up_weight, down_weight, attn_out, own_residual = staged(
        own_features,
        (up_weight, down_weight),
        ((attention, vmem), (residual, vmem)),
        (pltpu.HBM(own, jnp.bfloat16), pltpu.VMEM(own, jnp.float32)),
        (pl.BlockSpec(memory_space=pl.ANY), vmem),
        (pltpu.VMEM(own, jnp.bfloat16),),
    )
    near = jnp.stack(
        [packed] + [shifted(packed, "tp", tp_size, 2 * d) for d in range(1, tp_size // 2)]
    )
    near, up_weight, down_weight = lax.optimization_barrier((near, up_weight, down_weight))
    far = swapped(near, "tp", tp_size, 1)
    terms = pl.pallas_call(
        functools.partial(feed, capacity, steps, requests * steps, slices),
        out_shape=pltpu.VMEM((seq_size, tp_size, requests, steps, feature), jnp.bfloat16),
        in_specs=[vmem] * 6,
        out_specs=vmem,
        scratch_shapes=[pltpu.VMEM((tp_size * ROWS, width), jnp.bfloat16)],
        compiler_params=limit(16),
        name="feed",
    )(router_weight.T, gate_weight, up_weight, down_weight, near, far)
    terms = terms.reshape(seq_size * tp_size, requests, steps, feature)
    arrived = lax.all_to_all(terms, ("seq", "tp"), 0, 0, tiled=True)
    mixture = jnp.sum(arrived.astype(jnp.float32), axis=0)
    return (attn_out, (own_residual + mixture).astype(jnp.bfloat16))


def solution(mesh):
    return jax.shard_map(
        body,
        mesh=mesh,
        in_specs=(
            P("tp", None, None),
            P("tp", None, None),
            P("tp", None, None),
            P("tp", None, None),
            P("tp", "seq", None),
            P("tp", "seq", None),
            P("tp"),
            P(),
            P(),
            P(),
            P("tp", None, None),
            P(("seq", "tp"), None),
            P(("seq", "tp"), None),
            P(("seq", "tp"), None),
        ),
        out_specs=(P("tp", None, "seq"), P("tp", None, "seq")),
        check_vma=False,
    )
```
